32 devices in a mesh: grp: 2 (over x), band: 16 (over z, y, core).
Axes of the slice: x: 2, y: 2, z: 4, core: 2. Of those that a mesh axis runs over, the one named last changes fastest.
Arguments:
- samples: float32 [2, 192, 8192], P(None, None, ('grp', 'band')), parts along dimension 2, may hold values from -6 to 6
- prototype: float32 [16, 128], replicated, may hold values from -1.5 to 1.5
- dish_filter: float32 [2, 8, 192, 128], replicated, may hold values from -1.5 to 1.5
- beam_weights: float32 [16, 8, 2, 192, 192], P('band'), may hold values from -0.3125 to 0.3125
- dish_order: int32 [192], replicated, may hold values from 0 to 191, each once
Outputs:
- power: float32 [32, 8, 192, 8], P(('grp', 'band')), parts along dimension 0
The draws below stay inside these ranges and needn't reach their ends.
There are 2 independent parts, one for each index of `grp`. The reference program is written for one: setup_inputs(seed, part) draws one part's arguments, and reference() takes and returns one part's arrays. A program takes and returns all parts, laid end to end along the dimension named above; an argument that names none is the same for every part. Nothing has to cross between parts.
Inputs may be any that keep to these rules, and one draw needn't show every extreme that they name: `dish_order`: each of the 192 dishes stands in exactly one panel slot.
All inputs are finite; a program needn't handle non-finite values.
Results may differ from the reference program's by a relative error of at most 0.0003.
Values sent between devices are 32-bit elements; how exact they have to be, the bound alone decides.
No kernel may reach another device: no remote copies, remote signals or barrier semaphores. Data moves between devices by JAX's collectives and lax.ppermute only.
A program may use at most 64 MiB of HBM per device.

```python
import math
import jax
import jax.numpy as jnp
from jax import lax

DISHES = 192
CHAN = 128
BANDW = 8
PFB_TAPS = 16
FIR_TAPS = 8
BEAM_DEV = 192
INTEG = 4
OWNERS = 1
FRAMES = 32
SAMPLES = 4096
N_BAND = 16


def steps_of(rng, extent, split, smallest, largest):
    factor_of, own = 1.0, jax.random.fold_in(rng, 6)
    for dim, blocks in split:
        steps = jnp.exp(jax.random.uniform(jax.random.fold_in(own, dim), (blocks,), jnp.float32, smallest / len(split), largest / len(split)))
        factor_of = factor_of * jnp.repeat(steps, extent[dim] // blocks).reshape([-1 if axis == dim else 1 for axis in range(len(extent))])
    return factor_of


def bell_draw(key, shape, width, bound, cuts=(), kind=jnp.bfloat16):
    values = jax.random.normal(key, shape, jnp.float32) * width
    if len(cuts) > 0:
        values = steps_of(key, shape, cuts, -0.22, 0.18) * values
    return jnp.clip(values, min=-bound, max=bound).astype(kind)


def setup_inputs(seed: int = 0, part: int = 0) -> dict:
    streams_of = jax.random.split(jax.random.key(seed), 6)
    part_splits = jax.random.split(jax.random.fold_in(streams_of[5], part), 6)
    samples = bell_draw(part_splits[0], (2, DISHES, SAMPLES), 1.0, 6.0, ((2, 16),), jnp.float32)
    prototype = bell_draw(streams_of[1], (PFB_TAPS, CHAN), 0.25, 1.5, (), jnp.float32)
    dish_filter = bell_draw(streams_of[2], (2, FIR_TAPS, DISHES, CHAN), 0.25, 1.5, (), jnp.float32)
    beam_weights = bell_draw(streams_of[3], (N_BAND, BANDW, 2, DISHES, BEAM_DEV), (2 * DISHES) ** -0.5, 0.3125, ((0, 16),), jnp.float32)
    dish_order = jax.random.permutation(streams_of[4], DISHES).astype(jnp.int32)
    return dict(samples=samples, prototype=prototype, dish_filter=dish_filter, beam_weights=beam_weights, dish_order=dish_order)


def fourier_tables(length):
    counter = jnp.arange(length, dtype=jnp.int32)
    product = counter[:, None] * counter[None, :] % length
    angles = product.astype(jnp.float32) * (2.0 * math.pi / length)
    factor = 1.0 / math.sqrt(length)
    return (jnp.cos(angles) * factor, jnp.sin(angles) * factor)

def filter_frames(real_in, imag_in, tap_real, tap_imag, frame_count):
    tap_count = tap_real.shape[0]
    out_real = jnp.zeros(real_in.shape[:-1] + (frame_count,), real_in.dtype)
    out_imag = jnp.zeros(real_in.shape[:-1] + (frame_count,), real_in.dtype)
    for tap_index in range(tap_count):
        offset = tap_count - 1 - tap_index
        part_real = real_in[..., offset:offset + frame_count]
        part_imag = imag_in[..., offset:offset + frame_count]
        factor_real = tap_real[tap_index][..., None]
        factor_imag = tap_imag[tap_index][..., None]
        out_real = out_real + factor_real * part_real - factor_imag * part_imag
        out_imag = out_imag + factor_real * part_imag + factor_imag * part_real
    return (out_real, out_imag)

def detect(weights, field_real, field_imag):
    highest = lax.Precision.HIGHEST

    def contract(weight_part, field_part):
        return jnp.einsum('qds,dqf->qsf', weight_part, field_part, precision=highest)
    beam_real = contract(weights[:, 0], field_real) - contract(weights[:, 1], field_imag)
    beam_imag = contract(weights[:, 0], field_imag) + contract(weights[:, 1], field_real)
    energy = beam_real * beam_real + beam_imag * beam_imag
    shaped = energy.reshape(energy.shape[:-1] + (energy.shape[-1] // INTEG, INTEG))
    return lax.optimization_barrier(jnp.mean(shaped, axis=-1))

def reference(samples, prototype, dish_filter, beam_weights, dish_order):
    highest = lax.Precision.HIGHEST
    ordered = samples[:, dish_order, :]
    blocks = ordered.reshape(2, DISHES, FRAMES, CHAN)
    padded = jnp.pad(blocks, ((0, 0), (0, 0), (PFB_TAPS - 1, 0), (0, 0)))
    polyphase = jnp.zeros_like(blocks)
    for tap_index in range(PFB_TAPS):
        offset = PFB_TAPS - 1 - tap_index
        polyphase = polyphase + prototype[tap_index] * padded[:, :, offset:offset + FRAMES, :]
    cosine_table, sine_table = fourier_tables(CHAN)
    spec_real = jnp.dot(polyphase[0], cosine_table, precision=highest) + jnp.dot(polyphase[1], sine_table, precision=highest)
    spec_imag = jnp.dot(polyphase[1], cosine_table, precision=highest) - jnp.dot(polyphase[0], sine_table, precision=highest)
    spec_real = jnp.transpose(spec_real, (0, 2, 1))
    spec_imag = jnp.transpose(spec_imag, (0, 2, 1))
    widths = ((0, 0), (0, 0), (FIR_TAPS - 1, 0))
    taps_ordered = dish_filter[:, :, dish_order, :]
    filtered_real, filtered_imag = filter_frames(jnp.pad(spec_real, widths), jnp.pad(spec_imag, widths), taps_ordered[0], taps_ordered[1], FRAMES)

    def one_row(row_item):
        row_index, weights = row_item
        first_chan = row_index // OWNERS * BANDW
        band_real = lax.dynamic_slice_in_dim(filtered_real, first_chan, BANDW, 1)
        band_imag = lax.dynamic_slice_in_dim(filtered_imag, first_chan, BANDW, 1)
        return detect(weights, band_real, band_imag)
    return lax.map(one_row, (jnp.arange(N_BAND, dtype=jnp.int32), beam_weights))
```

```python
import math

import jax
import jax.numpy as jnp
from jax import lax
from jax.sharding import PartitionSpec as P

INTEG = 4
HIGHEST = lax.Precision.HIGHEST


def fourier_tables(length):
    counter = jnp.arange(length, dtype=jnp.int32)
    product = counter[:, None] * counter[None, :] % length
    angles = product.astype(jnp.float32) * (2.0 * math.pi / length)
    factor = 1.0 / math.sqrt(length)
    return (jnp.cos(angles) * factor, jnp.sin(angles) * factor)


def detect(weights, field_real, field_imag):
    def contract(weight_part, field_part):
        return jnp.einsum("qds,dqf->qsf", weight_part, field_part, precision=HIGHEST)

    beam_real = contract(weights[:, 0], field_real) - contract(weights[:, 1], field_imag)
    beam_imag = contract(weights[:, 0], field_imag) + contract(weights[:, 1], field_real)
    energy = beam_real * beam_real + beam_imag * beam_imag
    shaped = energy.reshape(energy.shape[:-1] + (energy.shape[-1] // INTEG, INTEG))
    return jnp.mean(shaped, axis=-1)


def body(samples, prototype, dish_filter, beam_weights, dish_order):
    devices = lax.axis_size("band")
    position = lax.axis_index("band")
    pfb_count, channels = prototype.shape
    fir_count = dish_filter.shape[1]
    dishes = dish_filter.shape[2]
    band_chans = beam_weights.shape[1]
    bands = channels // band_chans
    owners = devices // bands
    frames_dev = samples.shape[2] // channels
    frames = frames_dev * devices
    share = -(-dishes // devices)
    extra = share * devices - dishes

    padded = jnp.pad(samples, ((0, 0), (0, extra), (0, 0)))
    pieces = padded.reshape(2, devices, share, frames_dev, channels)
    pieces = jnp.transpose(pieces, (1, 3, 0, 2, 4)).reshape(
        devices, frames_dev, 2 * share, channels
    )
    arrived = lax.all_to_all(pieces, "band", split_axis=0, concat_axis=0, tiled=True)
    blocks = arrived.reshape(frames, 2 * share, channels)

    history = jnp.pad(blocks, ((pfb_count - 1, 0), (0, 0), (0, 0)))
    polyphase = jnp.zeros_like(blocks)
    for tap_index in range(pfb_count):
        offset = pfb_count - 1 - tap_index
        polyphase = polyphase + prototype[tap_index] * history[offset : offset + frames]
    cosine, sine = fourier_tables(channels)
    both = jnp.dot(polyphase, jnp.concatenate([cosine, sine], axis=1), precision=HIGHEST)
    with_cos = both[..., :channels].reshape(frames, 2, share, channels)
    with_sin = both[..., channels:].reshape(frames, 2, share, channels)
    spec_real = with_cos[:, 0] + with_sin[:, 1]
    spec_imag = with_cos[:, 1] - with_sin[:, 0]

    taps = jnp.pad(dish_filter, ((0, 0), (0, 0), (0, extra), (0, 0)))
    taps = lax.dynamic_slice_in_dim(taps, position * share, share, 2)
    lead = ((fir_count - 1, 0), (0, 0), (0, 0))
    past_real, past_imag = jnp.pad(spec_real, lead), jnp.pad(spec_imag, lead)
    out_real = jnp.zeros_like(spec_real)
    out_imag = jnp.zeros_like(spec_imag)
    for tap_index in range(fir_count):
        offset = fir_count - 1 - tap_index
        part_real = past_real[offset : offset + frames]
        part_imag = past_imag[offset : offset + frames]
        factor_real, factor_imag = taps[0, tap_index], taps[1, tap_index]
        out_real = out_real + factor_real * part_real - factor_imag * part_imag
        out_imag = out_imag + factor_real * part_imag + factor_imag * part_real

    filtered = jnp.stack([out_real, out_imag])
    filtered = filtered.reshape(2, frames, share, bands, band_chans)
    filtered = jnp.transpose(filtered, (3, 0, 2, 4, 1)).reshape(
        bands, 2 * share, band_chans * frames
    )
    filtered = jnp.repeat(filtered, owners, axis=0)
    field = lax.all_to_all(filtered, "band", split_axis=0, concat_axis=0, tiled=True)
    field = field.reshape(devices, 2, share, band_chans, frames)
    field = jnp.transpose(field, (1, 0, 2, 3, 4))
    field = field.reshape(2, devices * share, band_chans, frames)
    field = jnp.take(field, dish_order, axis=1)
    power = detect(beam_weights[0], field[0], field[1])
    return power[None]


def solution(mesh):
    placed = (P(None, None, ("grp", "band")), P(), P(), P("band", None, None, None, None), P())
    return jax.shard_map(
        body,
        mesh=mesh,
        in_specs=placed,
        out_specs=P(("grp", "band"), None, None, None),
        check_vma=False,
    )
```

```python
import math

import jax
import jax.numpy as jnp
import numpy as np
from jax import lax
from jax.experimental import pallas as pl
from jax.experimental.pallas import tpu as pltpu
from jax.sharding import PartitionSpec as P

INTEG = 4
HIGHEST = lax.Precision.HIGHEST
F32 = jnp.float32
BF16 = jnp.bfloat16
LANES = 128
VMEM = pl.BlockSpec(memory_space=pltpu.VMEM)


def fourier_tables(length):
    counter = jnp.arange(length, dtype=jnp.int32)
    product = counter[:, None] * counter[None, :] % length
    angles = product.astype(jnp.float32) * (2.0 * math.pi / length)
    factor = 1.0 / math.sqrt(length)
    return (jnp.cos(angles) * factor, jnp.sin(angles) * factor)


def split(value):
    high = value.astype(BF16)
    return high, (value - high.astype(F32)).astype(BF16)


def share_row(part, dish):
    return part * 8 + dish if dish < 8 else 16 + part * 4 + dish - 8


def pieces_kernel(x_ref, out_ref):
    devices, frames_dev = out_ref.shape[:2]
    low = lax.broadcasted_iota(jnp.int32, (8, LANES), 0) < 4
    for frame in range(frames_dev):
        lanes = slice(frame * LANES, (frame + 1) * LANES)
        for dev in range(0, devices, 2):
            for one in (dev, dev + 1):
                for part in range(2):
                    out_ref[one, frame, part * 8 : part * 8 + 8, :] = x_ref[
                        part, one * 8 : one * 8 + 8, lanes
                    ]
            start = devices * 8 + dev * 4
            real = x_ref[0, start : start + 8, lanes]
            imag = x_ref[1, start : start + 8, lanes]
            out_ref[dev, frame, 16:24, :] = jnp.where(low, real, pltpu.roll(imag, 4, 0))
            out_ref[dev + 1, frame, 16:24, :] = jnp.where(low, pltpu.roll(real, 4, 0), imag)


def weights_kernel(w_ref, order_ref, slot_ref, out_ref):
    order = order_ref[...]
    beams = w_ref.shape[3]
    for half in range(2):
        hot = (order == slot_ref[half : half + 1, :]).astype(BF16)
        for part in range(2):
            turned = w_ref[0, part].T
            value = split(turned)[half]
            product = jnp.dot(value, hot, preferred_element_type=F32)
            rows = slice(part * beams, (part + 1) * beams)
            if half == 0:
                out_ref[0, rows, :] = product.astype(BF16)
            else:
                out_ref[0, rows, :] += product.astype(BF16)


def channel_kernel(x_ref, proto_ref, table_ref, taps_ref, out_ref, poly, spec, filt):
    frames = x_ref.shape[0]
    pfb_count = proto_ref.shape[0]
    fir_count = taps_ref.shape[0]
    group = 8
    low = lax.broadcasted_iota(jnp.int32, (group, 8, LANES), 1) < 4

    spec[0 : fir_count - 1] = jnp.zeros((fir_count - 1, 24, 2 * LANES), F32)
    for first in range(0, frames, group):
        found = []
        for rows in range(0, 24, 8):
            total = None
            for tap in range(pfb_count):
                begin = first - tap
                lost = max(0, -begin)
                if lost >= group:
                    continue
                block = x_ref[begin + lost : begin + group, rows : rows + 8, :]
                term = block * proto_ref[tap : tap + 1, :][None]
                if lost:
                    term = jnp.concatenate([jnp.zeros((lost, 8, LANES), F32), term], axis=0)
                total = term if total is None else total + term
            found.append(total)
        turned = pltpu.roll(found[2], 4, 1)
        other = [found[1], -found[0], jnp.where(low, turned, -turned)]
        for index in range(3):
            rows = slice(index * 8, index * 8 + 8)
            poly[first : first + group, rows, 0:LANES] = found[index]
            poly[first : first + group, rows, LANES : 2 * LANES] = other[index]

    for first in range(0, frames, group):
        value = poly[first : first + group].reshape(group * 24, 2 * LANES)
        high, rest = split(value)
        stacked = jnp.concatenate([high, rest, high], axis=1)
        product = jnp.dot(stacked, table_ref[...], preferred_element_type=F32)
        begin = first + fir_count - 1
        spec[begin : begin + group] = product.reshape(group, 24, 2 * LANES)

    for rows in range(0, 24, 8):
        for first in range(0, frames, group):
            total = None
            for tap in range(fir_count):
                begin = first + fir_count - 1 - tap
                near = spec[begin : begin + group, rows : rows + 8, 0:LANES]
                cross = spec[begin : begin + group, rows : rows + 8, LANES : 2 * LANES]
                term = taps_ref[tap, 0, rows : rows + 8, :][None] * near
                term = term + taps_ref[tap, 1, rows : rows + 8, :][None] * cross
                total = term if total is None else total + term
            for frame in range(group):
                begin = (first + frame) * 24 + rows
                filt[begin : begin + 8, :] = total[frame]

    per_band = out_ref.shape[1] // 6
    for pair in range(6):
        rows = [
            filt[pl.ds(share_row(part, pair * 2 + odd), frames, stride=24), :]
            for part in range(2)
            for odd in range(2)
        ]
        turned = jnp.concatenate(rows, axis=0).T
        for dev in range(out_ref.shape[0]):
            out_ref[dev, pair * per_band : (pair + 1) * per_band, :] = turned[
                dev * per_band : (dev + 1) * per_band
            ]


def beams_kernel(x_ref, w_ref, pool_ref, out_ref):
    step = pl.program_id(0)
    rows = x_ref.shape[0] // 8
    beams = w_ref.shape[1] // 2
    lane = lax.broadcasted_iota(jnp.int32, (rows, LANES), 1)
    even = lane % 64 < 32
    one = x_ref[pl.ds(2 * step, rows, stride=8), :]
    two = x_ref[pl.ds(2 * step + 1, rows, stride=8), :]
    first = jnp.where(even, one, pltpu.roll(two, 32, 1))
    second = jnp.where(even, pltpu.roll(one, LANES - 32, 1), two)
    field = jnp.concatenate([first, second], axis=0)
    high, rest = split(field)
    both = jnp.concatenate([high, rest], axis=1)
    both = jnp.concatenate([both, both], axis=0)
    sums = []
    for index in range(2):
        product = jnp.dot(w_ref[index], both, preferred_element_type=F32)
        sums.append(product[:, 0:LANES] + product[:, LANES : 2 * LANES])
    wide = lax.broadcasted_iota(jnp.int32, (beams, LANES), 1)
    even = wide % 64 < 32
    by_real = jnp.where(even, sums[0][:beams], sums[1][:beams])
    by_imag = jnp.where(even, sums[0][beams:], sums[1][beams:])
    crossed = pltpu.roll(by_imag, 64, 1)
    beam = by_real + jnp.where(wide < 64, -crossed, crossed)
    high, rest = split(beam * beam)
    power = lax.dot_general(
        pool_ref[...],
        jnp.concatenate([high, rest], axis=1),
        (((1,), (1,)), ((), ())),
        preferred_element_type=F32,
    )
    out_ref[0] = power[0:8]
    out_ref[1] = power[8:16]


def slots_of(devices):
    dishes = np.zeros((2, devices, 6), np.int32)
    for odd in range(2):
        for dev in range(devices):
            for pair in range(6):
                own = pair * 2 + odd
                dishes[odd, dev, pair] = (
                    dev * 8 + own if own < 8 else devices * 8 + dev * 4 + own - 8
                )
    flat = dishes.reshape(-1)
    none = np.full_like(flat, -1)
    return np.stack([np.concatenate([flat, none]), np.concatenate([none, flat])])


def dft_parts(channels):
    index = np.arange(channels)
    angle = 2.0 * np.pi * (index[:, None] * index[None, :] % channels) / channels
    cosine = np.cos(angle) / np.sqrt(channels)
    sine = np.sin(angle) / np.sqrt(channels)
    table = np.block([[cosine, sine], [sine, -cosine]]).astype(np.float32)
    high = table.astype(jnp.bfloat16)
    rest = (table - high.astype(np.float32)).astype(jnp.bfloat16)
    return np.concatenate([high, high, rest], axis=0)


def pool_parts(frames):
    pool = np.zeros((2, 8, 2, 2, frames), np.float32)
    for which in range(2):
        for frame in range(frames):
            pool[which, frame // INTEG, :, which, frame] = 1.0 / INTEG
    pool = pool.reshape(16, LANES)
    return np.concatenate([pool, pool], axis=1).astype(jnp.bfloat16)


def close_body(samples, prototype, dish_filter, beam_weights, dish_order):
    devices = lax.axis_size("band")
    position = lax.axis_index("band")
    channels = prototype.shape[1]
    fir_count = dish_filter.shape[1]
    dishes = dish_filter.shape[2]
    band_chans = beam_weights.shape[1]
    beams = beam_weights.shape[4]
    frames_dev = samples.shape[2] // channels
    frames = frames_dev * devices

    pieces = pl.pallas_call(
        pieces_kernel,
        out_shape=jax.ShapeDtypeStruct((devices, frames_dev, 24, channels), F32),
        in_specs=[VMEM],
        out_specs=VMEM,
        name="pieces",
    )(samples)
    arrived = lax.all_to_all(pieces, "band", split_axis=0, concat_axis=0, tiled=True)

    eight = lax.dynamic_slice_in_dim(dish_filter, position * 8, 8, 2)
    four = lax.dynamic_slice_in_dim(dish_filter, devices * 8 + position * 4, 4, 2)
    taps = jnp.concatenate([eight, eight, four, four], axis=2)
    taps = jnp.transpose(taps, (1, 0, 2, 3))
    weights = pl.pallas_call(
        weights_kernel,
        grid=(band_chans,),
        out_shape=jax.ShapeDtypeStruct((band_chans, 2 * beams, 2 * dishes), BF16),
        in_specs=[
            pl.BlockSpec((1, 2, dishes, beams), lambda i: (i, 0, 0, 0)),
            pl.BlockSpec((dishes, 1), lambda i: (0, 0)),
            pl.BlockSpec((2, 2 * dishes), lambda i: (0, 0)),
        ],
        out_specs=pl.BlockSpec((1, 2 * beams, 2 * dishes), lambda i: (i, 0, 0)),
        name="weights",
        cost_estimate=pl.CostEstimate(
            flops=8 * 4 * 2 * 192 * 192 * 384, bytes_accessed=5 << 20, transcendentals=0
        ),
    )(beam_weights[0], dish_order.reshape(dishes, 1), slots_of(devices))

    filtered = pl.pallas_call(
        channel_kernel,
        out_shape=jax.ShapeDtypeStruct((devices, 6 * band_chans, channels), F32),
        in_specs=[VMEM] * 4,
        out_specs=VMEM,
        scratch_shapes=[
            pltpu.VMEM((frames, 24, 2 * LANES), F32),
            pltpu.VMEM((frames + fir_count - 1, 24, 2 * LANES), F32),
            pltpu.VMEM((frames * 24, LANES), F32),
        ],
        name="channels",
    )(arrived.reshape(frames, 24, channels), prototype, dft_parts(channels), taps)
    field = lax.all_to_all(filtered, "band", split_axis=0, concat_axis=0, tiled=True)
    field = field.reshape(devices * 6 * band_chans, channels)

    power = pl.pallas_call(
        beams_kernel,
        grid=(band_chans // 2,),
        out_shape=jax.ShapeDtypeStruct((band_chans, frames // INTEG, beams), F32),
        in_specs=[
            pl.BlockSpec(field.shape, lambda i: (0, 0)),
            pl.BlockSpec((2, 2 * beams, 2 * dishes), lambda i: (i, 0, 0)),
            pl.BlockSpec((16, 2 * LANES), lambda i: (0, 0)),
        ],
        out_specs=pl.BlockSpec((2, frames // INTEG, beams), lambda i: (i, 0, 0)),
        name="beams",
    )(field, weights, pool_parts(frames))
    return jnp.transpose(power, (0, 2, 1))[None]


def detect(weights, field_real, field_imag):
    def contract(weight_part, field_part):
        return jnp.einsum("qds,dqf->qsf", weight_part, field_part, precision=HIGHEST)

    beam_real = contract(weights[:, 0], field_real) - contract(weights[:, 1], field_imag)
    beam_imag = contract(weights[:, 0], field_imag) + contract(weights[:, 1], field_real)
    energy = beam_real * beam_real + beam_imag * beam_imag
    shaped = energy.reshape(energy.shape[:-1] + (energy.shape[-1] // INTEG, INTEG))
    return jnp.mean(shaped, axis=-1)


def wide_body(samples, prototype, dish_filter, beam_weights, dish_order):
    devices = lax.axis_size("band")
    position = lax.axis_index("band")
    pfb_count, channels = prototype.shape
    fir_count = dish_filter.shape[1]
    dishes = dish_filter.shape[2]
    band_chans = beam_weights.shape[1]
    bands = channels // band_chans
    owners = devices // bands
    frames_dev = samples.shape[2] // channels
    frames = frames_dev * devices
    share = -(-dishes // devices)
    extra = share * devices - dishes

    padded = jnp.pad(samples, ((0, 0), (0, extra), (0, 0)))
    pieces = padded.reshape(2, devices, share, frames_dev, channels)
    pieces = jnp.transpose(pieces, (1, 3, 0, 2, 4)).reshape(
        devices, frames_dev, 2 * share, channels
    )
    arrived = lax.all_to_all(pieces, "band", split_axis=0, concat_axis=0, tiled=True)
    blocks = arrived.reshape(frames, 2 * share, channels)

    history = jnp.pad(blocks, ((pfb_count - 1, 0), (0, 0), (0, 0)))
    polyphase = jnp.zeros_like(blocks)
    for tap_index in range(pfb_count):
        offset = pfb_count - 1 - tap_index
        polyphase = polyphase + prototype[tap_index] * history[offset : offset + frames]
    cosine, sine = fourier_tables(channels)
    both = jnp.dot(polyphase, jnp.concatenate([cosine, sine], axis=1), precision=HIGHEST)
    with_cos = both[..., :channels].reshape(frames, 2, share, channels)
    with_sin = both[..., channels:].reshape(frames, 2, share, channels)
    spec_real = with_cos[:, 0] + with_sin[:, 1]
    spec_imag = with_cos[:, 1] - with_sin[:, 0]

    taps = jnp.pad(dish_filter, ((0, 0), (0, 0), (0, extra), (0, 0)))
    taps = lax.dynamic_slice_in_dim(taps, position * share, share, 2)
    lead = ((fir_count - 1, 0), (0, 0), (0, 0))
    past_real, past_imag = jnp.pad(spec_real, lead), jnp.pad(spec_imag, lead)
    out_real = jnp.zeros_like(spec_real)
    out_imag = jnp.zeros_like(spec_imag)
    for tap_index in range(fir_count):
        offset = fir_count - 1 - tap_index
        part_real = past_real[offset : offset + frames]
        part_imag = past_imag[offset : offset + frames]
        factor_real, factor_imag = taps[0, tap_index], taps[1, tap_index]
        out_real = out_real + factor_real * part_real - factor_imag * part_imag
        out_imag = out_imag + factor_real * part_imag + factor_imag * part_real

    filtered = jnp.stack([out_real, out_imag])
    filtered = filtered.reshape(2, frames, share, bands, band_chans)
    filtered = jnp.transpose(filtered, (3, 0, 2, 4, 1)).reshape(
        bands, 2 * share, band_chans * frames
    )
    filtered = jnp.repeat(filtered, owners, axis=0)
    field = lax.all_to_all(filtered, "band", split_axis=0, concat_axis=0, tiled=True)
    field = field.reshape(devices, 2, share, band_chans, frames)
    field = jnp.transpose(field, (1, 0, 2, 3, 4))
    field = field.reshape(2, devices * share, band_chans, frames)
    field = jnp.take(field, dish_order, axis=1)
    power = detect(beam_weights[0], field[0], field[1])
    return power[None]


def solution(mesh):
    devices = mesh.shape["band"]

    def body(samples, prototype, dish_filter, beam_weights, dish_order):
        channels = prototype.shape[1]
        close = (
            channels == LANES
            and beam_weights.shape[1] == 8
            and devices * 8 == channels
            and dish_filter.shape[2] == 12 * devices
            and samples.shape[2] * devices == 32 * channels
        )
        chosen = close_body if close else wide_body
        return chosen(samples, prototype, dish_filter, beam_weights, dish_order)

    placed = (P(None, None, ("grp", "band")), P(), P(), P("band", None, None, None, None), P())
    return jax.shard_map(
        body,
        mesh=mesh,
        in_specs=placed,
        out_specs=P(("grp", "band"), None, None, None),
        check_vma=False,
    )
```

```python
import math

import jax
import jax.numpy as jnp
import numpy as np
from jax import lax
from jax.experimental import pallas as pl
from jax.experimental.pallas import tpu as pltpu
from jax.sharding import PartitionSpec as P

INTEG = 4
HIGHEST = lax.Precision.HIGHEST
F32 = jnp.float32
BF16 = jnp.bfloat16
LANES = 128
VMEM = pl.BlockSpec(memory_space=pltpu.VMEM)
GRANT = pltpu.CompilerParams(vmem_limit_bytes=16 << 20)


def fourier_tables(length):
    counter = jnp.arange(length, dtype=jnp.int32)
    product = counter[:, None] * counter[None, :] % length
    angles = product.astype(jnp.float32) * (2.0 * math.pi / length)
    factor = 1.0 / math.sqrt(length)
    return (jnp.cos(angles) * factor, jnp.sin(angles) * factor)


def split(value):
    high = value.astype(BF16)
    return high, (value - high.astype(F32)).astype(BF16)


def share_row(part, dish):
    return part * 8 + dish if dish < 8 else 16 + part * 4 + dish - 8


def pieces_kernel(x_ref, out_ref):
    devices, frames_dev = out_ref.shape[:2]
    low = lax.broadcasted_iota(jnp.int32, (8, LANES), 0) < 4
    for frame in range(frames_dev):
        lanes = slice(frame * LANES, (frame + 1) * LANES)
        for dev in range(0, devices, 2):
            for one in (dev, dev + 1):
                for part in range(2):
                    out_ref[one, frame, part * 8 : part * 8 + 8, :] = x_ref[
                        part, one * 8 : one * 8 + 8, lanes
                    ]
            start = devices * 8 + dev * 4
            real = x_ref[0, start : start + 8, lanes]
            imag = x_ref[1, start : start + 8, lanes]
            out_ref[dev, frame, 16:24, :] = jnp.where(low, real, pltpu.roll(imag, 4, 0))
            out_ref[dev + 1, frame, 16:24, :] = jnp.where(low, pltpu.roll(real, 4, 0), imag)


def weights_kernel(w_ref, order_ref, slot_ref, out_ref):
    order = order_ref[...]
    beams = w_ref.shape[3]
    for half in range(2):
        hot = (slot_ref[:, half : half + 1] == order).astype(F32).T.astype(BF16)
        for part in range(2):
            turned = w_ref[0, part].T
            value = split(turned)[half]
            product = jnp.dot(value, hot, preferred_element_type=F32)
            rows = slice(part * beams, (part + 1) * beams)
            if half == 0:
                out_ref[0, rows, :] = product.astype(BF16)
            else:
                out_ref[0, rows, :] += product.astype(BF16)


def channel_kernel(x_ref, proto_ref, table_ref, taps_ref, out_ref, poly, spec, filt):
    frames = x_ref.shape[0]
    pfb_count = proto_ref.shape[0]
    fir_count = taps_ref.shape[0]
    group = 8
    low = lax.broadcasted_iota(jnp.int32, (group, 8, LANES), 1) < 4

    spec[0 : fir_count - 1] = jnp.zeros((fir_count - 1, 24, 2 * LANES), F32)
    for first in range(0, frames, group):
        found = []
        for rows in range(0, 24, 8):
            total = None
            for tap in range(pfb_count):
                begin = first - tap
                lost = max(0, -begin)
                if lost >= group:
                    continue
                block = x_ref[begin + lost : begin + group, rows : rows + 8, :]
                term = block * proto_ref[tap : tap + 1, :][None]
                if lost:
                    term = jnp.concatenate([jnp.zeros((lost, 8, LANES), F32), term], axis=0)
                total = term if total is None else total + term
            found.append(total)
        turned = pltpu.roll(found[2], 4, 1)
        other = [found[1], -found[0], jnp.where(low, turned, -turned)]
        for index in range(3):
            rows = slice(index * 8, index * 8 + 8)
            poly[first : first + group, rows, 0:LANES] = found[index]
            poly[first : first + group, rows, LANES : 2 * LANES] = other[index]

    for first in range(0, frames, group):
        value = poly[first : first + group].reshape(group * 24, 2 * LANES)
        high, rest = split(value)
        stacked = jnp.concatenate([high, rest, high], axis=1)
        product = jnp.dot(stacked, table_ref[...], preferred_element_type=F32)
        begin = first + fir_count - 1
        spec[begin : begin + group] = product.reshape(group, 24, 2 * LANES)

    for rows in range(0, 24, 8):
        for first in range(0, frames, group):
            total = None
            for tap in range(fir_count):
                begin = first + fir_count - 1 - tap
                near = spec[begin : begin + group, rows : rows + 8, 0:LANES]
                cross = spec[begin : begin + group, rows : rows + 8, LANES : 2 * LANES]
                term = taps_ref[tap, 0, rows : rows + 8, :][None] * near
                term = term + taps_ref[tap, 1, rows : rows + 8, :][None] * cross
                total = term if total is None else total + term
            for frame in range(group):
                begin = (first + frame) * 24 + rows
                filt[begin : begin + 8, :] = total[frame]

    per_band = out_ref.shape[1] // 6
    for pair in range(6):
        rows = [
            filt[pl.ds(share_row(part, pair * 2 + odd), frames, stride=24), :]
            for part in range(2)
            for odd in range(2)
        ]
        turned = jnp.concatenate(rows, axis=0).T
        for dev in range(out_ref.shape[0]):
            out_ref[dev, pair * per_band : (pair + 1) * per_band, :] = turned[
                dev * per_band : (dev + 1) * per_band
            ]


def beams_kernel(x_ref, w_ref, out_ref):
    rows = x_ref.shape[0] // 8
    beams = w_ref.shape[1] // 2
    lane = lax.broadcasted_iota(jnp.int32, (rows, LANES), 1)
    even = lane % 64 < 32
    wide = lax.broadcasted_iota(jnp.int32, (beams, LANES), 1)
    even_wide = wide % 64 < 32
    row = lax.broadcasted_iota(jnp.int32, (16, 2 * LANES), 0)
    column = lax.broadcasted_iota(jnp.int32, (16, 2 * LANES), 1)
    pool = jnp.where(row == column % 64 // INTEG, 1.0 / INTEG, 0.0).astype(BF16)
    for step in range(w_ref.shape[0] // 2):
        one = x_ref[pl.ds(2 * step, rows, stride=8), :]
        two = x_ref[pl.ds(2 * step + 1, rows, stride=8), :]
        first = jnp.where(even, one, pltpu.roll(two, 32, 1))
        second = jnp.where(even, pltpu.roll(one, LANES - 32, 1), two)
        field = jnp.concatenate([first, second], axis=0)
        high, rest = split(field)
        both = jnp.concatenate([high, rest], axis=1)
        both = jnp.concatenate([both, both], axis=0)
        sums = []
        for index in range(2):
            product = jnp.dot(w_ref[2 * step + index], both, preferred_element_type=F32)
            sums.append(product[:, 0:LANES] + product[:, LANES : 2 * LANES])
        by_real = jnp.where(even_wide, sums[0][:beams], sums[1][:beams])
        by_imag = jnp.where(even_wide, sums[0][beams:], sums[1][beams:])
        crossed = pltpu.roll(by_imag, 64, 1)
        beam = by_real + jnp.where(wide < 64, -crossed, crossed)
        high, rest = split(beam * beam)
        power = lax.dot_general(
            pool,
            jnp.concatenate([high, rest], axis=1),
            (((1,), (1,)), ((), ())),
            preferred_element_type=F32,
        )
        out_ref[2 * step] = power[0:8]
        out_ref[2 * step + 1] = power[8:16]


def slots_of(devices):
    dishes = np.zeros((2, devices, 6), np.int32)
    for odd in range(2):
        for dev in range(devices):
            for pair in range(6):
                own = pair * 2 + odd
                dishes[odd, dev, pair] = (
                    dev * 8 + own if own < 8 else devices * 8 + dev * 4 + own - 8
                )
    flat = dishes.reshape(-1)
    none = np.full_like(flat, -1)
    return np.stack([np.concatenate([flat, none]), np.concatenate([none, flat])], axis=1)


def dft_parts(channels):
    index = np.arange(channels)
    angle = 2.0 * np.pi * (index[:, None] * index[None, :] % channels) / channels
    cosine = np.cos(angle) / np.sqrt(channels)
    sine = np.sin(angle) / np.sqrt(channels)
    table = np.block([[cosine, sine], [sine, -cosine]]).astype(np.float32)
    high = table.astype(jnp.bfloat16)
    rest = (table - high.astype(np.float32)).astype(jnp.bfloat16)
    return np.concatenate([high, high, rest], axis=0)


def close_body(samples, prototype, dish_filter, beam_weights, dish_order):
    devices = lax.axis_size("band")
    position = lax.axis_index("band")
    channels = prototype.shape[1]
    fir_count = dish_filter.shape[1]
    dishes = dish_filter.shape[2]
    band_chans = beam_weights.shape[1]
    beams = beam_weights.shape[4]
    frames_dev = samples.shape[2] // channels
    frames = frames_dev * devices

    pieces = pl.pallas_call(
        pieces_kernel,
        out_shape=jax.ShapeDtypeStruct((devices, frames_dev, 24, channels), F32),
        in_specs=[VMEM],
        out_specs=VMEM,
        name="pieces",
        compiler_params=GRANT,
    )(samples)
    arrived = lax.all_to_all(pieces, "band", split_axis=0, concat_axis=0, tiled=True)

    eight = lax.dynamic_slice_in_dim(dish_filter, position * 8, 8, 2)
    four = lax.dynamic_slice_in_dim(dish_filter, devices * 8 + position * 4, 4, 2)
    taps = jnp.concatenate([eight, eight, four, four], axis=2)
    taps = jnp.transpose(taps, (1, 0, 2, 3))
    weights = pl.pallas_call(
        weights_kernel,
        grid=(band_chans,),
        out_shape=jax.ShapeDtypeStruct((band_chans, 2 * beams, 2 * dishes), BF16),
        in_specs=[
            pl.BlockSpec((1, 2, dishes, beams), lambda i: (i, 0, 0, 0)),
            pl.BlockSpec((1, dishes), lambda i: (0, 0)),
            pl.BlockSpec((2 * dishes, 2), lambda i: (0, 0)),
        ],
        out_specs=pl.BlockSpec((1, 2 * beams, 2 * dishes), lambda i: (i, 0, 0)),
        name="weights",
        compiler_params=GRANT,
        cost_estimate=pl.CostEstimate(
            flops=8 * 4 * 2 * 192 * 192 * 384, bytes_accessed=5 << 20, transcendentals=0
        ),
    )(beam_weights[0], dish_order.reshape(1, dishes), slots_of(devices))

    filtered = pl.pallas_call(
        channel_kernel,
        out_shape=jax.ShapeDtypeStruct((devices, 6 * band_chans, channels), F32),
        in_specs=[VMEM] * 4,
        out_specs=VMEM,
        scratch_shapes=[
            pltpu.VMEM((frames, 24, 2 * LANES), F32),
            pltpu.VMEM((frames + fir_count - 1, 24, 2 * LANES), F32),
            pltpu.VMEM((frames * 24, LANES), F32),
        ],
        name="channels",
        compiler_params=GRANT,
    )(arrived.reshape(frames, 24, channels), prototype, dft_parts(channels), taps)
    field = lax.all_to_all(filtered, "band", split_axis=0, concat_axis=0, tiled=True)
    field = field.reshape(devices * 6 * band_chans, channels)

    power = pl.pallas_call(
        beams_kernel,
        out_shape=jax.ShapeDtypeStruct((band_chans, frames // INTEG, beams), F32),
        in_specs=[VMEM] * 2,
        out_specs=VMEM,
        name="beams",
        compiler_params=GRANT,
    )(field, weights)
    return jnp.transpose(power, (0, 2, 1))[None]


def detect(weights, field_real, field_imag):
    def contract(weight_part, field_part):
        return jnp.einsum("qds,dqf->qsf", weight_part, field_part, precision=HIGHEST)

    beam_real = contract(weights[:, 0], field_real) - contract(weights[:, 1], field_imag)
    beam_imag = contract(weights[:, 0], field_imag) + contract(weights[:, 1], field_real)
    energy = beam_real * beam_real + beam_imag * beam_imag
    shaped = energy.reshape(energy.shape[:-1] + (energy.shape[-1] // INTEG, INTEG))
    return jnp.mean(shaped, axis=-1)


def wide_body(samples, prototype, dish_filter, beam_weights, dish_order):
    devices = lax.axis_size("band")
    position = lax.axis_index("band")
    pfb_count, channels = prototype.shape
    fir_count = dish_filter.shape[1]
    dishes = dish_filter.shape[2]
    band_chans = beam_weights.shape[1]
    bands = channels // band_chans
    owners = devices // bands
    frames_dev = samples.shape[2] // channels
    frames = frames_dev * devices
    share = -(-dishes // devices)
    extra = share * devices - dishes

    padded = jnp.pad(samples, ((0, 0), (0, extra), (0, 0)))
    pieces = padded.reshape(2, devices, share, frames_dev, channels)
    pieces = jnp.transpose(pieces, (1, 3, 0, 2, 4)).reshape(
        devices, frames_dev, 2 * share, channels
    )
    arrived = lax.all_to_all(pieces, "band", split_axis=0, concat_axis=0, tiled=True)
    blocks = arrived.reshape(frames, 2 * share, channels)

    history = jnp.pad(blocks, ((pfb_count - 1, 0), (0, 0), (0, 0)))
    polyphase = jnp.zeros_like(blocks)
    for tap_index in range(pfb_count):
        offset = pfb_count - 1 - tap_index
        polyphase = polyphase + prototype[tap_index] * history[offset : offset + frames]
    cosine, sine = fourier_tables(channels)
    both = jnp.dot(polyphase, jnp.concatenate([cosine, sine], axis=1), precision=HIGHEST)
    with_cos = both[..., :channels].reshape(frames, 2, share, channels)
    with_sin = both[..., channels:].reshape(frames, 2, share, channels)
    spec_real = with_cos[:, 0] + with_sin[:, 1]
    spec_imag = with_cos[:, 1] - with_sin[:, 0]

    taps = jnp.pad(dish_filter, ((0, 0), (0, 0), (0, extra), (0, 0)))
    taps = lax.dynamic_slice_in_dim(taps, position * share, share, 2)
    lead = ((fir_count - 1, 0), (0, 0), (0, 0))
    past_real, past_imag = jnp.pad(spec_real, lead), jnp.pad(spec_imag, lead)
    out_real = jnp.zeros_like(spec_real)
    out_imag = jnp.zeros_like(spec_imag)
    for tap_index in range(fir_count):
        offset = fir_count - 1 - tap_index
        part_real = past_real[offset : offset + frames]
        part_imag = past_imag[offset : offset + frames]
        factor_real, factor_imag = taps[0, tap_index], taps[1, tap_index]
        out_real = out_real + factor_real * part_real - factor_imag * part_imag
        out_imag = out_imag + factor_real * part_imag + factor_imag * part_real

    filtered = jnp.stack([out_real, out_imag])
    filtered = filtered.reshape(2, frames, share, bands, band_chans)
    filtered = jnp.transpose(filtered, (3, 0, 2, 4, 1)).reshape(
        bands, 2 * share, band_chans * frames
    )
    filtered = jnp.repeat(filtered, owners, axis=0)
    field = lax.all_to_all(filtered, "band", split_axis=0, concat_axis=0, tiled=True)
    field = field.reshape(devices, 2, share, band_chans, frames)
    field = jnp.transpose(field, (1, 0, 2, 3, 4))
    field = field.reshape(2, devices * share, band_chans, frames)
    field = jnp.take(field, dish_order, axis=1)
    power = detect(beam_weights[0], field[0], field[1])
    return power[None]


def solution(mesh):
    devices = mesh.shape["band"]

    def body(samples, prototype, dish_filter, beam_weights, dish_order):
        channels = prototype.shape[1]
        close = (
            channels == LANES
            and beam_weights.shape[1] == 8
            and devices * 8 == channels
            and dish_filter.shape[2] == 12 * devices
            and samples.shape[2] * devices == 32 * channels
        )
        chosen = close_body if close else wide_body
        return chosen(samples, prototype, dish_filter, beam_weights, dish_order)

    placed = (P(None, None, ("grp", "band")), P(), P(), P("band", None, None, None, None), P())
    return jax.shard_map(
        body,
        mesh=mesh,
        in_specs=placed,
        out_specs=P(("grp", "band"), None, None, None),
        check_vma=False,
    )
```

```python
import math

import jax
import jax.numpy as jnp
import numpy as np
from jax import lax
from jax.experimental import pallas as pl
from jax.experimental.pallas import tpu as pltpu
from jax.sharding import PartitionSpec as P

INTEG = 4
HIGHEST = lax.Precision.HIGHEST
F32 = jnp.float32
BF16 = jnp.bfloat16
LANES = 128
VMEM = pl.BlockSpec(memory_space=pltpu.VMEM)
GRANT = pltpu.CompilerParams(vmem_limit_bytes=16 << 20)


def fourier_tables(length):
    counter = jnp.arange(length, dtype=jnp.int32)
    product = counter[:, None] * counter[None, :] % length
    angles = product.astype(jnp.float32) * (2.0 * math.pi / length)
    factor = 1.0 / math.sqrt(length)
    return (jnp.cos(angles) * factor, jnp.sin(angles) * factor)


def split(value):
    high = value.astype(BF16)
    return high, (value - high.astype(F32)).astype(BF16)


CHUNKS = (8, 4)


def eight_kernel(x_ref, out_ref, sems):
    devices, frames_dev = out_ref.shape[:2]
    tiles = x_ref.reshape(2, x_ref.shape[1] // 8, 8, x_ref.shape[2])
    copies = []
    for frame in range(frames_dev):
        for part in range(2):
            lanes = slice(frame * LANES, (frame + 1) * LANES)
            copies.append(
                pltpu.make_async_copy(
                    tiles.at[part, 0:devices, :, lanes],
                    out_ref.at[:, frame, part * 8 : part * 8 + 8, :],
                    sems.at[frame, part],
                )
            )
    for copy in copies:
        copy.start()
    for copy in copies:
        copy.wait()


def four_kernel(x_ref, out_ref):
    devices, frames_dev = out_ref.shape[:2]
    low = lax.broadcasted_iota(jnp.int32, (8, LANES), 0) < 4
    for frame in range(frames_dev):
        lanes = slice(frame * LANES, (frame + 1) * LANES)
        for dev in range(0, devices, 2):
            real = x_ref[0, dev * 4 : dev * 4 + 8, lanes]
            imag = x_ref[1, dev * 4 : dev * 4 + 8, lanes]
            out_ref[dev, frame] = jnp.where(low, real, pltpu.roll(imag, 4, 0))
            out_ref[dev + 1, frame] = jnp.where(low, pltpu.roll(real, 4, 0), imag)


def weights_kernel(w_ref, order_ref, slot_ref, *out_refs):
    hot = (slot_ref[...] == order_ref[...]).astype(F32).T.astype(BF16)
    beams = w_ref.shape[3]
    for part in range(2):
        halves = [
            jnp.dot(half, hot, preferred_element_type=F32).astype(BF16)
            for half in split(w_ref[0, part].T)
        ]
        begin = 0
        for out_ref in out_refs:
            width = out_ref.shape[2] // 2
            both = [half[:, begin : begin + width] for half in halves]
            out_ref[0, part * beams : (part + 1) * beams, :] = jnp.concatenate(both, axis=1)
            begin += width


def channel_kernel(after_ref, x_ref, proto_ref, table_ref, taps_ref, out_ref, poly, spec, filt):
    frames, height = x_ref.shape[:2]
    count = height // 2
    pfb_count = proto_ref.shape[0]
    fir_count = taps_ref.shape[0]
    group = 8
    low = lax.broadcasted_iota(jnp.int32, (group, 8, LANES), 1) < 4

    spec[0 : fir_count - 1] = jnp.zeros((fir_count - 1, height, 2 * LANES), F32)
    for first in range(0, frames, group):
        found = []
        for rows in range(0, height, 8):
            total = None
            for tap in range(pfb_count):
                begin = first - tap
                lost = max(0, -begin)
                if lost >= group:
                    continue
                block = x_ref[begin + lost : begin + group, rows : rows + 8, :]
                term = block * proto_ref[tap : tap + 1, :][None]
                if lost:
                    term = jnp.concatenate([jnp.zeros((lost, 8, LANES), F32), term], axis=0)
                total = term if total is None else total + term
            found.append(total)
        if count == 8:
            other = [found[1], -found[0]]
        else:
            turned = pltpu.roll(found[0], 4, 1)
            other = [jnp.where(low, turned, -turned)]
        for index in range(height // 8):
            rows = slice(index * 8, index * 8 + 8)
            poly[first : first + group, rows, 0:LANES] = found[index]
            poly[first : first + group, rows, LANES : 2 * LANES] = other[index]

    for first in range(0, frames, group):
        value = poly[first : first + group].reshape(group * height, 2 * LANES)
        high, rest = split(value)
        stacked = jnp.concatenate([high, rest, high], axis=1)
        product = jnp.dot(stacked, table_ref[...], preferred_element_type=F32)
        begin = first + fir_count - 1
        spec[begin : begin + group] = product.reshape(group, height, 2 * LANES)

    for rows in range(0, height, 8):
        for first in range(0, frames, group):
            total = None
            for tap in range(fir_count):
                begin = first + fir_count - 1 - tap
                near = spec[begin : begin + group, rows : rows + 8, 0:LANES]
                cross = spec[begin : begin + group, rows : rows + 8, LANES : 2 * LANES]
                term = taps_ref[tap, 0, rows : rows + 8, :][None] * near
                term = term + taps_ref[tap, 1, rows : rows + 8, :][None] * cross
                total = term if total is None else total + term
            for frame in range(group):
                begin = (first + frame) * height + rows
                filt[begin : begin + 8, :] = total[frame]

    per_band = out_ref.shape[1] // (count // 2)
    for pair in range(count // 2):
        rows = [
            filt[pl.ds(part * count + pair * 2 + odd, frames, stride=height), :]
            for part in range(2)
            for odd in range(2)
        ]
        turned = jnp.concatenate(rows, axis=0).T
        for dev in range(out_ref.shape[0]):
            out_ref[dev, pair * per_band : (pair + 1) * per_band, :] = turned[
                dev * per_band : (dev + 1) * per_band
            ]


def pair_beams(x_ref, w_ref, step):
    rows = x_ref.shape[0] // 8
    beams = w_ref.shape[1] // 2
    lane = lax.broadcasted_iota(jnp.int32, (rows, LANES), 1)
    even = lane % 64 < 32
    wide = lax.broadcasted_iota(jnp.int32, (beams, LANES), 1)
    even_wide = wide % 64 < 32
    one = x_ref[pl.ds(2 * step, rows, stride=8), :]
    two = x_ref[pl.ds(2 * step + 1, rows, stride=8), :]
    first = jnp.where(even, one, pltpu.roll(two, 32, 1))
    second = jnp.where(even, pltpu.roll(one, LANES - 32, 1), two)
    field = jnp.concatenate([first, second], axis=0)
    high, rest = split(field)
    both = jnp.concatenate([high, rest], axis=1)
    both = jnp.concatenate([both, both], axis=0)
    sums = []
    for index in range(2):
        product = jnp.dot(w_ref[2 * step + index], both, preferred_element_type=F32)
        sums.append(product[:, 0:LANES] + product[:, LANES : 2 * LANES])
    by_real = jnp.where(even_wide, sums[0][:beams], sums[1][:beams])
    by_imag = jnp.where(even_wide, sums[0][beams:], sums[1][beams:])
    crossed = pltpu.roll(by_imag, 64, 1)
    return by_real + jnp.where(wide < 64, -crossed, crossed)


def beams_kernel(*refs):
    x_ref, w_ref, out_ref = refs[0], refs[1], refs[-1]
    for step in range(w_ref.shape[0] // 2):
        beam = pair_beams(x_ref, w_ref, step)
        if len(refs) == 4:
            beam = beam + refs[2][step]
        out_ref[step] = beam


def power_kernel(*refs):
    x_ref, w_ref, out_ref = refs[0], refs[1], refs[-1]
    row = lax.broadcasted_iota(jnp.int32, (16, 2 * LANES), 0)
    column = lax.broadcasted_iota(jnp.int32, (16, 2 * LANES), 1)
    pool = jnp.where(row == column % 64 // INTEG, 1.0 / INTEG, 0.0).astype(BF16)
    for step in range(w_ref.shape[0] // 2):
        beam = pair_beams(x_ref, w_ref, step)
        if len(refs) == 4:
            beam = beam + refs[2][step]
        high, rest = split(beam * beam)
        power = lax.dot_general(
            pool,
            jnp.concatenate([high, rest], axis=1),
            (((1,), (1,)), ((), ())),
            preferred_element_type=F32,
        )
        out_ref[2 * step] = power[0:8]
        out_ref[2 * step + 1] = power[8:16]


def slots_of(devices):
    found, base = [], 0
    for count in CHUNKS:
        dishes = base + np.arange(count * devices, dtype=np.int32)
        found.append(dishes.reshape(devices, count // 2, 2).transpose(2, 0, 1).reshape(-1))
        base += count * devices
    return np.concatenate(found)[:, None]


def dft_parts(channels):
    index = np.arange(channels)
    angle = 2.0 * np.pi * (index[:, None] * index[None, :] % channels) / channels
    cosine = np.cos(angle) / np.sqrt(channels)
    sine = np.sin(angle) / np.sqrt(channels)
    table = np.block([[cosine, sine], [sine, -cosine]]).astype(np.float32)
    high = table.astype(jnp.bfloat16)
    rest = (table - high.astype(np.float32)).astype(jnp.bfloat16)
    return np.concatenate([high, high, rest], axis=0)


def close_body(samples, prototype, dish_filter, beam_weights, dish_order):
    devices = lax.axis_size("band")
    position = lax.axis_index("band")
    channels = prototype.shape[1]
    fir_count = dish_filter.shape[1]
    dishes = dish_filter.shape[2]
    band_chans = beam_weights.shape[1]
    beams = beam_weights.shape[4]
    frames_dev = samples.shape[2] // channels
    frames = frames_dev * devices

    def exchange(value):
        return lax.all_to_all(value, "band", split_axis=0, concat_axis=0, tiled=True)

    eight = pl.pallas_call(
        eight_kernel,
        out_shape=jax.ShapeDtypeStruct((devices, frames_dev, 16, channels), F32),
        in_specs=[pl.BlockSpec(memory_space=pl.ANY)],
        out_specs=pl.BlockSpec(memory_space=pl.ANY),
        scratch_shapes=[pltpu.SemaphoreType.DMA((frames_dev, 2))],
        name="eight",
        compiler_params=GRANT,
    )(samples)
    eight = exchange(eight)
    rest = dishes - devices * 8
    four = pl.pallas_call(
        four_kernel,
        grid=(1,),
        out_shape=jax.ShapeDtypeStruct((devices, frames_dev, 8, channels), F32),
        in_specs=[
            pl.BlockSpec((2, rest, samples.shape[2]), lambda i: (0, devices * 8 // rest, 0))
        ],
        out_specs=pl.BlockSpec((devices, frames_dev, 8, channels), lambda i: (0, 0, 0, 0)),
        name="four",
        compiler_params=GRANT,
    )(samples)
    four = exchange(four)
    arrived = [eight, four]

    weights = pl.pallas_call(
        weights_kernel,
        grid=(band_chans,),
        out_shape=[
            jax.ShapeDtypeStruct((band_chans, 2 * beams, 2 * count * devices), BF16)
            for count in CHUNKS
        ],
        in_specs=[
            pl.BlockSpec((1, 2, dishes, beams), lambda i: (i, 0, 0, 0)),
            pl.BlockSpec((1, dishes), lambda i: (0, 0)),
            pl.BlockSpec((dishes, 1), lambda i: (0, 0)),
        ],
        out_specs=[
            pl.BlockSpec((1, 2 * beams, 2 * count * devices), lambda i: (i, 0, 0))
            for count in CHUNKS
        ],
        name="weights",
        compiler_params=GRANT,
        cost_estimate=pl.CostEstimate(
            flops=8 * 4 * 2 * 192 * 192 * 384, bytes_accessed=5 << 20, transcendentals=0
        ),
    )(beam_weights[0], dish_order.reshape(1, dishes), slots_of(devices))

    table = dft_parts(channels)
    fields, base = [], 0
    for count, value in zip(CHUNKS, arrived):
        height = 2 * count
        taps = lax.dynamic_slice_in_dim(dish_filter, base + position * count, count, 2)
        taps = jnp.transpose(jnp.concatenate([taps, taps], axis=2), (1, 0, 2, 3))
        base += count * devices
        filtered = pl.pallas_call(
            channel_kernel,
            out_shape=jax.ShapeDtypeStruct(
                (devices, count // 2 * band_chans, channels), F32
            ),
            in_specs=[pl.BlockSpec(memory_space=pl.ANY)] + [VMEM] * 4,
            out_specs=VMEM,
            scratch_shapes=[
                pltpu.VMEM((frames, height, 2 * LANES), F32),
                pltpu.VMEM((frames + fir_count - 1, height, 2 * LANES), F32),
                pltpu.VMEM((frames * height, LANES), F32),
            ],
            name=f"channels_of_{count}",
            compiler_params=GRANT,
        )(weights[-1], value.reshape(frames, height, channels), prototype, table, taps)
        fields.append(exchange(filtered))

    partial = []
    for index, count in enumerate(CHUNKS):
        last = index + 1 == len(CHUNKS)
        shape = (band_chans, frames // INTEG, beams) if last else (band_chans // 2, beams, LANES)
        partial = [
            pl.pallas_call(
                power_kernel if last else beams_kernel,
                out_shape=jax.ShapeDtypeStruct(shape, F32),
                in_specs=[VMEM] * (2 + len(partial)),
                out_specs=VMEM,
                name="power" if last else f"beams_{index}",
                compiler_params=GRANT,
            )(fields[index].reshape(-1, channels), weights[index], *partial)
        ]
    return jnp.transpose(partial[0], (0, 2, 1))[None]


def detect(weights, field_real, field_imag):
    def contract(weight_part, field_part):
        return jnp.einsum("qds,dqf->qsf", weight_part, field_part, precision=HIGHEST)

    beam_real = contract(weights[:, 0], field_real) - contract(weights[:, 1], field_imag)
    beam_imag = contract(weights[:, 0], field_imag) + contract(weights[:, 1], field_real)
    energy = beam_real * beam_real + beam_imag * beam_imag
    shaped = energy.reshape(energy.shape[:-1] + (energy.shape[-1] // INTEG, INTEG))
    return jnp.mean(shaped, axis=-1)


def wide_body(samples, prototype, dish_filter, beam_weights, dish_order):
    devices = lax.axis_size("band")
    position = lax.axis_index("band")
    pfb_count, channels = prototype.shape
    fir_count = dish_filter.shape[1]
    dishes = dish_filter.shape[2]
    band_chans = beam_weights.shape[1]
    bands = channels // band_chans
    owners = devices // bands
    frames_dev = samples.shape[2] // channels
    frames = frames_dev * devices
    share = -(-dishes // devices)
    extra = share * devices - dishes

    padded = jnp.pad(samples, ((0, 0), (0, extra), (0, 0)))
    pieces = padded.reshape(2, devices, share, frames_dev, channels)
    pieces = jnp.transpose(pieces, (1, 3, 0, 2, 4)).reshape(
        devices, frames_dev, 2 * share, channels
    )
    arrived = lax.all_to_all(pieces, "band", split_axis=0, concat_axis=0, tiled=True)
    blocks = arrived.reshape(frames, 2 * share, channels)

    history = jnp.pad(blocks, ((pfb_count - 1, 0), (0, 0), (0, 0)))
    polyphase = jnp.zeros_like(blocks)
    for tap_index in range(pfb_count):
        offset = pfb_count - 1 - tap_index
        polyphase = polyphase + prototype[tap_index] * history[offset : offset + frames]
    cosine, sine = fourier_tables(channels)
    both = jnp.dot(polyphase, jnp.concatenate([cosine, sine], axis=1), precision=HIGHEST)
    with_cos = both[..., :channels].reshape(frames, 2, share, channels)
    with_sin = both[..., channels:].reshape(frames, 2, share, channels)
    spec_real = with_cos[:, 0] + with_sin[:, 1]
    spec_imag = with_cos[:, 1] - with_sin[:, 0]

    taps = jnp.pad(dish_filter, ((0, 0), (0, 0), (0, extra), (0, 0)))
    taps = lax.dynamic_slice_in_dim(taps, position * share, share, 2)
    lead = ((fir_count - 1, 0), (0, 0), (0, 0))
    past_real, past_imag = jnp.pad(spec_real, lead), jnp.pad(spec_imag, lead)
    out_real = jnp.zeros_like(spec_real)
    out_imag = jnp.zeros_like(spec_imag)
    for tap_index in range(fir_count):
        offset = fir_count - 1 - tap_index
        part_real = past_real[offset : offset + frames]
        part_imag = past_imag[offset : offset + frames]
        factor_real, factor_imag = taps[0, tap_index], taps[1, tap_index]
        out_real = out_real + factor_real * part_real - factor_imag * part_imag
        out_imag = out_imag + factor_real * part_imag + factor_imag * part_real

    filtered = jnp.stack([out_real, out_imag])
    filtered = filtered.reshape(2, frames, share, bands, band_chans)
    filtered = jnp.transpose(filtered, (3, 0, 2, 4, 1)).reshape(
        bands, 2 * share, band_chans * frames
    )
    filtered = jnp.repeat(filtered, owners, axis=0)
    field = lax.all_to_all(filtered, "band", split_axis=0, concat_axis=0, tiled=True)
    field = field.reshape(devices, 2, share, band_chans, frames)
    field = jnp.transpose(field, (1, 0, 2, 3, 4))
    field = field.reshape(2, devices * share, band_chans, frames)
    field = jnp.take(field, dish_order, axis=1)
    power = detect(beam_weights[0], field[0], field[1])
    return power[None]


def solution(mesh):
    devices = mesh.shape["band"]

    def body(samples, prototype, dish_filter, beam_weights, dish_order):
        channels = prototype.shape[1]
        close = (
            channels == LANES
            and beam_weights.shape[1] == 8
            and devices * 8 == channels
            and dish_filter.shape[2] == 12 * devices
            and samples.shape[2] * devices == 32 * channels
        )
        chosen = close_body if close else wide_body
        return chosen(samples, prototype, dish_filter, beam_weights, dish_order)

    placed = (P(None, None, ("grp", "band")), P(), P(), P("band", None, None, None, None), P())
    return jax.shard_map(
        body,
        mesh=mesh,
        in_specs=placed,
        out_specs=P(("grp", "band"), None, None, None),
        check_vma=False,
    )
```

```python
import math

import jax
import jax.numpy as jnp
import numpy as np
from jax import lax
from jax.experimental import pallas as pl
from jax.experimental.pallas import tpu as pltpu
from jax.sharding import PartitionSpec as P

INTEG = 4
HIGHEST = lax.Precision.HIGHEST
F32 = jnp.float32
BF16 = jnp.bfloat16
LANES = 128
VMEM = pl.BlockSpec(memory_space=pltpu.VMEM)
HBM = pl.BlockSpec(memory_space=pltpu.HBM)
GRANT = pltpu.CompilerParams(vmem_limit_bytes=16 << 20)


def fourier_tables(length):
    counter = jnp.arange(length, dtype=jnp.int32)
    product = counter[:, None] * counter[None, :] % length
    angles = product.astype(jnp.float32) * (2.0 * math.pi / length)
    factor = 1.0 / math.sqrt(length)
    return (jnp.cos(angles) * factor, jnp.sin(angles) * factor)


def split(value):
    high = value.astype(BF16)
    return high, (value - high.astype(F32)).astype(BF16)


def share_row(part, dish):
    return part * 8 + dish if dish < 8 else 16 + part * 4 + dish - 8


def pieces_kernel(x_ref, out_ref, rest, four, tile_sems, rest_sem, four_sem):
    devices, frames_dev = out_ref.shape[:2]
    low = lax.broadcasted_iota(jnp.int32, (8, LANES), 0) < 4
    load = pltpu.make_async_copy(x_ref.at[:, devices * 8 :, :], rest, rest_sem)
    load.start()
    tiles = x_ref.reshape(2, x_ref.shape[1] // 8, 8, x_ref.shape[2])
    moves = []
    for frame in range(frames_dev):
        lanes = slice(frame * LANES, (frame + 1) * LANES)
        for part in range(2):
            moves.append(
                pltpu.make_async_copy(
                    tiles.at[part, 0:devices, :, lanes],
                    out_ref.at[:, frame, part * 8 : part * 8 + 8, :],
                    tile_sems.at[frame, part],
                )
            )
    for move in moves:
        move.start()
    load.wait()
    for frame in range(frames_dev):
        lanes = slice(frame * LANES, (frame + 1) * LANES)
        for dev in range(0, devices, 2):
            real = rest[0, dev * 4 : dev * 4 + 8, lanes]
            imag = rest[1, dev * 4 : dev * 4 + 8, lanes]
            four[dev, frame] = jnp.where(low, real, pltpu.roll(imag, 4, 0))
            four[dev + 1, frame] = jnp.where(low, pltpu.roll(real, 4, 0), imag)
    store = pltpu.make_async_copy(four, out_ref.at[:, :, 16:24, :], four_sem)
    store.start()
    for move in moves:
        move.wait()
    store.wait()


def weights_kernel(w_ref, order_ref, slot_ref, out_ref):
    order = order_ref[...]
    beams = w_ref.shape[3]
    for half in range(2):
        hot = (slot_ref[:, half : half + 1] == order).astype(F32).T.astype(BF16)
        for part in range(2):
            turned = w_ref[0, part].T
            value = split(turned)[half]
            product = jnp.dot(value, hot, preferred_element_type=F32)
            rows = slice(part * beams, (part + 1) * beams)
            if half == 0:
                out_ref[0, rows, :] = product.astype(BF16)
            else:
                out_ref[0, rows, :] += product.astype(BF16)


def channel_kernel(x_ref, proto_ref, table_ref, taps_ref, out_ref, poly, spec, filt):
    frames = x_ref.shape[0]
    pfb_count = proto_ref.shape[0]
    fir_count = taps_ref.shape[0]
    group = 8
    low = lax.broadcasted_iota(jnp.int32, (group, 8, LANES), 1) < 4

    spec[0 : fir_count - 1] = jnp.zeros((fir_count - 1, 24, 2 * LANES), F32)
    for first in range(0, frames, group):
        found = []
        for rows in range(0, 24, 8):
            total = None
            for tap in range(pfb_count):
                begin = first - tap
                lost = max(0, -begin)
                if lost >= group:
                    continue
                block = x_ref[begin + lost : begin + group, rows : rows + 8, :]
                term = block * proto_ref[tap : tap + 1, :][None]
                if lost:
                    term = jnp.concatenate([jnp.zeros((lost, 8, LANES), F32), term], axis=0)
                total = term if total is None else total + term
            found.append(total)
        turned = pltpu.roll(found[2], 4, 1)
        other = [found[1], -found[0], jnp.where(low, turned, -turned)]
        for index in range(3):
            rows = slice(index * 8, index * 8 + 8)
            poly[first : first + group, rows, 0:LANES] = found[index]
            poly[first : first + group, rows, LANES : 2 * LANES] = other[index]

    for first in range(0, frames, group):
        value = poly[first : first + group].reshape(group * 24, 2 * LANES)
        high, rest = split(value)
        stacked = jnp.concatenate([high, rest, high], axis=1)
        product = jnp.dot(stacked, table_ref[...], preferred_element_type=F32)
        begin = first + fir_count - 1
        spec[begin : begin + group] = product.reshape(group, 24, 2 * LANES)

    for rows in range(0, 24, 8):
        for first in range(0, frames, group):
            total = None
            for tap in range(fir_count):
                begin = first + fir_count - 1 - tap
                near = spec[begin : begin + group, rows : rows + 8, 0:LANES]
                cross = spec[begin : begin + group, rows : rows + 8, LANES : 2 * LANES]
                term = taps_ref[tap, 0, rows : rows + 8, :][None] * near
                term = term + taps_ref[tap, 1, rows : rows + 8, :][None] * cross
                total = term if total is None else total + term
            for frame in range(group):
                begin = (first + frame) * 24 + rows
                filt[begin : begin + 8, :] = total[frame]

    per_band = out_ref.shape[1] // 6
    for pair in range(6):
        rows = [
            filt[pl.ds(share_row(part, pair * 2 + odd), frames, stride=24), :]
            for part in range(2)
            for odd in range(2)
        ]
        turned = jnp.concatenate(rows, axis=0).T
        for dev in range(out_ref.shape[0]):
            out_ref[dev, pair * per_band : (pair + 1) * per_band, :] = turned[
                dev * per_band : (dev + 1) * per_band
            ]


def beams_kernel(x_ref, w_hbm, out_ref, w_ref, sems):
    loads = [
        pltpu.make_async_copy(
            w_hbm.at[2 * step : 2 * step + 2], w_ref.at[2 * step : 2 * step + 2], sems.at[step]
        )
        for step in range(w_hbm.shape[0] // 2)
    ]
    for load in loads:
        load.start()
    rows = x_ref.shape[0] // 8
    beams = w_ref.shape[1] // 2
    lane = lax.broadcasted_iota(jnp.int32, (rows, LANES), 1)
    even = lane % 64 < 32
    wide = lax.broadcasted_iota(jnp.int32, (beams, LANES), 1)
    even_wide = wide % 64 < 32
    row = lax.broadcasted_iota(jnp.int32, (16, 2 * LANES), 0)
    column = lax.broadcasted_iota(jnp.int32, (16, 2 * LANES), 1)
    pool = jnp.where(row == column % 64 // INTEG, 1.0 / INTEG, 0.0).astype(BF16)
    for step in range(w_ref.shape[0] // 2):
        one = x_ref[pl.ds(2 * step, rows, stride=8), :]
        two = x_ref[pl.ds(2 * step + 1, rows, stride=8), :]
        first = jnp.where(even, one, pltpu.roll(two, 32, 1))
        second = jnp.where(even, pltpu.roll(one, LANES - 32, 1), two)
        field = jnp.concatenate([first, second], axis=0)
        high, rest = split(field)
        both = jnp.concatenate([high, rest], axis=1)
        both = jnp.concatenate([both, both], axis=0)
        loads[step].wait()
        sums = []
        for index in range(2):
            product = jnp.dot(w_ref[2 * step + index], both, preferred_element_type=F32)
            sums.append(product[:, 0:LANES] + product[:, LANES : 2 * LANES])
        by_real = jnp.where(even_wide, sums[0][:beams], sums[1][:beams])
        by_imag = jnp.where(even_wide, sums[0][beams:], sums[1][beams:])
        crossed = pltpu.roll(by_imag, 64, 1)
        beam = by_real + jnp.where(wide < 64, -crossed, crossed)
        high, rest = split(beam * beam)
        power = lax.dot_general(
            pool,
            jnp.concatenate([high, rest], axis=1),
            (((1,), (1,)), ((), ())),
            preferred_element_type=F32,
        )
        out_ref[2 * step] = power[0:8]
        out_ref[2 * step + 1] = power[8:16]


def slots_of(devices):
    dishes = np.zeros((2, devices, 6), np.int32)
    for odd in range(2):
        for dev in range(devices):
            for pair in range(6):
                own = pair * 2 + odd
                dishes[odd, dev, pair] = (
                    dev * 8 + own if own < 8 else devices * 8 + dev * 4 + own - 8
                )
    flat = dishes.reshape(-1)
    none = np.full_like(flat, -1)
    return np.stack([np.concatenate([flat, none]), np.concatenate([none, flat])], axis=1)


def dft_parts(channels):
    index = np.arange(channels)
    angle = 2.0 * np.pi * (index[:, None] * index[None, :] % channels) / channels
    cosine = np.cos(angle) / np.sqrt(channels)
    sine = np.sin(angle) / np.sqrt(channels)
    table = np.block([[cosine, sine], [sine, -cosine]]).astype(np.float32)
    high = table.astype(jnp.bfloat16)
    rest = (table - high.astype(np.float32)).astype(jnp.bfloat16)
    return np.concatenate([high, high, rest], axis=0)


def close_body(samples, prototype, dish_filter, beam_weights, dish_order):
    devices = lax.axis_size("band")
    position = lax.axis_index("band")
    channels = prototype.shape[1]
    fir_count = dish_filter.shape[1]
    dishes = dish_filter.shape[2]
    band_chans = beam_weights.shape[1]
    beams = beam_weights.shape[4]
    frames_dev = samples.shape[2] // channels
    frames = frames_dev * devices

    pieces = pl.pallas_call(
        pieces_kernel,
        out_shape=jax.ShapeDtypeStruct((devices, frames_dev, 24, channels), F32),
        in_specs=[HBM],
        out_specs=HBM,
        scratch_shapes=[
            pltpu.VMEM((2, dishes - devices * 8, frames_dev * channels), F32),
            pltpu.VMEM((devices, frames_dev, 8, channels), F32),
            pltpu.SemaphoreType.DMA((frames_dev, 2)),
            pltpu.SemaphoreType.DMA(()),
            pltpu.SemaphoreType.DMA(()),
        ],
        name="pieces",
        compiler_params=GRANT,
    )(samples)
    arrived = lax.all_to_all(pieces, "band", split_axis=0, concat_axis=0, tiled=True)

    eight = lax.dynamic_slice_in_dim(dish_filter, position * 8, 8, 2)
    four = lax.dynamic_slice_in_dim(dish_filter, devices * 8 + position * 4, 4, 2)
    taps = jnp.concatenate([eight, eight, four, four], axis=2)
    taps = jnp.transpose(taps, (1, 0, 2, 3))
    weights = pl.pallas_call(
        weights_kernel,
        grid=(band_chans,),
        out_shape=jax.ShapeDtypeStruct((band_chans, 2 * beams, 2 * dishes), BF16),
        in_specs=[
            pl.BlockSpec((1, 2, dishes, beams), lambda i: (i, 0, 0, 0)),
            pl.BlockSpec((1, dishes), lambda i: (0, 0)),
            pl.BlockSpec((2 * dishes, 2), lambda i: (0, 0)),
        ],
        out_specs=pl.BlockSpec((1, 2 * beams, 2 * dishes), lambda i: (i, 0, 0)),
        name="weights",
        compiler_params=GRANT,
        cost_estimate=pl.CostEstimate(
            flops=8 * 4 * 2 * 192 * 192 * 384, bytes_accessed=5 << 20, transcendentals=0
        ),
    )(beam_weights[0], dish_order.reshape(1, dishes), slots_of(devices))

    filtered = pl.pallas_call(
        channel_kernel,
        out_shape=jax.ShapeDtypeStruct((devices, 6 * band_chans, channels), F32),
        in_specs=[VMEM] * 4,
        out_specs=VMEM,
        scratch_shapes=[
            pltpu.VMEM((frames, 24, 2 * LANES), F32),
            pltpu.VMEM((frames + fir_count - 1, 24, 2 * LANES), F32),
            pltpu.VMEM((frames * 24, LANES), F32),
        ],
        name="channels",
        compiler_params=GRANT,
    )(arrived.reshape(frames, 24, channels), prototype, dft_parts(channels), taps)
    field = lax.all_to_all(filtered, "band", split_axis=0, concat_axis=0, tiled=True)
    field = field.reshape(devices * 6 * band_chans, channels)

    power = pl.pallas_call(
        beams_kernel,
        out_shape=jax.ShapeDtypeStruct((band_chans, frames // INTEG, beams), F32),
        in_specs=[VMEM, HBM],
        out_specs=VMEM,
        scratch_shapes=[
            pltpu.VMEM(weights.shape, BF16),
            pltpu.SemaphoreType.DMA((band_chans // 2,)),
        ],
        name="beams",
        compiler_params=GRANT,
    )(field, weights)
    return jnp.transpose(power, (0, 2, 1))[None]


def detect(weights, field_real, field_imag):
    def contract(weight_part, field_part):
        return jnp.einsum("qds,dqf->qsf", weight_part, field_part, precision=HIGHEST)

    beam_real = contract(weights[:, 0], field_real) - contract(weights[:, 1], field_imag)
    beam_imag = contract(weights[:, 0], field_imag) + contract(weights[:, 1], field_real)
    energy = beam_real * beam_real + beam_imag * beam_imag
    shaped = energy.reshape(energy.shape[:-1] + (energy.shape[-1] // INTEG, INTEG))
    return jnp.mean(shaped, axis=-1)


def wide_body(samples, prototype, dish_filter, beam_weights, dish_order):
    devices = lax.axis_size("band")
    position = lax.axis_index("band")
    pfb_count, channels = prototype.shape
    fir_count = dish_filter.shape[1]
    dishes = dish_filter.shape[2]
    band_chans = beam_weights.shape[1]
    bands = channels // band_chans
    owners = devices // bands
    frames_dev = samples.shape[2] // channels
    frames = frames_dev * devices
    share = -(-dishes // devices)
    extra = share * devices - dishes

    padded = jnp.pad(samples, ((0, 0), (0, extra), (0, 0)))
    pieces = padded.reshape(2, devices, share, frames_dev, channels)
    pieces = jnp.transpose(pieces, (1, 3, 0, 2, 4)).reshape(
        devices, frames_dev, 2 * share, channels
    )
    arrived = lax.all_to_all(pieces, "band", split_axis=0, concat_axis=0, tiled=True)
    blocks = arrived.reshape(frames, 2 * share, channels)

    history = jnp.pad(blocks, ((pfb_count - 1, 0), (0, 0), (0, 0)))
    polyphase = jnp.zeros_like(blocks)
    for tap_index in range(pfb_count):
        offset = pfb_count - 1 - tap_index
        polyphase = polyphase + prototype[tap_index] * history[offset : offset + frames]
    cosine, sine = fourier_tables(channels)
    both = jnp.dot(polyphase, jnp.concatenate([cosine, sine], axis=1), precision=HIGHEST)
    with_cos = both[..., :channels].reshape(frames, 2, share, channels)
    with_sin = both[..., channels:].reshape(frames, 2, share, channels)
    spec_real = with_cos[:, 0] + with_sin[:, 1]
    spec_imag = with_cos[:, 1] - with_sin[:, 0]

    taps = jnp.pad(dish_filter, ((0, 0), (0, 0), (0, extra), (0, 0)))
    taps = lax.dynamic_slice_in_dim(taps, position * share, share, 2)
    lead = ((fir_count - 1, 0), (0, 0), (0, 0))
    past_real, past_imag = jnp.pad(spec_real, lead), jnp.pad(spec_imag, lead)
    out_real = jnp.zeros_like(spec_real)
    out_imag = jnp.zeros_like(spec_imag)
    for tap_index in range(fir_count):
        offset = fir_count - 1 - tap_index
        part_real = past_real[offset : offset + frames]
        part_imag = past_imag[offset : offset + frames]
        factor_real, factor_imag = taps[0, tap_index], taps[1, tap_index]
        out_real = out_real + factor_real * part_real - factor_imag * part_imag
        out_imag = out_imag + factor_real * part_imag + factor_imag * part_real

    filtered = jnp.stack([out_real, out_imag])
    filtered = filtered.reshape(2, frames, share, bands, band_chans)
    filtered = jnp.transpose(filtered, (3, 0, 2, 4, 1)).reshape(
        bands, 2 * share, band_chans * frames
    )
    filtered = jnp.repeat(filtered, owners, axis=0)
    field = lax.all_to_all(filtered, "band", split_axis=0, concat_axis=0, tiled=True)
    field = field.reshape(devices, 2, share, band_chans, frames)
    field = jnp.transpose(field, (1, 0, 2, 3, 4))
    field = field.reshape(2, devices * share, band_chans, frames)
    field = jnp.take(field, dish_order, axis=1)
    power = detect(beam_weights[0], field[0], field[1])
    return power[None]


def solution(mesh):
    devices = mesh.shape["band"]

    def body(samples, prototype, dish_filter, beam_weights, dish_order):
        channels = prototype.shape[1]
        close = (
            channels == LANES
            and beam_weights.shape[1] == 8
            and devices * 8 == channels
            and dish_filter.shape[2] == 12 * devices
            and samples.shape[2] * devices == 32 * channels
        )
        chosen = close_body if close else wide_body
        return chosen(samples, prototype, dish_filter, beam_weights, dish_order)

    placed = (P(None, None, ("grp", "band")), P(), P(), P("band", None, None, None, None), P())
    return jax.shard_map(
        body,
        mesh=mesh,
        in_specs=placed,
        out_specs=P(("grp", "band"), None, None, None),
        check_vma=False,
    )
```

```python
import math

import jax
import jax.numpy as jnp
import numpy as np
from jax import lax
from jax.experimental import pallas as pl
from jax.experimental.pallas import tpu as pltpu
from jax.sharding import PartitionSpec as P

INTEG = 4
HIGHEST = lax.Precision.HIGHEST
F32 = jnp.float32
BF16 = jnp.bfloat16
LANES = 128
VMEM = pl.BlockSpec(memory_space=pltpu.VMEM)
HBM = pl.BlockSpec(memory_space=pltpu.HBM)
GRANT = pltpu.CompilerParams(vmem_limit_bytes=16 << 20)
LARGE_GRANT = pltpu.CompilerParams(vmem_limit_bytes=62_800_000)


def fourier_tables(length):
    counter = jnp.arange(length, dtype=jnp.int32)
    product = counter[:, None] * counter[None, :] % length
    angles = product.astype(jnp.float32) * (2.0 * math.pi / length)
    factor = 1.0 / math.sqrt(length)
    return (jnp.cos(angles) * factor, jnp.sin(angles) * factor)


def split(value):
    high = value.astype(BF16)
    return high, (value - high.astype(F32)).astype(BF16)


def share_row(part, dish):
    return part * 8 + dish if dish < 8 else 16 + part * 4 + dish - 8


def pieces_kernel(x_ref, out_ref, rest, four, tile_sems, rest_sem, four_sem):
    devices, frames_dev = out_ref.shape[:2]
    low = lax.broadcasted_iota(jnp.int32, (8, LANES), 0) < 4
    load = pltpu.make_async_copy(x_ref.at[:, devices * 8 :, :], rest, rest_sem)
    load.start()
    tiles = x_ref.reshape(2, x_ref.shape[1] // 8, 8, x_ref.shape[2])
    moves = []
    for frame in range(frames_dev):
        lanes = slice(frame * LANES, (frame + 1) * LANES)
        for part in range(2):
            moves.append(
                pltpu.make_async_copy(
                    tiles.at[part, 0:devices, :, lanes],
                    out_ref.at[:, frame, part * 8 : part * 8 + 8, :],
                    tile_sems.at[frame, part],
                )
            )
    for move in moves:
        move.start()
    load.wait()
    for frame in range(frames_dev):
        lanes = slice(frame * LANES, (frame + 1) * LANES)
        for dev in range(0, devices, 2):
            real = rest[0, dev * 4 : dev * 4 + 8, lanes]
            imag = rest[1, dev * 4 : dev * 4 + 8, lanes]
            four[dev, frame] = jnp.where(low, real, pltpu.roll(imag, 4, 0))
            four[dev + 1, frame] = jnp.where(low, pltpu.roll(real, 4, 0), imag)
    store = pltpu.make_async_copy(four, out_ref.at[:, :, 16:24, :], four_sem)
    store.start()
    for move in moves:
        move.wait()
    store.wait()


def weights_kernel(w_ref, order_ref, slot_ref, out_ref):
    order = order_ref[...]
    beams = w_ref.shape[3]
    for half in range(2):
        hot = (slot_ref[:, half : half + 1] == order).astype(F32).T.astype(BF16)
        for part in range(2):
            turned = w_ref[0, part].T
            value = split(turned)[half]
            product = jnp.dot(value, hot, preferred_element_type=F32)
            rows = slice(part * beams, (part + 1) * beams)
            if half == 0:
                out_ref[0, rows, :] = product.astype(BF16)
            else:
                out_ref[0, rows, :] += product.astype(BF16)


def channel_kernel(x_ref, proto_ref, table_ref, taps_ref, out_ref, poly, spec, filt):
    frames = x_ref.shape[0]
    pfb_count = proto_ref.shape[0]
    fir_count = taps_ref.shape[0]
    group = 8
    low = lax.broadcasted_iota(jnp.int32, (group, 8, LANES), 1) < 4

    spec[0 : fir_count - 1] = jnp.zeros((fir_count - 1, 24, 2 * LANES), F32)
    for first in range(0, frames, group):
        found = []
        for rows in range(0, 24, 8):
            total = None
            for tap in range(pfb_count):
                begin = first - tap
                lost = max(0, -begin)
                if lost >= group:
                    continue
                block = x_ref[begin + lost : begin + group, rows : rows + 8, :]
                term = block * proto_ref[tap : tap + 1, :][None]
                if lost:
                    term = jnp.concatenate([jnp.zeros((lost, 8, LANES), F32), term], axis=0)
                total = term if total is None else total + term
            found.append(total)
        turned = pltpu.roll(found[2], 4, 1)
        other = [found[1], -found[0], jnp.where(low, turned, -turned)]
        for index in range(3):
            rows = slice(index * 8, index * 8 + 8)
            poly[first : first + group, rows, 0:LANES] = found[index]
            poly[first : first + group, rows, LANES : 2 * LANES] = other[index]

    for first in range(0, frames, group):
        value = poly[first : first + group].reshape(group * 24, 2 * LANES)
        high, rest = split(value)
        stacked = jnp.concatenate([high, rest, high], axis=1)
        product = jnp.dot(stacked, table_ref[...], preferred_element_type=F32)
        begin = first + fir_count - 1
        spec[begin : begin + group] = product.reshape(group, 24, 2 * LANES)

    for rows in range(0, 24, 8):
        for first in range(0, frames, group):
            total = None
            for tap in range(fir_count):
                begin = first + fir_count - 1 - tap
                near = spec[begin : begin + group, rows : rows + 8, 0:LANES]
                cross = spec[begin : begin + group, rows : rows + 8, LANES : 2 * LANES]
                term = taps_ref[tap, 0, rows : rows + 8, :][None] * near
                term = term + taps_ref[tap, 1, rows : rows + 8, :][None] * cross
                total = term if total is None else total + term
            for frame in range(group):
                begin = (first + frame) * 24 + rows
                filt[begin : begin + 8, :] = total[frame]

    per_band = out_ref.shape[1] // 6
    for pair in range(6):
        rows = [
            filt[pl.ds(share_row(part, pair * 2 + odd), frames, stride=24), :]
            for part in range(2)
            for odd in range(2)
        ]
        turned = jnp.concatenate(rows, axis=0).T
        for dev in range(out_ref.shape[0]):
            out_ref[dev, pair * per_band : (pair + 1) * per_band, :] = turned[
                dev * per_band : (dev + 1) * per_band
            ]


def beams_kernel(x_ref, w_hbm, out_ref, w_ref, sems):
    loads = [
        pltpu.make_async_copy(
            w_hbm.at[2 * step : 2 * step + 2], w_ref.at[2 * step : 2 * step + 2], sems.at[step]
        )
        for step in range(w_hbm.shape[0] // 2)
    ]
    for load in loads:
        load.start()
    rows = x_ref.shape[0] // 8
    beams = w_ref.shape[1] // 2
    lane = lax.broadcasted_iota(jnp.int32, (rows, LANES), 1)
    even = lane % 64 < 32
    wide = lax.broadcasted_iota(jnp.int32, (beams, LANES), 1)
    even_wide = wide % 64 < 32
    row = lax.broadcasted_iota(jnp.int32, (16, 2 * LANES), 0)
    column = lax.broadcasted_iota(jnp.int32, (16, 2 * LANES), 1)
    pool = jnp.where(row == column % 64 // INTEG, 1.0 / INTEG, 0.0).astype(BF16)
    for step in range(w_ref.shape[0] // 2):
        one = x_ref[pl.ds(2 * step, rows, stride=8), :]
        two = x_ref[pl.ds(2 * step + 1, rows, stride=8), :]
        first = jnp.where(even, one, pltpu.roll(two, 32, 1))
        second = jnp.where(even, pltpu.roll(one, LANES - 32, 1), two)
        field = jnp.concatenate([first, second], axis=0)
        high, rest = split(field)
        both = jnp.concatenate([high, rest], axis=1)
        both = jnp.concatenate([both, both], axis=0)
        loads[step].wait()
        sums = []
        for index in range(2):
            product = jnp.dot(w_ref[2 * step + index], both, preferred_element_type=F32)
            sums.append(product[:, 0:LANES] + product[:, LANES : 2 * LANES])
        by_real = jnp.where(even_wide, sums[0][:beams], sums[1][:beams])
        by_imag = jnp.where(even_wide, sums[0][beams:], sums[1][beams:])
        crossed = pltpu.roll(by_imag, 64, 1)
        beam = by_real + jnp.where(wide < 64, -crossed, crossed)
        high, rest = split(beam * beam)
        power = lax.dot_general(
            pool,
            jnp.concatenate([high, rest], axis=1),
            (((1,), (1,)), ((), ())),
            preferred_element_type=F32,
        )
        out_ref[2 * step] = power[0:8]
        out_ref[2 * step + 1] = power[8:16]


def slots_of(devices):
    dishes = np.zeros((2, devices, 6), np.int32)
    for odd in range(2):
        for dev in range(devices):
            for pair in range(6):
                own = pair * 2 + odd
                dishes[odd, dev, pair] = (
                    dev * 8 + own if own < 8 else devices * 8 + dev * 4 + own - 8
                )
    flat = dishes.reshape(-1)
    none = np.full_like(flat, -1)
    return np.stack([np.concatenate([flat, none]), np.concatenate([none, flat])], axis=1)


def dft_parts(channels):
    index = np.arange(channels)
    angle = 2.0 * np.pi * (index[:, None] * index[None, :] % channels) / channels
    cosine = np.cos(angle) / np.sqrt(channels)
    sine = np.sin(angle) / np.sqrt(channels)
    table = np.block([[cosine, sine], [sine, -cosine]]).astype(np.float32)
    high = table.astype(jnp.bfloat16)
    rest = (table - high.astype(np.float32)).astype(jnp.bfloat16)
    return np.concatenate([high, high, rest], axis=0)


def close_body(samples, prototype, dish_filter, beam_weights, dish_order):
    devices = lax.axis_size("band")
    position = lax.axis_index("band")
    channels = prototype.shape[1]
    fir_count = dish_filter.shape[1]
    dishes = dish_filter.shape[2]
    band_chans = beam_weights.shape[1]
    beams = beam_weights.shape[4]
    frames_dev = samples.shape[2] // channels
    frames = frames_dev * devices

    pieces = pl.pallas_call(
        pieces_kernel,
        out_shape=jax.ShapeDtypeStruct((devices, frames_dev, 24, channels), F32),
        in_specs=[HBM],
        out_specs=HBM,
        scratch_shapes=[
            pltpu.VMEM((2, dishes - devices * 8, frames_dev * channels), F32),
            pltpu.VMEM((devices, frames_dev, 8, channels), F32),
            pltpu.SemaphoreType.DMA((frames_dev, 2)),
            pltpu.SemaphoreType.DMA(()),
            pltpu.SemaphoreType.DMA(()),
        ],
        name="pieces",
    )(samples)
    arrived = lax.all_to_all(pieces, "band", split_axis=0, concat_axis=0, tiled=True)

    eight = lax.dynamic_slice_in_dim(dish_filter, position * 8, 8, 2)
    four = lax.dynamic_slice_in_dim(dish_filter, devices * 8 + position * 4, 4, 2)
    taps = jnp.concatenate([eight, eight, four, four], axis=2)
    taps = jnp.transpose(taps, (1, 0, 2, 3))
    weights = pl.pallas_call(
        weights_kernel,
        grid=(band_chans,),
        out_shape=jax.ShapeDtypeStruct((band_chans, 2 * beams, 2 * dishes), BF16),
        in_specs=[
            pl.BlockSpec((1, 2, dishes, beams), lambda i: (i, 0, 0, 0)),
            pl.BlockSpec((1, dishes), lambda i: (0, 0)),
            pl.BlockSpec((2 * dishes, 2), lambda i: (0, 0)),
        ],
        out_specs=pl.BlockSpec((1, 2 * beams, 2 * dishes), lambda i: (i, 0, 0)),
        name="weights",
        compiler_params=GRANT,
        cost_estimate=pl.CostEstimate(
            flops=8 * 4 * 2 * 192 * 192 * 384, bytes_accessed=5 << 20, transcendentals=0
        ),
    )(beam_weights[0], dish_order.reshape(1, dishes), slots_of(devices))

    filtered = pl.pallas_call(
        channel_kernel,
        out_shape=jax.ShapeDtypeStruct((devices, 6 * band_chans, channels), F32),
        in_specs=[VMEM] * 4,
        out_specs=VMEM,
        scratch_shapes=[
            pltpu.VMEM((frames, 24, 2 * LANES), F32),
            pltpu.VMEM((frames + fir_count - 1, 24, 2 * LANES), F32),
            pltpu.VMEM((frames * 24, LANES), F32),
        ],
        name="channels",
        compiler_params=GRANT,
    )(arrived.reshape(frames, 24, channels), prototype, dft_parts(channels), taps)
    field = lax.all_to_all(filtered, "band", split_axis=0, concat_axis=0, tiled=True)
    field = field.reshape(devices * 6 * band_chans, channels)

    power = pl.pallas_call(
        beams_kernel,
        out_shape=jax.ShapeDtypeStruct((band_chans, frames // INTEG, beams), F32),
        in_specs=[VMEM, HBM],
        out_specs=VMEM,
        scratch_shapes=[
            pltpu.VMEM(weights.shape, BF16),
            pltpu.SemaphoreType.DMA((band_chans // 2,)),
        ],
        name="beams",
        compiler_params=LARGE_GRANT,
    )(field, weights)
    return jnp.transpose(power, (0, 2, 1))[None]


def detect(weights, field_real, field_imag):
    def contract(weight_part, field_part):
        return jnp.einsum("qds,dqf->qsf", weight_part, field_part, precision=HIGHEST)

    beam_real = contract(weights[:, 0], field_real) - contract(weights[:, 1], field_imag)
    beam_imag = contract(weights[:, 0], field_imag) + contract(weights[:, 1], field_real)
    energy = beam_real * beam_real + beam_imag * beam_imag
    shaped = energy.reshape(energy.shape[:-1] + (energy.shape[-1] // INTEG, INTEG))
    return jnp.mean(shaped, axis=-1)


def wide_body(samples, prototype, dish_filter, beam_weights, dish_order):
    devices = lax.axis_size("band")
    position = lax.axis_index("band")
    pfb_count, channels = prototype.shape
    fir_count = dish_filter.shape[1]
    dishes = dish_filter.shape[2]
    band_chans = beam_weights.shape[1]
    bands = channels // band_chans
    owners = devices // bands
    frames_dev = samples.shape[2] // channels
    frames = frames_dev * devices
    share = -(-dishes // devices)
    extra = share * devices - dishes

    padded = jnp.pad(samples, ((0, 0), (0, extra), (0, 0)))
    pieces = padded.reshape(2, devices, share, frames_dev, channels)
    pieces = jnp.transpose(pieces, (1, 3, 0, 2, 4)).reshape(
        devices, frames_dev, 2 * share, channels
    )
    arrived = lax.all_to_all(pieces, "band", split_axis=0, concat_axis=0, tiled=True)
    blocks = arrived.reshape(frames, 2 * share, channels)

    history = jnp.pad(blocks, ((pfb_count - 1, 0), (0, 0), (0, 0)))
    polyphase = jnp.zeros_like(blocks)
    for tap_index in range(pfb_count):
        offset = pfb_count - 1 - tap_index
        polyphase = polyphase + prototype[tap_index] * history[offset : offset + frames]
    cosine, sine = fourier_tables(channels)
    both = jnp.dot(polyphase, jnp.concatenate([cosine, sine], axis=1), precision=HIGHEST)
    with_cos = both[..., :channels].reshape(frames, 2, share, channels)
    with_sin = both[..., channels:].reshape(frames, 2, share, channels)
    spec_real = with_cos[:, 0] + with_sin[:, 1]
    spec_imag = with_cos[:, 1] - with_sin[:, 0]

    taps = jnp.pad(dish_filter, ((0, 0), (0, 0), (0, extra), (0, 0)))
    taps = lax.dynamic_slice_in_dim(taps, position * share, share, 2)
    lead = ((fir_count - 1, 0), (0, 0), (0, 0))
    past_real, past_imag = jnp.pad(spec_real, lead), jnp.pad(spec_imag, lead)
    out_real = jnp.zeros_like(spec_real)
    out_imag = jnp.zeros_like(spec_imag)
    for tap_index in range(fir_count):
        offset = fir_count - 1 - tap_index
        part_real = past_real[offset : offset + frames]
        part_imag = past_imag[offset : offset + frames]
        factor_real, factor_imag = taps[0, tap_index], taps[1, tap_index]
        out_real = out_real + factor_real * part_real - factor_imag * part_imag
        out_imag = out_imag + factor_real * part_imag + factor_imag * part_real

    filtered = jnp.stack([out_real, out_imag])
    filtered = filtered.reshape(2, frames, share, bands, band_chans)
    filtered = jnp.transpose(filtered, (3, 0, 2, 4, 1)).reshape(
        bands, 2 * share, band_chans * frames
    )
    filtered = jnp.repeat(filtered, owners, axis=0)
    field = lax.all_to_all(filtered, "band", split_axis=0, concat_axis=0, tiled=True)
    field = field.reshape(devices, 2, share, band_chans, frames)
    field = jnp.transpose(field, (1, 0, 2, 3, 4))
    field = field.reshape(2, devices * share, band_chans, frames)
    field = jnp.take(field, dish_order, axis=1)
    power = detect(beam_weights[0], field[0], field[1])
    return power[None]


def solution(mesh):
    devices = mesh.shape["band"]

    def body(samples, prototype, dish_filter, beam_weights, dish_order):
        channels = prototype.shape[1]
        close = (
            channels == LANES
            and beam_weights.shape[1] == 8
            and devices * 8 == channels
            and dish_filter.shape[2] == 12 * devices
            and samples.shape[2] * devices == 32 * channels
        )
        chosen = close_body if close else wide_body
        return chosen(samples, prototype, dish_filter, beam_weights, dish_order)

    placed = (P(None, None, ("grp", "band")), P(), P(), P("band", None, None, None, None), P())
    return jax.shard_map(
        body,
        mesh=mesh,
        in_specs=placed,
        out_specs=P(("grp", "band"), None, None, None),
        check_vma=False,
    )
```

```python
import math

import jax
import jax.numpy as jnp
import numpy as np
from jax import lax
from jax.experimental import pallas as pl
from jax.experimental.pallas import tpu as pltpu
from jax.sharding import PartitionSpec as P

INTEG = 4
HIGHEST = lax.Precision.HIGHEST
F32 = jnp.float32
BF16 = jnp.bfloat16
LANES = 128
VMEM = pl.BlockSpec(memory_space=pltpu.VMEM)
HBM = pl.BlockSpec(memory_space=pltpu.HBM)
GRANT = pltpu.CompilerParams(vmem_limit_bytes=16 << 20)


def fourier_tables(length):
    counter = jnp.arange(length, dtype=jnp.int32)
    product = counter[:, None] * counter[None, :] % length
    angles = product.astype(jnp.float32) * (2.0 * math.pi / length)
    factor = 1.0 / math.sqrt(length)
    return (jnp.cos(angles) * factor, jnp.sin(angles) * factor)


held = pltpu.with_memory_space_constraint


def split(value):
    high = value.astype(BF16)
    return high, (value - high.astype(F32)).astype(BF16)


def share_row(part, dish):
    return part * 8 + dish if dish < 8 else 16 + part * 4 + dish - 8


def pieces_kernel(x_ref, out_ref, main, rest, four, in_sems, out_sems, four_sem):
    devices, frames_dev = out_ref.shape[:2]
    low = lax.broadcasted_iota(jnp.int32, (8, LANES), 0) < 4
    rests = [
        pltpu.make_async_copy(x_ref.at[part, devices * 8 :], rest.at[part], in_sems.at[1, part])
        for part in range(2)
    ]
    mains = [
        pltpu.make_async_copy(x_ref.at[part, 0 : devices * 8], main.at[part], in_sems.at[0, part])
        for part in range(2)
    ]
    for load in rests + mains:
        load.start()
    for load in rests:
        load.wait()
    for frame in range(frames_dev):
        lanes = slice(frame * LANES, (frame + 1) * LANES)
        for dev in range(0, devices, 2):
            real = rest[0, dev * 4 : dev * 4 + 8, lanes]
            imag = rest[1, dev * 4 : dev * 4 + 8, lanes]
            four[dev, frame] = jnp.where(low, real, pltpu.roll(imag, 4, 0))
            four[dev + 1, frame] = jnp.where(low, pltpu.roll(real, 4, 0), imag)
    moves = [pltpu.make_async_copy(four, out_ref.at[:, :, 16:24, :], four_sem)]
    moves[0].start()
    tiles = main.reshape(2, devices, 8, main.shape[2])
    for part in range(2):
        mains[part].wait()
        for frame in range(frames_dev):
            lanes = slice(frame * LANES, (frame + 1) * LANES)
            moves.append(
                pltpu.make_async_copy(
                    tiles.at[part, :, :, lanes],
                    out_ref.at[:, frame, part * 8 : part * 8 + 8, :],
                    out_sems.at[frame, part],
                )
            )
            moves[-1].start()
    for move in moves:
        move.wait()


def weights_kernel(w_ref, order_ref, slot_ref, out_ref):
    order = order_ref[...]
    beams = w_ref.shape[3]
    for half in range(2):
        hot = (slot_ref[:, half : half + 1] == order).astype(F32).T.astype(BF16)
        for part in range(2):
            turned = w_ref[0, part].T
            value = split(turned)[half]
            product = jnp.dot(value, hot, preferred_element_type=F32)
            rows = slice(part * beams, (part + 1) * beams)
            if half == 0:
                out_ref[0, rows, :] = product.astype(BF16)
            else:
                out_ref[0, rows, :] += product.astype(BF16)


def channel_kernel(x_ref, proto_ref, table_ref, taps_ref, out_ref, poly, spec, filt):
    frames = x_ref.shape[0]
    pfb_count = proto_ref.shape[0]
    fir_count = taps_ref.shape[0]
    group = 8
    low = lax.broadcasted_iota(jnp.int32, (group, 8, LANES), 1) < 4

    spec[0 : fir_count - 1] = jnp.zeros((fir_count - 1, 24, 2 * LANES), F32)
    for first in range(0, frames, group):
        found = []
        for rows in range(0, 24, 8):
            total = None
            for tap in range(pfb_count):
                begin = first - tap
                lost = max(0, -begin)
                if lost >= group:
                    continue
                block = x_ref[begin + lost : begin + group, rows : rows + 8, :]
                term = block * proto_ref[tap : tap + 1, :][None]
                if lost:
                    term = jnp.concatenate([jnp.zeros((lost, 8, LANES), F32), term], axis=0)
                total = term if total is None else total + term
            found.append(total)
        turned = pltpu.roll(found[2], 4, 1)
        other = [found[1], -found[0], jnp.where(low, turned, -turned)]
        for index in range(3):
            rows = slice(index * 8, index * 8 + 8)
            poly[first : first + group, rows, 0:LANES] = found[index]
            poly[first : first + group, rows, LANES : 2 * LANES] = other[index]

    for first in range(0, frames, group):
        value = poly[first : first + group].reshape(group * 24, 2 * LANES)
        high, rest = split(value)
        stacked = jnp.concatenate([high, rest, high], axis=1)
        product = jnp.dot(stacked, table_ref[...], preferred_element_type=F32)
        begin = first + fir_count - 1
        spec[begin : begin + group] = product.reshape(group, 24, 2 * LANES)

    for rows in range(0, 24, 8):
        for first in range(0, frames, group):
            total = None
            for tap in range(fir_count):
                begin = first + fir_count - 1 - tap
                near = spec[begin : begin + group, rows : rows + 8, 0:LANES]
                cross = spec[begin : begin + group, rows : rows + 8, LANES : 2 * LANES]
                term = taps_ref[tap, 0, rows : rows + 8, :][None] * near
                term = term + taps_ref[tap, 1, rows : rows + 8, :][None] * cross
                total = term if total is None else total + term
            for frame in range(group):
                begin = (first + frame) * 24 + rows
                filt[begin : begin + 8, :] = total[frame]

    per_band = out_ref.shape[1] // 6
    for pair in range(6):
        rows = [
            filt[pl.ds(share_row(part, pair * 2 + odd), frames, stride=24), :]
            for part in range(2)
            for odd in range(2)
        ]
        turned = jnp.concatenate(rows, axis=0).T
        for dev in range(out_ref.shape[0]):
            out_ref[dev, pair * per_band : (pair + 1) * per_band, :] = turned[
                dev * per_band : (dev + 1) * per_band
            ]


def beams_kernel(x_ref, w_hbm, out_ref, w_ref, sems):
    loads = [
        pltpu.make_async_copy(
            w_hbm.at[2 * step : 2 * step + 2], w_ref.at[2 * step : 2 * step + 2], sems.at[step]
        )
        for step in range(w_hbm.shape[0] // 2)
    ]
    for load in loads:
        load.start()
    rows = x_ref.shape[0] // 8
    beams = w_ref.shape[1] // 2
    lane = lax.broadcasted_iota(jnp.int32, (rows, LANES), 1)
    even = lane % 64 < 32
    wide = lax.broadcasted_iota(jnp.int32, (beams, LANES), 1)
    even_wide = wide % 64 < 32
    row = lax.broadcasted_iota(jnp.int32, (16, 2 * LANES), 0)
    column = lax.broadcasted_iota(jnp.int32, (16, 2 * LANES), 1)
    pool = jnp.where(row == column % 64 // INTEG, 1.0 / INTEG, 0.0).astype(BF16)
    for step in range(w_ref.shape[0] // 2):
        one = x_ref[pl.ds(2 * step, rows, stride=8), :]
        two = x_ref[pl.ds(2 * step + 1, rows, stride=8), :]
        first = jnp.where(even, one, pltpu.roll(two, 32, 1))
        second = jnp.where(even, pltpu.roll(one, LANES - 32, 1), two)
        field = jnp.concatenate([first, second], axis=0)
        high, rest = split(field)
        both = jnp.concatenate([high, rest], axis=1)
        both = jnp.concatenate([both, both], axis=0)
        loads[step].wait()
        sums = []
        for index in range(2):
            product = jnp.dot(w_ref[2 * step + index], both, preferred_element_type=F32)
            sums.append(product[:, 0:LANES] + product[:, LANES : 2 * LANES])
        by_real = jnp.where(even_wide, sums[0][:beams], sums[1][:beams])
        by_imag = jnp.where(even_wide, sums[0][beams:], sums[1][beams:])
        crossed = pltpu.roll(by_imag, 64, 1)
        beam = by_real + jnp.where(wide < 64, -crossed, crossed)
        high, rest = split(beam * beam)
        power = lax.dot_general(
            pool,
            jnp.concatenate([high, rest], axis=1),
            (((1,), (1,)), ((), ())),
            preferred_element_type=F32,
        )
        out_ref[2 * step] = power[0:8]
        out_ref[2 * step + 1] = power[8:16]


def slots_of(devices):
    dishes = np.zeros((2, devices, 6), np.int32)
    for odd in range(2):
        for dev in range(devices):
            for pair in range(6):
                own = pair * 2 + odd
                dishes[odd, dev, pair] = (
                    dev * 8 + own if own < 8 else devices * 8 + dev * 4 + own - 8
                )
    flat = dishes.reshape(-1)
    none = np.full_like(flat, -1)
    return np.stack([np.concatenate([flat, none]), np.concatenate([none, flat])], axis=1)


def dft_parts(channels):
    index = np.arange(channels)
    angle = 2.0 * np.pi * (index[:, None] * index[None, :] % channels) / channels
    cosine = np.cos(angle) / np.sqrt(channels)
    sine = np.sin(angle) / np.sqrt(channels)
    table = np.block([[cosine, sine], [sine, -cosine]]).astype(np.float32)
    high = table.astype(jnp.bfloat16)
    rest = (table - high.astype(np.float32)).astype(jnp.bfloat16)
    return np.concatenate([high, high, rest], axis=0)


def close_body(samples, prototype, dish_filter, beam_weights, dish_order):
    devices = lax.axis_size("band")
    position = lax.axis_index("band")
    channels = prototype.shape[1]
    fir_count = dish_filter.shape[1]
    dishes = dish_filter.shape[2]
    band_chans = beam_weights.shape[1]
    beams = beam_weights.shape[4]
    frames_dev = samples.shape[2] // channels
    frames = frames_dev * devices

    pieces = pl.pallas_call(
        pieces_kernel,
        out_shape=jax.ShapeDtypeStruct((devices, frames_dev, 24, channels), F32),
        in_specs=[HBM],
        out_specs=HBM,
        scratch_shapes=[
            pltpu.VMEM((2, devices * 8, frames_dev * channels), F32),
            pltpu.VMEM((2, dishes - devices * 8, frames_dev * channels), F32),
            pltpu.VMEM((devices, frames_dev, 8, channels), F32),
            pltpu.SemaphoreType.DMA((2, 2)),
            pltpu.SemaphoreType.DMA((frames_dev, 2)),
            pltpu.SemaphoreType.DMA(()),
        ],
        name="pieces",
        compiler_params=GRANT,
    )(held(samples, pltpu.HBM))
    arrived = lax.all_to_all(pieces, "band", split_axis=0, concat_axis=0, tiled=True)

    eight = lax.dynamic_slice_in_dim(dish_filter, position * 8, 8, 2)
    four = lax.dynamic_slice_in_dim(dish_filter, devices * 8 + position * 4, 4, 2)
    taps = jnp.concatenate([eight, eight, four, four], axis=2)
    taps = jnp.transpose(taps, (1, 0, 2, 3))
    weights = pl.pallas_call(
        weights_kernel,
        grid=(band_chans,),
        out_shape=jax.ShapeDtypeStruct((band_chans, 2 * beams, 2 * dishes), BF16),
        in_specs=[
            pl.BlockSpec((1, 2, dishes, beams), lambda i: (i, 0, 0, 0)),
            pl.BlockSpec((1, dishes), lambda i: (0, 0)),
            pl.BlockSpec((2 * dishes, 2), lambda i: (0, 0)),
        ],
        out_specs=pl.BlockSpec((1, 2 * beams, 2 * dishes), lambda i: (i, 0, 0)),
        name="weights",
        compiler_params=GRANT,
        cost_estimate=pl.CostEstimate(
            flops=8 * 4 * 2 * 192 * 192 * 384, bytes_accessed=5 << 20, transcendentals=0
        ),
    )(beam_weights[0], dish_order.reshape(1, dishes), slots_of(devices))

    filtered = pl.pallas_call(
        channel_kernel,
        out_shape=jax.ShapeDtypeStruct((devices, 6 * band_chans, channels), F32),
        in_specs=[VMEM] * 4,
        out_specs=VMEM,
        scratch_shapes=[
            pltpu.VMEM((frames, 24, 2 * LANES), F32),
            pltpu.VMEM((frames + fir_count - 1, 24, 2 * LANES), F32),
            pltpu.VMEM((frames * 24, LANES), F32),
        ],
        name="channels",
        compiler_params=GRANT,
    )(held(arrived.reshape(frames, 24, channels), pltpu.VMEM), prototype, dft_parts(channels), taps)
    field = lax.all_to_all(filtered, "band", split_axis=0, concat_axis=0, tiled=True)
    field = field.reshape(devices * 6 * band_chans, channels)

    power = pl.pallas_call(
        beams_kernel,
        out_shape=jax.ShapeDtypeStruct((band_chans, frames // INTEG, beams), F32),
        in_specs=[VMEM, HBM],
        out_specs=VMEM,
        scratch_shapes=[
            pltpu.VMEM(weights.shape, BF16),
            pltpu.SemaphoreType.DMA((band_chans // 2,)),
        ],
        name="beams",
        compiler_params=GRANT,
    )(held(field, pltpu.VMEM), held(weights, pltpu.HBM))
    return jnp.transpose(power, (0, 2, 1))[None]


def detect(weights, field_real, field_imag):
    def contract(weight_part, field_part):
        return jnp.einsum("qds,dqf->qsf", weight_part, field_part, precision=HIGHEST)

    beam_real = contract(weights[:, 0], field_real) - contract(weights[:, 1], field_imag)
    beam_imag = contract(weights[:, 0], field_imag) + contract(weights[:, 1], field_real)
    energy = beam_real * beam_real + beam_imag * beam_imag
    shaped = energy.reshape(energy.shape[:-1] + (energy.shape[-1] // INTEG, INTEG))
    return jnp.mean(shaped, axis=-1)


def wide_body(samples, prototype, dish_filter, beam_weights, dish_order):
    devices = lax.axis_size("band")
    position = lax.axis_index("band")
    pfb_count, channels = prototype.shape
    fir_count = dish_filter.shape[1]
    dishes = dish_filter.shape[2]
    band_chans = beam_weights.shape[1]
    bands = channels // band_chans
    owners = devices // bands
    frames_dev = samples.shape[2] // channels
    frames = frames_dev * devices
    share = -(-dishes // devices)
    extra = share * devices - dishes

    padded = jnp.pad(samples, ((0, 0), (0, extra), (0, 0)))
    pieces = padded.reshape(2, devices, share, frames_dev, channels)
    pieces = jnp.transpose(pieces, (1, 3, 0, 2, 4)).reshape(
        devices, frames_dev, 2 * share, channels
    )
    arrived = lax.all_to_all(pieces, "band", split_axis=0, concat_axis=0, tiled=True)
    blocks = arrived.reshape(frames, 2 * share, channels)

    history = jnp.pad(blocks, ((pfb_count - 1, 0), (0, 0), (0, 0)))
    polyphase = jnp.zeros_like(blocks)
    for tap_index in range(pfb_count):
        offset = pfb_count - 1 - tap_index
        polyphase = polyphase + prototype[tap_index] * history[offset : offset + frames]
    cosine, sine = fourier_tables(channels)
    both = jnp.dot(polyphase, jnp.concatenate([cosine, sine], axis=1), precision=HIGHEST)
    with_cos = both[..., :channels].reshape(frames, 2, share, channels)
    with_sin = both[..., channels:].reshape(frames, 2, share, channels)
    spec_real = with_cos[:, 0] + with_sin[:, 1]
    spec_imag = with_cos[:, 1] - with_sin[:, 0]

    taps = jnp.pad(dish_filter, ((0, 0), (0, 0), (0, extra), (0, 0)))
    taps = lax.dynamic_slice_in_dim(taps, position * share, share, 2)
    lead = ((fir_count - 1, 0), (0, 0), (0, 0))
    past_real, past_imag = jnp.pad(spec_real, lead), jnp.pad(spec_imag, lead)
    out_real = jnp.zeros_like(spec_real)
    out_imag = jnp.zeros_like(spec_imag)
    for tap_index in range(fir_count):
        offset = fir_count - 1 - tap_index
        part_real = past_real[offset : offset + frames]
        part_imag = past_imag[offset : offset + frames]
        factor_real, factor_imag = taps[0, tap_index], taps[1, tap_index]
        out_real = out_real + factor_real * part_real - factor_imag * part_imag
        out_imag = out_imag + factor_real * part_imag + factor_imag * part_real

    filtered = jnp.stack([out_real, out_imag])
    filtered = filtered.reshape(2, frames, share, bands, band_chans)
    filtered = jnp.transpose(filtered, (3, 0, 2, 4, 1)).reshape(
        bands, 2 * share, band_chans * frames
    )
    filtered = jnp.repeat(filtered, owners, axis=0)
    field = lax.all_to_all(filtered, "band", split_axis=0, concat_axis=0, tiled=True)
    field = field.reshape(devices, 2, share, band_chans, frames)
    field = jnp.transpose(field, (1, 0, 2, 3, 4))
    field = field.reshape(2, devices * share, band_chans, frames)
    field = jnp.take(field, dish_order, axis=1)
    power = detect(beam_weights[0], field[0], field[1])
    return power[None]


def solution(mesh):
    devices = mesh.shape["band"]

    def body(samples, prototype, dish_filter, beam_weights, dish_order):
        channels = prototype.shape[1]
        close = (
            channels == LANES
            and beam_weights.shape[1] == 8
            and devices * 8 == channels
            and dish_filter.shape[2] == 12 * devices
            and samples.shape[2] * devices == 32 * channels
        )
        chosen = close_body if close else wide_body
        return chosen(samples, prototype, dish_filter, beam_weights, dish_order)

    placed = (P(None, None, ("grp", "band")), P(), P(), P("band", None, None, None, None), P())
    return jax.shard_map(
        body,
        mesh=mesh,
        in_specs=placed,
        out_specs=P(("grp", "band"), None, None, None),
        check_vma=False,
    )
```

```python
import math

import jax
import jax.numpy as jnp
import numpy as np
from jax import lax
from jax.experimental import pallas as pl
from jax.experimental.pallas import tpu as pltpu
from jax.sharding import PartitionSpec as P

INTEG = 4
EARLY = 2
SIDE = 4
HIGHEST = lax.Precision.HIGHEST
F32 = jnp.float32
BF16 = jnp.bfloat16
LANES = 128
VMEM = pl.BlockSpec(memory_space=pltpu.VMEM)
HBM = pl.BlockSpec(memory_space=pltpu.HBM)
GRANT = pltpu.CompilerParams(vmem_limit_bytes=16 << 20)


def fourier_tables(length):
    counter = jnp.arange(length, dtype=jnp.int32)
    product = counter[:, None] * counter[None, :] % length
    angles = product.astype(jnp.float32) * (2.0 * math.pi / length)
    factor = 1.0 / math.sqrt(length)
    return (jnp.cos(angles) * factor, jnp.sin(angles) * factor)


held = pltpu.with_memory_space_constraint


def split(value):
    high = value.astype(BF16)
    return high, (value - high.astype(F32)).astype(BF16)


def share_row(part, dish):
    return part * 8 + dish if dish < 8 else 16 + part * 4 + dish - 8


def pieces_kernel(x_ref, out_ref, main, rest, four, in_sems, out_sems, four_sem):
    devices, frames_dev = out_ref.shape[:2]
    low = lax.broadcasted_iota(jnp.int32, (8, LANES), 0) < 4
    rests = [
        pltpu.make_async_copy(x_ref.at[part, devices * 8 :], rest.at[part], in_sems.at[1, part])
        for part in range(2)
    ]
    mains = [
        pltpu.make_async_copy(x_ref.at[part, 0 : devices * 8], main.at[part], in_sems.at[0, part])
        for part in range(2)
    ]
    for load in rests + mains:
        load.start()
    for load in rests:
        load.wait()
    for frame in range(frames_dev):
        lanes = slice(frame * LANES, (frame + 1) * LANES)
        for dev in range(0, devices, 2):
            real = rest[0, dev * 4 : dev * 4 + 8, lanes]
            imag = rest[1, dev * 4 : dev * 4 + 8, lanes]
            four[dev, frame] = jnp.where(low, real, pltpu.roll(imag, 4, 0))
            four[dev + 1, frame] = jnp.where(low, pltpu.roll(real, 4, 0), imag)
    moves = [pltpu.make_async_copy(four, out_ref.at[:, :, 16:24, :], four_sem)]
    moves[0].start()
    tiles = main.reshape(2, devices, 8, main.shape[2])
    for part in range(2):
        mains[part].wait()
        for frame in range(frames_dev):
            lanes = slice(frame * LANES, (frame + 1) * LANES)
            moves.append(
                pltpu.make_async_copy(
                    tiles.at[part, :, :, lanes],
                    out_ref.at[:, frame, part * 8 : part * 8 + 8, :],
                    out_sems.at[frame, part],
                )
            )
            moves[-1].start()
    for move in moves:
        move.wait()


def weights_kernel(w_ref, order_ref, slot_ref, first_ref, later_ref):
    step = pl.program_id(0)
    order = order_ref[...]
    beams = w_ref.shape[3]

    def make(out_ref):
        for half in range(2):
            hot = (slot_ref[:, half : half + 1] == order).astype(F32).T.astype(BF16)
            for part in range(2):
                value = split(w_ref[0, part].T)[half]
                product = jnp.dot(value, hot, preferred_element_type=F32).astype(BF16)
                rows = slice(part * beams, (part + 1) * beams)
                if half == 0:
                    out_ref[0, rows, :] = product
                else:
                    out_ref[0, rows, :] += product

    @pl.when(step < EARLY)
    def _():
        make(first_ref)

    @pl.when(step >= EARLY)
    def _():
        make(later_ref)


def channel_kernel(
    place_ref, x_ref, proto_ref, table_ref, taps_ref, *refs
):
    out_refs, (poly, spec, filt, ready) = refs[:SIDE], refs[SIDE:]
    place = place_ref[0]
    frames = x_ref.shape[0]
    pfb_count = proto_ref.shape[0]
    fir_count = taps_ref.shape[0]
    group = 8
    low = lax.broadcasted_iota(jnp.int32, (group, 8, LANES), 1) < 4

    spec[0 : fir_count - 1] = jnp.zeros((fir_count - 1, 24, 2 * LANES), F32)
    for first in range(0, frames, group):
        found = []
        for rows in range(0, 24, 8):
            total = None
            for tap in range(pfb_count):
                begin = first - tap
                lost = max(0, -begin)
                if lost >= group:
                    continue
                block = x_ref[begin + lost : begin + group, rows : rows + 8, :]
                term = block * proto_ref[tap : tap + 1, :][None]
                if lost:
                    term = jnp.concatenate([jnp.zeros((lost, 8, LANES), F32), term], axis=0)
                total = term if total is None else total + term
            found.append(total)
        turned = pltpu.roll(found[2], 4, 1)
        other = [found[1], -found[0], jnp.where(low, turned, -turned)]
        for index in range(3):
            rows = slice(index * 8, index * 8 + 8)
            poly[first : first + group, rows, 0:LANES] = found[index]
            poly[first : first + group, rows, LANES : 2 * LANES] = other[index]

    for first in range(0, frames, group):
        value = poly[first : first + group].reshape(group * 24, 2 * LANES)
        high, rest = split(value)
        stacked = jnp.concatenate([high, rest, high], axis=1)
        product = jnp.dot(stacked, table_ref[...], preferred_element_type=F32)
        begin = first + fir_count - 1
        spec[begin : begin + group] = product.reshape(group, 24, 2 * LANES)

    for rows in range(0, 24, 8):
        for first in range(0, frames, group):
            total = None
            for tap in range(fir_count):
                begin = first + fir_count - 1 - tap
                near = spec[begin : begin + group, rows : rows + 8, 0:LANES]
                cross = spec[begin : begin + group, rows : rows + 8, LANES : 2 * LANES]
                term = taps_ref[tap, 0, rows : rows + 8, :][None] * near
                term = term + taps_ref[tap, 1, rows : rows + 8, :][None] * cross
                total = term if total is None else total + term
            for frame in range(group):
                begin = (first + frame) * 24 + rows
                filt[begin : begin + 8, :] = total[frame]

    per_band = ready.shape[1] // 6
    for pair in range(6):
        rows = [
            filt[pl.ds(share_row(part, pair * 2 + odd), frames, stride=24), :]
            for part in range(2)
            for odd in range(2)
        ]
        turned = jnp.concatenate(rows, axis=0).T
        for dev in range(SIDE * SIDE):
            ready[dev ^ place, pair * per_band : (pair + 1) * per_band, :] = turned[
                dev * per_band : (dev + 1) * per_band
            ]
    for outer in range(SIDE):
        out_refs[outer][...] = ready[outer * SIDE : (outer + 1) * SIDE]


def regroup_kernel(*refs):
    arrived, out_refs = refs[:SIDE], refs[SIDE:]
    for outer in range(SIDE):
        for inner in range(1, SIDE):
            out_refs[inner - 1][outer] = arrived[outer][inner]


def beams_kernel(*refs):
    near, far = refs[:SIDE], refs[SIDE : 2 * SIDE - 1]
    early_ref, late_hbm, out_ref, x_ref, late_ref, sems = refs[2 * SIDE - 1 :]
    loads = []
    for step in range(late_ref.shape[0] // 2):
        pair = slice(2 * step, 2 * step + 2)
        loads.append(
            pltpu.make_async_copy(late_hbm.at[pair], late_ref.at[pair], sems.at[step])
        )
        loads[-1].start()
    height = near[0].shape[1]
    for outer in range(SIDE):
        for inner in range(SIDE):
            begin = (outer * SIDE + inner) * height
            block = near[outer][0] if inner == 0 else far[inner - 1][outer]
            x_ref[begin : begin + height, :] = block
    rows = x_ref.shape[0] // 8
    beams = early_ref.shape[1] // 2
    lane = lax.broadcasted_iota(jnp.int32, (rows, LANES), 1)
    even = lane % 64 < 32
    wide = lax.broadcasted_iota(jnp.int32, (beams, LANES), 1)
    even_wide = wide % 64 < 32
    row = lax.broadcasted_iota(jnp.int32, (16, 2 * LANES), 0)
    column = lax.broadcasted_iota(jnp.int32, (16, 2 * LANES), 1)
    pool = jnp.where(row == column % 64 // INTEG, 1.0 / INTEG, 0.0).astype(BF16)
    for step in range(out_ref.shape[0] // 2):
        one = x_ref[pl.ds(2 * step, rows, stride=8), :]
        two = x_ref[pl.ds(2 * step + 1, rows, stride=8), :]
        first = jnp.where(even, one, pltpu.roll(two, 32, 1))
        second = jnp.where(even, pltpu.roll(one, LANES - 32, 1), two)
        field = jnp.concatenate([first, second], axis=0)
        high, rest = split(field)
        both = jnp.concatenate([high, rest], axis=1)
        both = jnp.concatenate([both, both], axis=0)
        if 2 * step < EARLY:
            w_ref, begin = early_ref, 2 * step
        else:
            w_ref, begin = late_ref, 2 * step - EARLY
            loads[begin // 2].wait()
        sums = []
        for index in range(2):
            product = jnp.dot(w_ref[begin + index], both, preferred_element_type=F32)
            sums.append(product[:, 0:LANES] + product[:, LANES : 2 * LANES])
        by_real = jnp.where(even_wide, sums[0][:beams], sums[1][:beams])
        by_imag = jnp.where(even_wide, sums[0][beams:], sums[1][beams:])
        crossed = pltpu.roll(by_imag, 64, 1)
        beam = by_real + jnp.where(wide < 64, -crossed, crossed)
        high, rest = split(beam * beam)
        power = lax.dot_general(
            pool,
            jnp.concatenate([high, rest], axis=1),
            (((1,), (1,)), ((), ())),
            preferred_element_type=F32,
        )
        out_ref[2 * step] = power[0:8]
        out_ref[2 * step + 1] = power[8:16]


def slots_of(devices, place):
    index = np.arange(devices * 12)
    odd, other, pair = index // (devices * 6), index // 6 % devices, index % 6
    own = jnp.asarray(pair * 2 + odd, jnp.int32)
    source = jnp.asarray(other, jnp.int32) ^ place
    dishes = jnp.where(own < 8, source * 8 + own, devices * 8 + source * 4 + own - 8)
    none = jnp.full_like(dishes, -1)
    return jnp.stack([jnp.concatenate([dishes, none]), jnp.concatenate([none, dishes])], axis=1)


def moved(value, step):
    devices = lax.axis_size("band")
    return lax.ppermute(value, "band", [(dev, dev ^ step) for dev in range(devices)])


def dft_parts(channels):
    index = np.arange(channels)
    angle = 2.0 * np.pi * (index[:, None] * index[None, :] % channels) / channels
    cosine = np.cos(angle) / np.sqrt(channels)
    sine = np.sin(angle) / np.sqrt(channels)
    table = np.block([[cosine, sine], [sine, -cosine]]).astype(np.float32)
    high = table.astype(jnp.bfloat16)
    rest = (table - high.astype(np.float32)).astype(jnp.bfloat16)
    return np.concatenate([high, high, rest], axis=0)


def close_body(samples, prototype, dish_filter, beam_weights, dish_order):
    devices = lax.axis_size("band")
    position = lax.axis_index("band")
    channels = prototype.shape[1]
    fir_count = dish_filter.shape[1]
    dishes = dish_filter.shape[2]
    band_chans = beam_weights.shape[1]
    beams = beam_weights.shape[4]
    frames_dev = samples.shape[2] // channels
    frames = frames_dev * devices

    pieces = pl.pallas_call(
        pieces_kernel,
        out_shape=jax.ShapeDtypeStruct((devices, frames_dev, 24, channels), F32),
        in_specs=[HBM],
        out_specs=HBM,
        scratch_shapes=[
            pltpu.VMEM((2, devices * 8, frames_dev * channels), F32),
            pltpu.VMEM((2, dishes - devices * 8, frames_dev * channels), F32),
            pltpu.VMEM((devices, frames_dev, 8, channels), F32),
            pltpu.SemaphoreType.DMA((2, 2)),
            pltpu.SemaphoreType.DMA((frames_dev, 2)),
            pltpu.SemaphoreType.DMA(()),
        ],
        name="pieces",
        compiler_params=GRANT,
    )(held(samples, pltpu.HBM))
    arrived = lax.all_to_all(pieces, "band", split_axis=0, concat_axis=0, tiled=True)

    eight = lax.dynamic_slice_in_dim(dish_filter, position * 8, 8, 2)
    four = lax.dynamic_slice_in_dim(dish_filter, devices * 8 + position * 4, 4, 2)
    taps = jnp.concatenate([eight, eight, four, four], axis=2)
    taps = jnp.transpose(taps, (1, 0, 2, 3))
    def weight_shape(count):
        return jax.ShapeDtypeStruct((count, 2 * beams, 2 * dishes), BF16)

    early, late = pl.pallas_call(
        weights_kernel,
        grid=(band_chans,),
        out_shape=[weight_shape(EARLY), weight_shape(band_chans - EARLY)],
        in_specs=[
            pl.BlockSpec((1, 2, dishes, beams), lambda i: (i, 0, 0, 0)),
            pl.BlockSpec((1, dishes), lambda i: (0, 0)),
            pl.BlockSpec((2 * dishes, 2), lambda i: (0, 0)),
        ],
        out_specs=[
            pl.BlockSpec(
                (1, 2 * beams, 2 * dishes), lambda i: (jnp.minimum(i, EARLY - 1), 0, 0)
            ),
            pl.BlockSpec((1, 2 * beams, 2 * dishes), lambda i: (jnp.maximum(i - EARLY, 0), 0, 0)),
        ],
        name="weights",
        compiler_params=GRANT,
        cost_estimate=pl.CostEstimate(
            flops=8 * 4 * 2 * 192 * 192 * 384, bytes_accessed=5 << 20, transcendentals=0
        ),
    )(beam_weights[0], dish_order.reshape(1, dishes), slots_of(devices, position))
    arrived, early, late = lax.optimization_barrier((arrived, early, late))

    block = (6 * band_chans, channels)
    filtered = pl.pallas_call(
        channel_kernel,
        out_shape=[jax.ShapeDtypeStruct((SIDE,) + block, F32)] * SIDE,
        in_specs=[pl.BlockSpec(memory_space=pltpu.SMEM)] + [VMEM] * 4,
        out_specs=[VMEM] * SIDE,
        scratch_shapes=[
            pltpu.VMEM((frames, 24, 2 * LANES), F32),
            pltpu.VMEM((frames + fir_count - 1, 24, 2 * LANES), F32),
            pltpu.VMEM((frames * 24, LANES), F32),
            pltpu.VMEM((devices,) + block, F32),
        ],
        name="channels",
        compiler_params=GRANT,
    )(
        position.reshape(1),
        held(arrived.reshape(frames, 24, channels), pltpu.VMEM),
        prototype,
        dft_parts(channels),
        taps,
    )
    near = [filtered[0]] + [None] * (SIDE - 1)
    for outer in range(SIDE - 1, 0, -1):
        near[outer] = moved(filtered[outer], outer * SIDE)
    grouped = pl.pallas_call(
        regroup_kernel,
        out_shape=[jax.ShapeDtypeStruct((SIDE,) + block, F32)] * (SIDE - 1),
        in_specs=[VMEM] * SIDE,
        out_specs=[VMEM] * (SIDE - 1),
        name="regroup",
        compiler_params=GRANT,
    )(*near)
    far = [None] * (SIDE - 1)
    for inner in range(SIDE - 1, 0, -1):
        far[inner - 1] = moved(grouped[inner - 1], inner)

    power = pl.pallas_call(
        beams_kernel,
        out_shape=jax.ShapeDtypeStruct((band_chans, frames // INTEG, beams), F32),
        in_specs=[VMEM] * (2 * SIDE) + [HBM],
        out_specs=VMEM,
        scratch_shapes=[
            pltpu.VMEM((devices * 6 * band_chans, channels), F32),
            pltpu.VMEM(late.shape, BF16),
            pltpu.SemaphoreType.DMA((band_chans // 2 - 1,)),
        ],
        name="beams",
        compiler_params=GRANT,
    )(*near, *far, held(early, pltpu.VMEM), held(late, pltpu.HBM))
    return jnp.transpose(power, (0, 2, 1))[None]


def detect(weights, field_real, field_imag):
    def contract(weight_part, field_part):
        return jnp.einsum("qds,dqf->qsf", weight_part, field_part, precision=HIGHEST)

    beam_real = contract(weights[:, 0], field_real) - contract(weights[:, 1], field_imag)
    beam_imag = contract(weights[:, 0], field_imag) + contract(weights[:, 1], field_real)
    energy = beam_real * beam_real + beam_imag * beam_imag
    shaped = energy.reshape(energy.shape[:-1] + (energy.shape[-1] // INTEG, INTEG))
    return jnp.mean(shaped, axis=-1)


def wide_body(samples, prototype, dish_filter, beam_weights, dish_order):
    devices = lax.axis_size("band")
    position = lax.axis_index("band")
    pfb_count, channels = prototype.shape
    fir_count = dish_filter.shape[1]
    dishes = dish_filter.shape[2]
    band_chans = beam_weights.shape[1]
    bands = channels // band_chans
    owners = devices // bands
    frames_dev = samples.shape[2] // channels
    frames = frames_dev * devices
    share = -(-dishes // devices)
    extra = share * devices - dishes

    padded = jnp.pad(samples, ((0, 0), (0, extra), (0, 0)))
    pieces = padded.reshape(2, devices, share, frames_dev, channels)
    pieces = jnp.transpose(pieces, (1, 3, 0, 2, 4)).reshape(
        devices, frames_dev, 2 * share, channels
    )
    arrived = lax.all_to_all(pieces, "band", split_axis=0, concat_axis=0, tiled=True)
    blocks = arrived.reshape(frames, 2 * share, channels)

    history = jnp.pad(blocks, ((pfb_count - 1, 0), (0, 0), (0, 0)))
    polyphase = jnp.zeros_like(blocks)
    for tap_index in range(pfb_count):
        offset = pfb_count - 1 - tap_index
        polyphase = polyphase + prototype[tap_index] * history[offset : offset + frames]
    cosine, sine = fourier_tables(channels)
    both = jnp.dot(polyphase, jnp.concatenate([cosine, sine], axis=1), precision=HIGHEST)
    with_cos = both[..., :channels].reshape(frames, 2, share, channels)
    with_sin = both[..., channels:].reshape(frames, 2, share, channels)
    spec_real = with_cos[:, 0] + with_sin[:, 1]
    spec_imag = with_cos[:, 1] - with_sin[:, 0]

    taps = jnp.pad(dish_filter, ((0, 0), (0, 0), (0, extra), (0, 0)))
    taps = lax.dynamic_slice_in_dim(taps, position * share, share, 2)
    lead = ((fir_count - 1, 0), (0, 0), (0, 0))
    past_real, past_imag = jnp.pad(spec_real, lead), jnp.pad(spec_imag, lead)
    out_real = jnp.zeros_like(spec_real)
    out_imag = jnp.zeros_like(spec_imag)
    for tap_index in range(fir_count):
        offset = fir_count - 1 - tap_index
        part_real = past_real[offset : offset + frames]
        part_imag = past_imag[offset : offset + frames]
        factor_real, factor_imag = taps[0, tap_index], taps[1, tap_index]
        out_real = out_real + factor_real * part_real - factor_imag * part_imag
        out_imag = out_imag + factor_real * part_imag + factor_imag * part_real

    filtered = jnp.stack([out_real, out_imag])
    filtered = filtered.reshape(2, frames, share, bands, band_chans)
    filtered = jnp.transpose(filtered, (3, 0, 2, 4, 1)).reshape(
        bands, 2 * share, band_chans * frames
    )
    filtered = jnp.repeat(filtered, owners, axis=0)
    field = lax.all_to_all(filtered, "band", split_axis=0, concat_axis=0, tiled=True)
    field = field.reshape(devices, 2, share, band_chans, frames)
    field = jnp.transpose(field, (1, 0, 2, 3, 4))
    field = field.reshape(2, devices * share, band_chans, frames)
    field = jnp.take(field, dish_order, axis=1)
    power = detect(beam_weights[0], field[0], field[1])
    return power[None]


def solution(mesh):
    devices = mesh.shape["band"]

    def body(samples, prototype, dish_filter, beam_weights, dish_order):
        channels = prototype.shape[1]
        close = (
            channels == LANES
            and beam_weights.shape[1] == 8
            and devices * 8 == channels
            and devices == SIDE * SIDE
            and dish_filter.shape[2] == 12 * devices
            and samples.shape[2] * devices == 32 * channels
        )
        chosen = close_body if close else wide_body
        return chosen(samples, prototype, dish_filter, beam_weights, dish_order)

    placed = (P(None, None, ("grp", "band")), P(), P(), P("band", None, None, None, None), P())
    return jax.shard_map(
        body,
        mesh=mesh,
        in_specs=placed,
        out_specs=P(("grp", "band"), None, None, None),
        check_vma=False,
    )
```

```python
import math

import jax
import jax.numpy as jnp
import numpy as np
from jax import lax
from jax.experimental import pallas as pl
from jax.experimental.pallas import tpu as pltpu
from jax.sharding import PartitionSpec as P

INTEG = 4
ORDERS = ((6, 2, 5, 1, 7, 3, 4), (2, 7, 1, 4, 3, 6, 5))
STEPS = len(ORDERS[0])
HIGHEST = lax.Precision.HIGHEST
F32 = jnp.float32
BF16 = jnp.bfloat16
LANES = 128
VMEM = pl.BlockSpec(memory_space=pltpu.VMEM)
GRANT = pltpu.CompilerParams(vmem_limit_bytes=16 << 20)


def fourier_tables(length):
    counter = jnp.arange(length, dtype=jnp.int32)
    product = counter[:, None] * counter[None, :] % length
    angles = product.astype(jnp.float32) * (2.0 * math.pi / length)
    factor = 1.0 / math.sqrt(length)
    return (jnp.cos(angles) * factor, jnp.sin(angles) * factor)


def split(value):
    high = value.astype(BF16)
    return high, (value - high.astype(F32)).astype(BF16)


def share_row(part, dish):
    return part * 8 + dish if dish < 8 else 16 + part * 4 + dish - 8


def chip_at(place, step):
    return jnp.where(place % 2 == 0, ORDERS[0][step], ORDERS[1][step])


def pieces_kernel(x_ref, own_ref, other_ref):
    place = lax.axis_index("band")
    chips, frames_dev = own_ref.shape[:2]
    first_rest = chips * 16
    low = lax.broadcasted_iota(jnp.int32, (8, LANES), 0) < 4
    for chip in range(chips):
        for core, out_ref in enumerate((own_ref, other_ref)):
            dest = place ^ (2 * chip + core)
            rows = pl.ds(pl.multiple_of(dest * 8, 8), 8)
            for frame in range(frames_dev):
                lanes = slice(frame * LANES, (frame + 1) * LANES)
                for part in range(2):
                    out_ref[chip, frame, part * 8 : part * 8 + 8, :] = x_ref[part, rows, lanes]
        pair = (place ^ (2 * chip)) // 2
        rows = pl.ds(pl.multiple_of(first_rest + pair * 8, 8), 8)
        for frame in range(frames_dev):
            lanes = slice(frame * LANES, (frame + 1) * LANES)
            real, imag = x_ref[0, rows, lanes], x_ref[1, rows, lanes]
            even = jnp.where(low, real, pltpu.roll(imag, 4, 0))
            odd = jnp.where(low, pltpu.roll(real, 4, 0), imag)
            is_even = place % 2 == 0
            own_ref[chip, frame, 16:24, :] = jnp.where(is_even, even, odd)
            other_ref[chip, frame, 16:24, :] = jnp.where(is_even, odd, even)


def regroup_kernel(own_ref, came_ref, *out_refs):
    place = lax.axis_index("band")
    for step, out_ref in enumerate(out_refs):
        chip = chip_at(place, step)
        out_ref[0] = own_ref[chip]
        out_ref[1] = came_ref[chip]


def sources(place, own_ref, came_ref, far_refs):
    yield 0, own_ref[0]
    yield 1, came_ref[0]
    for step, far_ref in enumerate(far_refs):
        for core in range(2):
            yield 2 * chip_at(place, step) + core, far_ref[core]


def weights_kernel(w_ref, order_ref, slot_ref, out_ref):
    hot = (slot_ref[...] == order_ref[...]).astype(F32).T.astype(BF16)
    beams = w_ref.shape[3]
    for chan in range(w_ref.shape[0]):
        for part in range(2):
            halves = [
                jnp.dot(half, hot, preferred_element_type=F32).astype(BF16)
                for half in split(w_ref[chan, part].T)
            ]
            rows = slice(part * beams, (part + 1) * beams)
            out_ref[chan, rows, :] = jnp.concatenate(halves, axis=1)


def channel_kernel(*refs):
    came, refs = refs[: 2 + STEPS], refs[2 + STEPS :]
    proto_ref, table_ref, taps_ref, own_ref, other_ref = refs[:5]
    past, poly, spec, filt, ready = refs[5:]
    place = lax.axis_index("band")
    pfb_count = proto_ref.shape[0]
    fir_count = taps_ref.shape[0]
    frames_dev = came[0].shape[1]
    frames = poly.shape[0]
    group = 8
    low = lax.broadcasted_iota(jnp.int32, (group, 8, LANES), 1) < 4

    past[0 : pfb_count - 1] = jnp.zeros((pfb_count - 1, 24, LANES), F32)
    for other, block in sources(place, came[0], came[1], came[2:]):
        begin = pfb_count - 1 + (place ^ other) * frames_dev
        past[pl.ds(begin, frames_dev)] = block

    spec[0 : fir_count - 1] = jnp.zeros((fir_count - 1, 24, 2 * LANES), F32)
    for first in range(0, frames, group):
        found = []
        for rows in range(0, 24, 8):
            total = None
            for tap in range(pfb_count):
                begin = first + pfb_count - 1 - tap
                block = past[begin : begin + group, rows : rows + 8, :]
                term = block * proto_ref[tap : tap + 1, :][None]
                total = term if total is None else total + term
            found.append(total)
        turned = pltpu.roll(found[2], 4, 1)
        other = [found[1], -found[0], jnp.where(low, turned, -turned)]
        for index in range(3):
            rows = slice(index * 8, index * 8 + 8)
            poly[first : first + group, rows, 0:LANES] = found[index]
            poly[first : first + group, rows, LANES : 2 * LANES] = other[index]

    for first in range(0, frames, group):
        value = poly[first : first + group].reshape(group * 24, 2 * LANES)
        high, rest = split(value)
        stacked = jnp.concatenate([high, rest, high], axis=1)
        product = jnp.dot(stacked, table_ref[...], preferred_element_type=F32)
        begin = first + fir_count - 1
        spec[begin : begin + group] = product.reshape(group, 24, 2 * LANES)

    for rows in range(0, 24, 8):
        for first in range(0, frames, group):
            total = None
            for tap in range(fir_count):
                begin = first + fir_count - 1 - tap
                near = spec[begin : begin + group, rows : rows + 8, 0:LANES]
                cross = spec[begin : begin + group, rows : rows + 8, LANES : 2 * LANES]
                term = taps_ref[tap, 0, rows : rows + 8, :][None] * near
                term = term + taps_ref[tap, 1, rows : rows + 8, :][None] * cross
                total = term if total is None else total + term
            for frame in range(group):
                begin = (first + frame) * 24 + rows
                filt[begin : begin + 8, :] = total[frame]

    per_band = ready.shape[1] // 6
    for pair in range(6):
        rows = [
            filt[pl.ds(share_row(part, pair * 2 + odd), frames, stride=24), :]
            for part in range(2)
            for odd in range(2)
        ]
        turned = jnp.concatenate(rows, axis=0).T
        for dev in range(ready.shape[0]):
            ready[dev ^ place, pair * per_band : (pair + 1) * per_band, :] = turned[
                dev * per_band : (dev + 1) * per_band
            ]
    for chip in range(ready.shape[0] // 2):
        own_ref[chip] = ready[2 * chip]
        other_ref[chip] = ready[2 * chip + 1]


def beams_kernel(*refs):
    came, (w_ref, out_ref, x_ref) = refs[: 2 + STEPS], refs[2 + STEPS :]
    place = lax.axis_index("band")
    height = came[0].shape[1]
    for other, block in sources(place, came[0], came[1], came[2:]):
        x_ref[pl.ds(pl.multiple_of(other * height, 8), height), :] = block
    rows = x_ref.shape[0] // 8
    beams = w_ref.shape[1] // 2
    lane = lax.broadcasted_iota(jnp.int32, (rows, LANES), 1)
    even = lane % 64 < 32
    wide = lax.broadcasted_iota(jnp.int32, (beams, LANES), 1)
    even_wide = wide % 64 < 32
    row = lax.broadcasted_iota(jnp.int32, (16, 2 * LANES), 0)
    column = lax.broadcasted_iota(jnp.int32, (16, 2 * LANES), 1)
    pool = jnp.where(row == column % 64 // INTEG, 1.0 / INTEG, 0.0).astype(BF16)
    for step in range(out_ref.shape[0] // 2):
        one = x_ref[pl.ds(2 * step, rows, stride=8), :]
        two = x_ref[pl.ds(2 * step + 1, rows, stride=8), :]
        first = jnp.where(even, one, pltpu.roll(two, 32, 1))
        second = jnp.where(even, pltpu.roll(one, LANES - 32, 1), two)
        field = jnp.concatenate([first, second], axis=0)
        high, rest = split(field)
        both = jnp.concatenate([high, rest], axis=1)
        both = jnp.concatenate([both, both], axis=0)
        sums = []
        for index in range(2):
            product = jnp.dot(w_ref[2 * step + index], both, preferred_element_type=F32)
            sums.append(product[:, 0:LANES] + product[:, LANES : 2 * LANES])
        by_real = jnp.where(even_wide, sums[0][:beams], sums[1][:beams])
        by_imag = jnp.where(even_wide, sums[0][beams:], sums[1][beams:])
        crossed = pltpu.roll(by_imag, 64, 1)
        beam = by_real + jnp.where(wide < 64, -crossed, crossed)
        high, rest = split(beam * beam)
        power = lax.dot_general(
            pool,
            jnp.concatenate([high, rest], axis=1),
            (((1,), (1,)), ((), ())),
            preferred_element_type=F32,
        )
        out_ref[2 * step] = power[0:8]
        out_ref[2 * step + 1] = power[8:16]


def slots_of(devices, place):
    index = np.arange(devices * 12)
    odd, other, pair = index // (devices * 6), index // 6 % devices, index % 6
    own = jnp.asarray(pair * 2 + odd, jnp.int32)
    source = jnp.asarray(other, jnp.int32) ^ place
    dishes = jnp.where(own < 8, source * 8 + own, devices * 8 + source * 4 + own - 8)
    return dishes[:, None]


def exchange(own, other):
    devices = lax.axis_size("band")

    def moved(value, steps):
        pairs = [(dev, dev ^ steps[dev % 2]) for dev in range(devices)]
        return lax.ppermute(value, "band", pairs)

    came = moved(other, (1, 1))
    grouped = pl.pallas_call(
        regroup_kernel,
        out_shape=[jax.ShapeDtypeStruct((2,) + own.shape[1:], F32)] * STEPS,
        in_specs=[VMEM] * 2,
        out_specs=[VMEM] * STEPS,
        name="regroup",
        compiler_params=GRANT,
    )(own, came)
    far = [
        moved(grouped[step], (2 * ORDERS[0][step], 2 * ORDERS[1][step])) for step in range(STEPS)
    ]
    return [own, came] + far


def dft_parts(channels):
    index = np.arange(channels)
    angle = 2.0 * np.pi * (index[:, None] * index[None, :] % channels) / channels
    cosine = np.cos(angle) / np.sqrt(channels)
    sine = np.sin(angle) / np.sqrt(channels)
    table = np.block([[cosine, sine], [sine, -cosine]]).astype(np.float32)
    high = table.astype(jnp.bfloat16)
    rest = (table - high.astype(np.float32)).astype(jnp.bfloat16)
    return np.concatenate([high, high, rest], axis=0)


def close_body(samples, prototype, dish_filter, beam_weights, dish_order):
    devices = lax.axis_size("band")
    position = lax.axis_index("band")
    channels = prototype.shape[1]
    fir_count = dish_filter.shape[1]
    dishes = dish_filter.shape[2]
    band_chans = beam_weights.shape[1]
    beams = beam_weights.shape[4]
    frames_dev = samples.shape[2] // channels
    frames = frames_dev * devices

    chips = devices // 2
    pieces = pl.pallas_call(
        pieces_kernel,
        out_shape=[jax.ShapeDtypeStruct((chips, frames_dev, 24, channels), F32)] * 2,
        in_specs=[VMEM],
        out_specs=[VMEM] * 2,
        name="pieces",
        compiler_params=GRANT,
    )(samples)
    arrived = exchange(*pieces)

    eight = lax.dynamic_slice_in_dim(dish_filter, position * 8, 8, 2)
    four = lax.dynamic_slice_in_dim(dish_filter, devices * 8 + position * 4, 4, 2)
    taps = jnp.concatenate([eight, eight, four, four], axis=2)
    taps = jnp.transpose(taps, (1, 0, 2, 3))
    weights = pl.pallas_call(
        weights_kernel,
        out_shape=jax.ShapeDtypeStruct((band_chans, 2 * beams, 2 * dishes), BF16),
        in_specs=[VMEM] * 3,
        out_specs=VMEM,
        name="weights",
        compiler_params=GRANT,
        cost_estimate=pl.CostEstimate(
            flops=8 * 4 * 2 * 192 * 192 * 384, bytes_accessed=5 << 20, transcendentals=0
        ),
    )(beam_weights[0], dish_order.reshape(1, dishes), slots_of(devices, position))

    block = (6 * band_chans, channels)
    filtered = pl.pallas_call(
        channel_kernel,
        out_shape=[jax.ShapeDtypeStruct((chips,) + block, F32)] * 2,
        in_specs=[VMEM] * (5 + STEPS),
        out_specs=[VMEM] * 2,
        scratch_shapes=[
            pltpu.VMEM((frames + prototype.shape[0] - 1, 24, LANES), F32),
            pltpu.VMEM((frames, 24, 2 * LANES), F32),
            pltpu.VMEM((frames + fir_count - 1, 24, 2 * LANES), F32),
            pltpu.VMEM((frames * 24, LANES), F32),
            pltpu.VMEM((devices,) + block, F32),
        ],
        name="channels",
        compiler_params=GRANT,
    )(*arrived, prototype, dft_parts(channels), taps)
    field = exchange(*filtered)

    power = pl.pallas_call(
        beams_kernel,
        out_shape=jax.ShapeDtypeStruct((band_chans, frames // INTEG, beams), F32),
        in_specs=[VMEM] * (3 + STEPS),
        out_specs=VMEM,
        scratch_shapes=[pltpu.VMEM((devices * 6 * band_chans, channels), F32)],
        name="beams",
        compiler_params=GRANT,
    )(*field, weights)
    return jnp.transpose(power, (0, 2, 1))[None]


def detect(weights, field_real, field_imag):
    def contract(weight_part, field_part):
        return jnp.einsum("qds,dqf->qsf", weight_part, field_part, precision=HIGHEST)

    beam_real = contract(weights[:, 0], field_real) - contract(weights[:, 1], field_imag)
    beam_imag = contract(weights[:, 0], field_imag) + contract(weights[:, 1], field_real)
    energy = beam_real * beam_real + beam_imag * beam_imag
    shaped = energy.reshape(energy.shape[:-1] + (energy.shape[-1] // INTEG, INTEG))
    return jnp.mean(shaped, axis=-1)


def wide_body(samples, prototype, dish_filter, beam_weights, dish_order):
    devices = lax.axis_size("band")
    position = lax.axis_index("band")
    pfb_count, channels = prototype.shape
    fir_count = dish_filter.shape[1]
    dishes = dish_filter.shape[2]
    band_chans = beam_weights.shape[1]
    bands = channels // band_chans
    owners = devices // bands
    frames_dev = samples.shape[2] // channels
    frames = frames_dev * devices
    share = -(-dishes // devices)
    extra = share * devices - dishes

    padded = jnp.pad(samples, ((0, 0), (0, extra), (0, 0)))
    pieces = padded.reshape(2, devices, share, frames_dev, channels)
    pieces = jnp.transpose(pieces, (1, 3, 0, 2, 4)).reshape(
        devices, frames_dev, 2 * share, channels
    )
    arrived = lax.all_to_all(pieces, "band", split_axis=0, concat_axis=0, tiled=True)
    blocks = arrived.reshape(frames, 2 * share, channels)

    history = jnp.pad(blocks, ((pfb_count - 1, 0), (0, 0), (0, 0)))
    polyphase = jnp.zeros_like(blocks)
    for tap_index in range(pfb_count):
        offset = pfb_count - 1 - tap_index
        polyphase = polyphase + prototype[tap_index] * history[offset : offset + frames]
    cosine, sine = fourier_tables(channels)
    both = jnp.dot(polyphase, jnp.concatenate([cosine, sine], axis=1), precision=HIGHEST)
    with_cos = both[..., :channels].reshape(frames, 2, share, channels)
    with_sin = both[..., channels:].reshape(frames, 2, share, channels)
    spec_real = with_cos[:, 0] + with_sin[:, 1]
    spec_imag = with_cos[:, 1] - with_sin[:, 0]

    taps = jnp.pad(dish_filter, ((0, 0), (0, 0), (0, extra), (0, 0)))
    taps = lax.dynamic_slice_in_dim(taps, position * share, share, 2)
    lead = ((fir_count - 1, 0), (0, 0), (0, 0))
    past_real, past_imag = jnp.pad(spec_real, lead), jnp.pad(spec_imag, lead)
    out_real = jnp.zeros_like(spec_real)
    out_imag = jnp.zeros_like(spec_imag)
    for tap_index in range(fir_count):
        offset = fir_count - 1 - tap_index
        part_real = past_real[offset : offset + frames]
        part_imag = past_imag[offset : offset + frames]
        factor_real, factor_imag = taps[0, tap_index], taps[1, tap_index]
        out_real = out_real + factor_real * part_real - factor_imag * part_imag
        out_imag = out_imag + factor_real * part_imag + factor_imag * part_real

    filtered = jnp.stack([out_real, out_imag])
    filtered = filtered.reshape(2, frames, share, bands, band_chans)
    filtered = jnp.transpose(filtered, (3, 0, 2, 4, 1)).reshape(
        bands, 2 * share, band_chans * frames
    )
    filtered = jnp.repeat(filtered, owners, axis=0)
    field = lax.all_to_all(filtered, "band", split_axis=0, concat_axis=0, tiled=True)
    field = field.reshape(devices, 2, share, band_chans, frames)
    field = jnp.transpose(field, (1, 0, 2, 3, 4))
    field = field.reshape(2, devices * share, band_chans, frames)
    field = jnp.take(field, dish_order, axis=1)
    power = detect(beam_weights[0], field[0], field[1])
    return power[None]


def solution(mesh):
    devices = mesh.shape["band"]

    def body(samples, prototype, dish_filter, beam_weights, dish_order):
        channels = prototype.shape[1]
        close = (
            channels == LANES
            and beam_weights.shape[1] == 8
            and devices * 8 == channels
            and devices == 2 * (STEPS + 1)
            and dish_filter.shape[2] == 12 * devices
            and samples.shape[2] * devices == 32 * channels
        )
        chosen = close_body if close else wide_body
        return chosen(samples, prototype, dish_filter, beam_weights, dish_order)

    placed = (P(None, None, ("grp", "band")), P(), P(), P("band", None, None, None, None), P())
    return jax.shard_map(
        body,
        mesh=mesh,
        in_specs=placed,
        out_specs=P(("grp", "band"), None, None, None),
        check_vma=False,
    )
```

```python
import math

import jax
import jax.numpy as jnp
import numpy as np
from jax import lax
from jax.experimental import pallas as pl
from jax.experimental.pallas import tpu as pltpu
from jax.sharding import PartitionSpec as P

INTEG = 4
ORDERS = ((6, 2, 5, 1, 7, 3, 4), (2, 7, 1, 4, 3, 6, 5))
STEPS = len(ORDERS[0])
HIGHEST = lax.Precision.HIGHEST
F32 = jnp.float32
BF16 = jnp.bfloat16
LANES = 128
VMEM = pl.BlockSpec(memory_space=pltpu.VMEM)
HBM = pl.BlockSpec(memory_space=pltpu.HBM)
GRANT = pltpu.CompilerParams(vmem_limit_bytes=16 << 20)


def fourier_tables(length):
    counter = jnp.arange(length, dtype=jnp.int32)
    product = counter[:, None] * counter[None, :] % length
    angles = product.astype(jnp.float32) * (2.0 * math.pi / length)
    factor = 1.0 / math.sqrt(length)
    return (jnp.cos(angles) * factor, jnp.sin(angles) * factor)


held = pltpu.with_memory_space_constraint


def split(value):
    high = value.astype(BF16)
    return high, (value - high.astype(F32)).astype(BF16)


def share_row(part, dish):
    return part * 8 + dish if dish < 8 else 16 + part * 4 + dish - 8


def chip_at(place, step):
    return jnp.where(place % 2 == 0, ORDERS[0][step], ORDERS[1][step])


def pieces_kernel(x_ref, own_ref, other_ref):
    place = lax.axis_index("band")
    chips, frames_dev = own_ref.shape[:2]
    first_rest = chips * 16
    low = lax.broadcasted_iota(jnp.int32, (8, LANES), 0) < 4
    for chip in range(chips):
        for core, out_ref in enumerate((own_ref, other_ref)):
            dest = place ^ (2 * chip + core)
            rows = pl.ds(pl.multiple_of(dest * 8, 8), 8)
            for frame in range(frames_dev):
                lanes = slice(frame * LANES, (frame + 1) * LANES)
                for part in range(2):
                    out_ref[chip, frame, part * 8 : part * 8 + 8, :] = x_ref[part, rows, lanes]
        pair = (place ^ (2 * chip)) // 2
        rows = pl.ds(pl.multiple_of(first_rest + pair * 8, 8), 8)
        for frame in range(frames_dev):
            lanes = slice(frame * LANES, (frame + 1) * LANES)
            real, imag = x_ref[0, rows, lanes], x_ref[1, rows, lanes]
            even = jnp.where(low, real, pltpu.roll(imag, 4, 0))
            odd = jnp.where(low, pltpu.roll(real, 4, 0), imag)
            is_even = place % 2 == 0
            own_ref[chip, frame, 16:24, :] = jnp.where(is_even, even, odd)
            other_ref[chip, frame, 16:24, :] = jnp.where(is_even, odd, even)


def regroup_kernel(own_ref, came_ref, *out_refs):
    place = lax.axis_index("band")
    for step, out_ref in enumerate(out_refs):
        chip = chip_at(place, step)
        out_ref[0] = own_ref[chip]
        out_ref[1] = came_ref[chip]


def sources(place, own_ref, came_ref, far_refs):
    yield 0, own_ref[0]
    yield 1, came_ref[0]
    for step, far_ref in enumerate(far_refs):
        for core in range(2):
            yield 2 * chip_at(place, step) + core, far_ref[core]


def weights_kernel(
    w_ref, order_ref, slot_ref, table_ref, out_ref, table_out_ref, buffer, sems, table_sem
):
    table_copy = pltpu.make_async_copy(table_ref, table_out_ref, table_sem)
    loads = [
        pltpu.make_async_copy(w_ref.at[chan], buffer.at[chan], sems.at[chan])
        for chan in range(w_ref.shape[0])
    ]
    ahead = 3
    for load in loads[:ahead]:
        load.start()
    hot = (slot_ref[...] == order_ref[...]).astype(F32).T.astype(BF16)
    beams = w_ref.shape[3]
    for chan, load in enumerate(loads):
        load.wait()
        if chan + ahead < len(loads):
            loads[chan + ahead].start()
        elif chan + ahead == len(loads):
            table_copy.start()
        for part in range(2):
            halves = [
                jnp.dot(half, hot, preferred_element_type=F32).astype(BF16)
                for half in split(buffer[chan, part].T)
            ]
            rows = slice(part * beams, (part + 1) * beams)
            out_ref[chan, rows, :] = jnp.concatenate(halves, axis=1)
    table_copy.wait()


def channel_kernel(*refs):
    came, refs = refs[: 2 + STEPS], refs[2 + STEPS :]
    proto_ref, table_ref, taps_ref, own_ref, other_ref = refs[:5]
    past, poly, spec, filt, ready = refs[5:]
    place = lax.axis_index("band")
    pfb_count = proto_ref.shape[0]
    fir_count = taps_ref.shape[0]
    frames_dev = came[0].shape[1]
    frames = poly.shape[0]
    group = 8
    low = lax.broadcasted_iota(jnp.int32, (group, 8, LANES), 1) < 4

    past[0 : pfb_count - 1] = jnp.zeros((pfb_count - 1, 24, LANES), F32)
    for other, block in sources(place, came[0], came[1], came[2:]):
        begin = pfb_count - 1 + (place ^ other) * frames_dev
        past[pl.ds(begin, frames_dev)] = block

    spec[0 : fir_count - 1] = jnp.zeros((fir_count - 1, 24, 2 * LANES), F32)
    for first in range(0, frames, group):
        found = []
        for rows in range(0, 24, 8):
            total = None
            for tap in range(pfb_count):
                begin = first + pfb_count - 1 - tap
                block = past[begin : begin + group, rows : rows + 8, :]
                term = block * proto_ref[tap : tap + 1, :][None]
                total = term if total is None else total + term
            found.append(total)
        turned = pltpu.roll(found[2], 4, 1)
        other = [found[1], -found[0], jnp.where(low, turned, -turned)]
        for index in range(3):
            rows = slice(index * 8, index * 8 + 8)
            poly[first : first + group, rows, 0:LANES] = found[index]
            poly[first : first + group, rows, LANES : 2 * LANES] = other[index]

    for first in range(0, frames, group):
        value = poly[first : first + group].reshape(group * 24, 2 * LANES)
        high, rest = split(value)
        stacked = jnp.concatenate([high, rest, high], axis=1)
        product = jnp.dot(stacked, table_ref[...], preferred_element_type=F32)
        begin = first + fir_count - 1
        spec[begin : begin + group] = product.reshape(group, 24, 2 * LANES)

    for rows in range(0, 24, 8):
        for first in range(0, frames, group):
            total = None
            for tap in range(fir_count):
                begin = first + fir_count - 1 - tap
                near = spec[begin : begin + group, rows : rows + 8, 0:LANES]
                cross = spec[begin : begin + group, rows : rows + 8, LANES : 2 * LANES]
                term = taps_ref[tap, 0, rows : rows + 8, :][None] * near
                term = term + taps_ref[tap, 1, rows : rows + 8, :][None] * cross
                total = term if total is None else total + term
            for frame in range(group):
                begin = (first + frame) * 24 + rows
                filt[begin : begin + 8, :] = total[frame]

    per_band = ready.shape[1] // 6
    for pair in range(6):
        rows = [
            filt[pl.ds(share_row(part, pair * 2 + odd), frames, stride=24), :]
            for part in range(2)
            for odd in range(2)
        ]
        turned = jnp.concatenate(rows, axis=0).T
        for dev in range(ready.shape[0]):
            ready[dev ^ place, pair * per_band : (pair + 1) * per_band, :] = turned[
                dev * per_band : (dev + 1) * per_band
            ]
    for chip in range(ready.shape[0] // 2):
        own_ref[chip] = ready[2 * chip]
        other_ref[chip] = ready[2 * chip + 1]


def beams_kernel(*refs):
    came, (w_ref, out_ref, x_ref) = refs[: 2 + STEPS], refs[2 + STEPS :]
    place = lax.axis_index("band")
    height = came[0].shape[1]
    for other, block in sources(place, came[0], came[1], came[2:]):
        x_ref[pl.ds(pl.multiple_of(other * height, 8), height), :] = block
    rows = x_ref.shape[0] // 8
    beams = w_ref.shape[1] // 2
    lane = lax.broadcasted_iota(jnp.int32, (rows, LANES), 1)
    even = lane % 64 < 32
    wide = lax.broadcasted_iota(jnp.int32, (beams, LANES), 1)
    even_wide = wide % 64 < 32
    row = lax.broadcasted_iota(jnp.int32, (16, 2 * LANES), 0)
    column = lax.broadcasted_iota(jnp.int32, (16, 2 * LANES), 1)
    pool = jnp.where(row == column % 64 // INTEG, 1.0 / INTEG, 0.0).astype(BF16)
    steps = range(out_ref.shape[0] // 2)
    fields = []
    for step in steps:
        one = x_ref[pl.ds(2 * step, rows, stride=8), :]
        two = x_ref[pl.ds(2 * step + 1, rows, stride=8), :]
        first = jnp.where(even, one, pltpu.roll(two, 32, 1))
        second = jnp.where(even, pltpu.roll(one, LANES - 32, 1), two)
        both = jnp.concatenate(split(jnp.concatenate([first, second], axis=0)), axis=1)
        fields.append(jnp.concatenate([both, both], axis=0))
    beam_of = []
    for step in steps:
        sums = []
        for index in range(2):
            product = jnp.dot(w_ref[2 * step + index], fields[step], preferred_element_type=F32)
            sums.append(product[:, 0:LANES] + product[:, LANES : 2 * LANES])
        by_real = jnp.where(even_wide, sums[0][:beams], sums[1][:beams])
        by_imag = jnp.where(even_wide, sums[0][beams:], sums[1][beams:])
        crossed = pltpu.roll(by_imag, 64, 1)
        beam_of.append(by_real + jnp.where(wide < 64, -crossed, crossed))
    for step in steps:
        power = lax.dot_general(
            pool,
            jnp.concatenate(split(beam_of[step] * beam_of[step]), axis=1),
            (((1,), (1,)), ((), ())),
            preferred_element_type=F32,
        )
        out_ref[2 * step] = power[0:8]
        out_ref[2 * step + 1] = power[8:16]


def slots_of(devices, place):
    index = np.arange(devices * 12)
    odd, other, pair = index // (devices * 6), index // 6 % devices, index % 6
    own = jnp.asarray(pair * 2 + odd, jnp.int32)
    source = jnp.asarray(other, jnp.int32) ^ place
    dishes = jnp.where(own < 8, source * 8 + own, devices * 8 + source * 4 + own - 8)
    return dishes[:, None]


def exchange(own, other):
    devices = lax.axis_size("band")

    def moved(value, steps):
        pairs = [(dev, dev ^ steps[dev % 2]) for dev in range(devices)]
        return lax.ppermute(value, "band", pairs)

    came = moved(other, (1, 1))
    grouped = pl.pallas_call(
        regroup_kernel,
        out_shape=[jax.ShapeDtypeStruct((2,) + own.shape[1:], F32)] * STEPS,
        in_specs=[VMEM] * 2,
        out_specs=[VMEM] * STEPS,
        name="regroup",
        compiler_params=GRANT,
    )(own, came)
    far = [
        moved(grouped[step], (2 * ORDERS[0][step], 2 * ORDERS[1][step])) for step in range(STEPS)
    ]
    return [own, came] + far


def dft_parts(channels):
    index = np.arange(channels)
    angle = 2.0 * np.pi * (index[:, None] * index[None, :] % channels) / channels
    cosine = np.cos(angle) / np.sqrt(channels)
    sine = np.sin(angle) / np.sqrt(channels)
    table = np.block([[cosine, sine], [sine, -cosine]]).astype(np.float32)
    high = table.astype(jnp.bfloat16)
    rest = (table - high.astype(np.float32)).astype(jnp.bfloat16)
    return np.concatenate([high, high, rest], axis=0)


def close_body(samples, prototype, dish_filter, beam_weights, dish_order):
    devices = lax.axis_size("band")
    position = lax.axis_index("band")
    channels = prototype.shape[1]
    fir_count = dish_filter.shape[1]
    dishes = dish_filter.shape[2]
    band_chans = beam_weights.shape[1]
    beams = beam_weights.shape[4]
    frames_dev = samples.shape[2] // channels
    frames = frames_dev * devices

    chips = devices // 2
    pieces = pl.pallas_call(
        pieces_kernel,
        out_shape=[jax.ShapeDtypeStruct((chips, frames_dev, 24, channels), F32)] * 2,
        in_specs=[VMEM],
        out_specs=[VMEM] * 2,
        name="pieces",
        compiler_params=GRANT,
    )(samples)
    arrived = exchange(*pieces)

    eight = lax.dynamic_slice_in_dim(dish_filter, position * 8, 8, 2)
    four = lax.dynamic_slice_in_dim(dish_filter, devices * 8 + position * 4, 4, 2)
    taps = jnp.concatenate([eight, eight, four, four], axis=2)
    taps = jnp.transpose(taps, (1, 0, 2, 3))
    table = dft_parts(channels)
    weights, table = pl.pallas_call(
        weights_kernel,
        out_shape=[
            jax.ShapeDtypeStruct((band_chans, 2 * beams, 2 * dishes), BF16),
            jax.ShapeDtypeStruct(table.shape, BF16),
        ],
        in_specs=[HBM, VMEM, VMEM, HBM],
        out_specs=[VMEM] * 2,
        scratch_shapes=[
            pltpu.VMEM((band_chans, 2, dishes, beams), F32),
            pltpu.SemaphoreType.DMA((band_chans,)),
            pltpu.SemaphoreType.DMA(()),
        ],
        name="weights",
        compiler_params=GRANT,
        cost_estimate=pl.CostEstimate(
            flops=8 * 4 * 2 * 192 * 192 * 384, bytes_accessed=5 << 20, transcendentals=0
        ),
    )(
        held(beam_weights[0], pltpu.HBM),
        dish_order.reshape(1, dishes),
        slots_of(devices, position),
        held(jnp.asarray(table), pltpu.HBM),
    )
    *arrived, weights, table = lax.optimization_barrier((*arrived, weights, table))

    block = (6 * band_chans, channels)
    filtered = pl.pallas_call(
        channel_kernel,
        out_shape=[jax.ShapeDtypeStruct((chips,) + block, F32)] * 2,
        in_specs=[VMEM] * (5 + STEPS),
        out_specs=[VMEM] * 2,
        scratch_shapes=[
            pltpu.VMEM((frames + prototype.shape[0] - 1, 24, LANES), F32),
            pltpu.VMEM((frames, 24, 2 * LANES), F32),
            pltpu.VMEM((frames + fir_count - 1, 24, 2 * LANES), F32),
            pltpu.VMEM((frames * 24, LANES), F32),
            pltpu.VMEM((devices,) + block, F32),
        ],
        name="channels",
        compiler_params=GRANT,
    )(*arrived, prototype, table, taps)
    field = exchange(*filtered)

    power = pl.pallas_call(
        beams_kernel,
        out_shape=jax.ShapeDtypeStruct((band_chans, frames // INTEG, beams), F32),
        in_specs=[VMEM] * (3 + STEPS),
        out_specs=VMEM,
        scratch_shapes=[pltpu.VMEM((devices * 6 * band_chans, channels), F32)],
        name="beams",
        compiler_params=GRANT,
    )(*field, weights)
    return jnp.transpose(power, (0, 2, 1))[None]


def detect(weights, field_real, field_imag):
    def contract(weight_part, field_part):
        return jnp.einsum("qds,dqf->qsf", weight_part, field_part, precision=HIGHEST)

    beam_real = contract(weights[:, 0], field_real) - contract(weights[:, 1], field_imag)
    beam_imag = contract(weights[:, 0], field_imag) + contract(weights[:, 1], field_real)
    energy = beam_real * beam_real + beam_imag * beam_imag
    shaped = energy.reshape(energy.shape[:-1] + (energy.shape[-1] // INTEG, INTEG))
    return jnp.mean(shaped, axis=-1)


def wide_body(samples, prototype, dish_filter, beam_weights, dish_order):
    devices = lax.axis_size("band")
    position = lax.axis_index("band")
    pfb_count, channels = prototype.shape
    fir_count = dish_filter.shape[1]
    dishes = dish_filter.shape[2]
    band_chans = beam_weights.shape[1]
    bands = channels // band_chans
    owners = devices // bands
    frames_dev = samples.shape[2] // channels
    frames = frames_dev * devices
    share = -(-dishes // devices)
    extra = share * devices - dishes

    padded = jnp.pad(samples, ((0, 0), (0, extra), (0, 0)))
    pieces = padded.reshape(2, devices, share, frames_dev, channels)
    pieces = jnp.transpose(pieces, (1, 3, 0, 2, 4)).reshape(
        devices, frames_dev, 2 * share, channels
    )
    arrived = lax.all_to_all(pieces, "band", split_axis=0, concat_axis=0, tiled=True)
    blocks = arrived.reshape(frames, 2 * share, channels)

    history = jnp.pad(blocks, ((pfb_count - 1, 0), (0, 0), (0, 0)))
    polyphase = jnp.zeros_like(blocks)
    for tap_index in range(pfb_count):
        offset = pfb_count - 1 - tap_index
        polyphase = polyphase + prototype[tap_index] * history[offset : offset + frames]
    cosine, sine = fourier_tables(channels)
    both = jnp.dot(polyphase, jnp.concatenate([cosine, sine], axis=1), precision=HIGHEST)
    with_cos = both[..., :channels].reshape(frames, 2, share, channels)
    with_sin = both[..., channels:].reshape(frames, 2, share, channels)
    spec_real = with_cos[:, 0] + with_sin[:, 1]
    spec_imag = with_cos[:, 1] - with_sin[:, 0]

    taps = jnp.pad(dish_filter, ((0, 0), (0, 0), (0, extra), (0, 0)))
    taps = lax.dynamic_slice_in_dim(taps, position * share, share, 2)
    lead = ((fir_count - 1, 0), (0, 0), (0, 0))
    past_real, past_imag = jnp.pad(spec_real, lead), jnp.pad(spec_imag, lead)
    out_real = jnp.zeros_like(spec_real)
    out_imag = jnp.zeros_like(spec_imag)
    for tap_index in range(fir_count):
        offset = fir_count - 1 - tap_index
        part_real = past_real[offset : offset + frames]
        part_imag = past_imag[offset : offset + frames]
        factor_real, factor_imag = taps[0, tap_index], taps[1, tap_index]
        out_real = out_real + factor_real * part_real - factor_imag * part_imag
        out_imag = out_imag + factor_real * part_imag + factor_imag * part_real

    filtered = jnp.stack([out_real, out_imag])
    filtered = filtered.reshape(2, frames, share, bands, band_chans)
    filtered = jnp.transpose(filtered, (3, 0, 2, 4, 1)).reshape(
        bands, 2 * share, band_chans * frames
    )
    filtered = jnp.repeat(filtered, owners, axis=0)
    field = lax.all_to_all(filtered, "band", split_axis=0, concat_axis=0, tiled=True)
    field = field.reshape(devices, 2, share, band_chans, frames)
    field = jnp.transpose(field, (1, 0, 2, 3, 4))
    field = field.reshape(2, devices * share, band_chans, frames)
    field = jnp.take(field, dish_order, axis=1)
    power = detect(beam_weights[0], field[0], field[1])
    return power[None]


def solution(mesh):
    devices = mesh.shape["band"]

    def body(samples, prototype, dish_filter, beam_weights, dish_order):
        channels = prototype.shape[1]
        close = (
            channels == LANES
            and beam_weights.shape[1] == 8
            and devices * 8 == channels
            and devices == 2 * (STEPS + 1)
            and dish_filter.shape[2] == 12 * devices
            and samples.shape[2] * devices == 32 * channels
        )
        chosen = close_body if close else wide_body
        return chosen(samples, prototype, dish_filter, beam_weights, dish_order)

    placed = (P(None, None, ("grp", "band")), P(), P(), P("band", None, None, None, None), P())
    return jax.shard_map(
        body,
        mesh=mesh,
        in_specs=placed,
        out_specs=P(("grp", "band"), None, None, None),
        check_vma=False,
    )
```

```python
import math

import jax
import jax.numpy as jnp
import numpy as np
from jax import lax
from jax.experimental import pallas as pl
from jax.experimental.pallas import tpu as pltpu
from jax.sharding import PartitionSpec as P

INTEG = 4
HIGHEST = lax.Precision.HIGHEST
F32 = jnp.float32
BF16 = jnp.bfloat16
LANES = 128
VMEM = pl.BlockSpec(memory_space=pltpu.VMEM)
HBM = pl.BlockSpec(memory_space=pltpu.HBM)
GRANT = pltpu.CompilerParams(vmem_limit_bytes=16 << 20)


def fourier_tables(length):
    counter = jnp.arange(length, dtype=jnp.int32)
    product = counter[:, None] * counter[None, :] % length
    angles = product.astype(jnp.float32) * (2.0 * math.pi / length)
    factor = 1.0 / math.sqrt(length)
    return (jnp.cos(angles) * factor, jnp.sin(angles) * factor)


held = pltpu.with_memory_space_constraint


def split(value):
    high = value.astype(BF16)
    return high, (value - high.astype(F32)).astype(BF16)


def share_row(part, dish):
    return part * 8 + dish if dish < 8 else 16 + part * 4 + dish - 8


def pieces_kernel(x_ref, own_ref, other_ref):
    core = lax.axis_index("band") % 2
    chips, frames_dev = own_ref.shape[:2]
    first_rest = chips * 16
    low = lax.broadcasted_iota(jnp.int32, (8, LANES), 0) < 4
    for chip in range(chips):
        for other, out_ref in enumerate((own_ref, other_ref)):
            dest = 2 * chip + (core ^ other)
            rows = pl.ds(pl.multiple_of(dest * 8, 8), 8)
            for frame in range(frames_dev):
                lanes = slice(frame * LANES, (frame + 1) * LANES)
                for part in range(2):
                    out_ref[chip, frame, part * 8 : part * 8 + 8, :] = x_ref[part, rows, lanes]
        rows = slice(first_rest + chip * 8, first_rest + chip * 8 + 8)
        for frame in range(frames_dev):
            lanes = slice(frame * LANES, (frame + 1) * LANES)
            real, imag = x_ref[0, rows, lanes], x_ref[1, rows, lanes]
            even = jnp.where(low, real, pltpu.roll(imag, 4, 0))
            odd = jnp.where(low, pltpu.roll(real, 4, 0), imag)
            own_ref[chip, frame, 16:24, :] = jnp.where(core == 0, even, odd)
            other_ref[chip, frame, 16:24, :] = jnp.where(core == 0, odd, even)


def join_kernel(own_ref, came_ref, out_ref, sems):
    copies = [
        pltpu.make_async_copy(ref, out_ref.at[:, other], sems.at[other])
        for other, ref in enumerate((own_ref, came_ref))
    ]
    for copy in copies:
        copy.start()
    for copy in copies:
        copy.wait()


def weights_kernel(
    w_ref, order_ref, slot_ref, table_ref, out_ref, table_out_ref, buffer, made, sems, table_sem
):
    table_copy = pltpu.make_async_copy(table_ref, table_out_ref, table_sem)
    loads = [
        pltpu.make_async_copy(w_ref.at[chan], buffer.at[chan], sems.at[0, chan])
        for chan in range(w_ref.shape[0])
    ]
    stores = [
        pltpu.make_async_copy(made.at[chan], out_ref.at[chan], sems.at[1, chan])
        for chan in range(w_ref.shape[0])
    ]
    ahead = 3
    for load in loads[:ahead]:
        load.start()
    hot = (slot_ref[...] == order_ref[...]).astype(F32).T.astype(BF16)
    beams = w_ref.shape[3]
    for chan, load in enumerate(loads):
        load.wait()
        if chan + ahead < len(loads):
            loads[chan + ahead].start()
        elif chan + ahead == len(loads):
            table_copy.start()
        for part in range(2):
            halves = [
                jnp.dot(half, hot, preferred_element_type=F32).astype(BF16)
                for half in split(buffer[chan, part].T)
            ]
            rows = slice(part * beams, (part + 1) * beams)
            made[chan, rows, :] = jnp.concatenate(halves, axis=1)
        stores[chan].start()
    for store in stores:
        store.wait()
    table_copy.wait()


def channel_kernel(
    x_ref, proto_ref, table_ref, taps_ref, own_ref, other_ref, past, poly, spec, filt, ready
):
    core = lax.axis_index("band") % 2
    pfb_count = proto_ref.shape[0]
    fir_count = taps_ref.shape[0]
    chips, _, frames_dev = x_ref.shape[:3]
    frames = poly.shape[0]
    group = 8
    low = lax.broadcasted_iota(jnp.int32, (group, 8, LANES), 1) < 4

    past[0 : pfb_count - 1] = jnp.zeros((pfb_count - 1, 24, LANES), F32)
    for chip in range(chips):
        for other in range(2):
            begin = pfb_count - 1 + (2 * chip + (core ^ other)) * frames_dev
            past[pl.ds(begin, frames_dev)] = x_ref[chip, other]

    spec[0 : fir_count - 1] = jnp.zeros((fir_count - 1, 24, 2 * LANES), F32)
    for first in range(0, frames, group):
        found = []
        for rows in range(0, 24, 8):
            total = None
            for tap in range(pfb_count):
                begin = first + pfb_count - 1 - tap
                block = past[begin : begin + group, rows : rows + 8, :]
                term = block * proto_ref[tap : tap + 1, :][None]
                total = term if total is None else total + term
            found.append(total)
        turned = pltpu.roll(found[2], 4, 1)
        other = [found[1], -found[0], jnp.where(low, turned, -turned)]
        for index in range(3):
            rows = slice(index * 8, index * 8 + 8)
            poly[first : first + group, rows, 0:LANES] = found[index]
            poly[first : first + group, rows, LANES : 2 * LANES] = other[index]

    for first in range(0, frames, group):
        value = poly[first : first + group].reshape(group * 24, 2 * LANES)
        high, rest = split(value)
        stacked = jnp.concatenate([high, rest, high], axis=1)
        product = jnp.dot(stacked, table_ref[...], preferred_element_type=F32)
        begin = first + fir_count - 1
        spec[begin : begin + group] = product.reshape(group, 24, 2 * LANES)

    for rows in range(0, 24, 8):
        for first in range(0, frames, group):
            total = None
            for tap in range(fir_count):
                begin = first + fir_count - 1 - tap
                near = spec[begin : begin + group, rows : rows + 8, 0:LANES]
                cross = spec[begin : begin + group, rows : rows + 8, LANES : 2 * LANES]
                term = taps_ref[tap, 0, rows : rows + 8, :][None] * near
                term = term + taps_ref[tap, 1, rows : rows + 8, :][None] * cross
                total = term if total is None else total + term
            for frame in range(group):
                begin = (first + frame) * 24 + rows
                filt[begin : begin + 8, :] = total[frame]

    per_band = ready.shape[2] // 6
    for pair in range(6):
        rows = [
            filt[pl.ds(share_row(part, pair * 2 + odd), frames, stride=24), :]
            for part in range(2)
            for odd in range(2)
        ]
        turned = jnp.concatenate(rows, axis=0).T
        for dev in range(2 * chips):
            ready[(dev % 2) ^ core, dev // 2, pair * per_band : (pair + 1) * per_band, :] = turned[
                dev * per_band : (dev + 1) * per_band
            ]
    own_ref[...] = ready[0]
    other_ref[...] = ready[1]


def beams_kernel(x_ref, w_hbm, out_ref, w_ref, sems):
    loads = [
        pltpu.make_async_copy(w_hbm.at[chan], w_ref.at[chan], sems.at[chan])
        for chan in range(w_hbm.shape[0])
    ]
    ahead = 3
    for load in loads[:ahead]:
        load.start()
    rows = x_ref.shape[0] // 8
    beams = w_ref.shape[1] // 2
    lane = lax.broadcasted_iota(jnp.int32, (rows, LANES), 1)
    even = lane % 64 < 32
    wide = lax.broadcasted_iota(jnp.int32, (beams, LANES), 1)
    even_wide = wide % 64 < 32
    row = lax.broadcasted_iota(jnp.int32, (16, 2 * LANES), 0)
    column = lax.broadcasted_iota(jnp.int32, (16, 2 * LANES), 1)
    pool = jnp.where(row == column % 64 // INTEG, 1.0 / INTEG, 0.0).astype(BF16)
    steps = range(out_ref.shape[0] // 2)
    fields = []
    for step in steps:
        one = x_ref[pl.ds(2 * step, rows, stride=8), :]
        two = x_ref[pl.ds(2 * step + 1, rows, stride=8), :]
        first = jnp.where(even, one, pltpu.roll(two, 32, 1))
        second = jnp.where(even, pltpu.roll(one, LANES - 32, 1), two)
        both = jnp.concatenate(split(jnp.concatenate([first, second], axis=0)), axis=1)
        fields.append(jnp.concatenate([both, both], axis=0))
    beam_of = []
    for step in steps:
        sums = []
        for index in range(2):
            chan = 2 * step + index
            loads[chan].wait()
            if chan + ahead < len(loads):
                loads[chan + ahead].start()
            product = jnp.dot(w_ref[chan], fields[step], preferred_element_type=F32)
            sums.append(product[:, 0:LANES] + product[:, LANES : 2 * LANES])
        by_real = jnp.where(even_wide, sums[0][:beams], sums[1][:beams])
        by_imag = jnp.where(even_wide, sums[0][beams:], sums[1][beams:])
        crossed = pltpu.roll(by_imag, 64, 1)
        beam_of.append(by_real + jnp.where(wide < 64, -crossed, crossed))
    for step in steps:
        power = lax.dot_general(
            pool,
            jnp.concatenate(split(beam_of[step] * beam_of[step]), axis=1),
            (((1,), (1,)), ((), ())),
            preferred_element_type=F32,
        )
        out_ref[2 * step] = power[0:8]
        out_ref[2 * step + 1] = power[8:16]


def slots_of(devices, core):
    index = np.arange(devices * 12)
    odd, other, pair = index // (devices * 6), index // 6 % devices, index % 6
    own = jnp.asarray(pair * 2 + odd, jnp.int32)
    source = jnp.asarray(other, jnp.int32) ^ core
    dishes = jnp.where(own < 8, source * 8 + own, devices * 8 + source * 4 + own - 8)
    return dishes[:, None]


def exchange(own, other):
    devices = lax.axis_size("band")
    came = lax.ppermute(other, "band", [(dev, dev ^ 1) for dev in range(devices)])
    joined = pl.pallas_call(
        join_kernel,
        out_shape=jax.ShapeDtypeStruct((own.shape[0], 2) + own.shape[1:], F32),
        in_specs=[VMEM] * 2,
        out_specs=HBM,
        scratch_shapes=[pltpu.SemaphoreType.DMA((2,))],
        name="join",
        compiler_params=GRANT,
    )(held(own, pltpu.VMEM), held(came, pltpu.VMEM))
    groups = [list(range(core, devices, 2)) for core in range(2)]
    return lax.all_to_all(
        joined, "band", split_axis=0, concat_axis=0, tiled=True, axis_index_groups=groups
    )


def dft_parts(channels):
    index = np.arange(channels)
    angle = 2.0 * np.pi * (index[:, None] * index[None, :] % channels) / channels
    cosine = np.cos(angle) / np.sqrt(channels)
    sine = np.sin(angle) / np.sqrt(channels)
    table = np.block([[cosine, sine], [sine, -cosine]]).astype(np.float32)
    high = table.astype(jnp.bfloat16)
    rest = (table - high.astype(np.float32)).astype(jnp.bfloat16)
    return np.concatenate([high, high, rest], axis=0)


def close_body(samples, prototype, dish_filter, beam_weights, dish_order):
    devices = lax.axis_size("band")
    position = lax.axis_index("band")
    channels = prototype.shape[1]
    fir_count = dish_filter.shape[1]
    dishes = dish_filter.shape[2]
    band_chans = beam_weights.shape[1]
    beams = beam_weights.shape[4]
    frames_dev = samples.shape[2] // channels
    frames = frames_dev * devices

    chips = devices // 2
    pieces = pl.pallas_call(
        pieces_kernel,
        out_shape=[jax.ShapeDtypeStruct((chips, frames_dev, 24, channels), F32)] * 2,
        in_specs=[VMEM],
        out_specs=[VMEM] * 2,
        name="pieces",
        compiler_params=GRANT,
    )(samples)
    arrived = exchange(*pieces)

    eight = lax.dynamic_slice_in_dim(dish_filter, position * 8, 8, 2)
    four = lax.dynamic_slice_in_dim(dish_filter, devices * 8 + position * 4, 4, 2)
    taps = jnp.concatenate([eight, eight, four, four], axis=2)
    taps = jnp.transpose(taps, (1, 0, 2, 3))
    table = dft_parts(channels)
    weights, table = pl.pallas_call(
        weights_kernel,
        out_shape=[
            jax.ShapeDtypeStruct((band_chans, 2 * beams, 2 * dishes), BF16),
            jax.ShapeDtypeStruct(table.shape, BF16),
        ],
        in_specs=[HBM, VMEM, VMEM, HBM],
        out_specs=[HBM, VMEM],
        scratch_shapes=[
            pltpu.VMEM((band_chans, 2, dishes, beams), F32),
            pltpu.VMEM((band_chans, 2 * beams, 2 * dishes), BF16),
            pltpu.SemaphoreType.DMA((2, band_chans)),
            pltpu.SemaphoreType.DMA(()),
        ],
        name="weights",
        compiler_params=GRANT,
        cost_estimate=pl.CostEstimate(
            flops=8 * 4 * 2 * 192 * 192 * 384, bytes_accessed=5 << 20, transcendentals=0
        ),
    )(
        held(beam_weights[0], pltpu.HBM),
        dish_order.reshape(1, dishes),
        slots_of(devices, position % 2),
        held(jnp.asarray(table), pltpu.HBM),
    )
    arrived, weights, table = lax.optimization_barrier((arrived, weights, table))

    block = (6 * band_chans, channels)
    filtered = pl.pallas_call(
        channel_kernel,
        out_shape=[jax.ShapeDtypeStruct((chips,) + block, F32)] * 2,
        in_specs=[VMEM] * 4,
        out_specs=[VMEM] * 2,
        scratch_shapes=[
            pltpu.VMEM((frames + prototype.shape[0] - 1, 24, LANES), F32),
            pltpu.VMEM((frames, 24, 2 * LANES), F32),
            pltpu.VMEM((frames + fir_count - 1, 24, 2 * LANES), F32),
            pltpu.VMEM((frames * 24, LANES), F32),
            pltpu.VMEM((2, chips) + block, F32),
        ],
        name="channels",
        compiler_params=GRANT,
    )(held(arrived, pltpu.VMEM), prototype, held(table, pltpu.VMEM), taps)
    field = exchange(*filtered).reshape(devices * 6 * band_chans, channels)

    power = pl.pallas_call(
        beams_kernel,
        out_shape=jax.ShapeDtypeStruct((band_chans, frames // INTEG, beams), F32),
        in_specs=[VMEM, HBM],
        out_specs=VMEM,
        scratch_shapes=[
            pltpu.VMEM(weights.shape, BF16),
            pltpu.SemaphoreType.DMA((band_chans,)),
        ],
        name="beams",
        compiler_params=GRANT,
    )(held(field, pltpu.VMEM), held(weights, pltpu.HBM))
    return jnp.transpose(power, (0, 2, 1))[None]


def detect(weights, field_real, field_imag):
    def contract(weight_part, field_part):
        return jnp.einsum("qds,dqf->qsf", weight_part, field_part, precision=HIGHEST)

    beam_real = contract(weights[:, 0], field_real) - contract(weights[:, 1], field_imag)
    beam_imag = contract(weights[:, 0], field_imag) + contract(weights[:, 1], field_real)
    energy = beam_real * beam_real + beam_imag * beam_imag
    shaped = energy.reshape(energy.shape[:-1] + (energy.shape[-1] // INTEG, INTEG))
    return jnp.mean(shaped, axis=-1)


def wide_body(samples, prototype, dish_filter, beam_weights, dish_order):
    devices = lax.axis_size("band")
    position = lax.axis_index("band")
    pfb_count, channels = prototype.shape
    fir_count = dish_filter.shape[1]
    dishes = dish_filter.shape[2]
    band_chans = beam_weights.shape[1]
    bands = channels // band_chans
    owners = devices // bands
    frames_dev = samples.shape[2] // channels
    frames = frames_dev * devices
    share = -(-dishes // devices)
    extra = share * devices - dishes

    padded = jnp.pad(samples, ((0, 0), (0, extra), (0, 0)))
    pieces = padded.reshape(2, devices, share, frames_dev, channels)
    pieces = jnp.transpose(pieces, (1, 3, 0, 2, 4)).reshape(
        devices, frames_dev, 2 * share, channels
    )
    arrived = lax.all_to_all(pieces, "band", split_axis=0, concat_axis=0, tiled=True)
    blocks = arrived.reshape(frames, 2 * share, channels)

    history = jnp.pad(blocks, ((pfb_count - 1, 0), (0, 0), (0, 0)))
    polyphase = jnp.zeros_like(blocks)
    for tap_index in range(pfb_count):
        offset = pfb_count - 1 - tap_index
        polyphase = polyphase + prototype[tap_index] * history[offset : offset + frames]
    cosine, sine = fourier_tables(channels)
    both = jnp.dot(polyphase, jnp.concatenate([cosine, sine], axis=1), precision=HIGHEST)
    with_cos = both[..., :channels].reshape(frames, 2, share, channels)
    with_sin = both[..., channels:].reshape(frames, 2, share, channels)
    spec_real = with_cos[:, 0] + with_sin[:, 1]
    spec_imag = with_cos[:, 1] - with_sin[:, 0]

    taps = jnp.pad(dish_filter, ((0, 0), (0, 0), (0, extra), (0, 0)))
    taps = lax.dynamic_slice_in_dim(taps, position * share, share, 2)
    lead = ((fir_count - 1, 0), (0, 0), (0, 0))
    past_real, past_imag = jnp.pad(spec_real, lead), jnp.pad(spec_imag, lead)
    out_real = jnp.zeros_like(spec_real)
    out_imag = jnp.zeros_like(spec_imag)
    for tap_index in range(fir_count):
        offset = fir_count - 1 - tap_index
        part_real = past_real[offset : offset + frames]
        part_imag = past_imag[offset : offset + frames]
        factor_real, factor_imag = taps[0, tap_index], taps[1, tap_index]
        out_real = out_real + factor_real * part_real - factor_imag * part_imag
        out_imag = out_imag + factor_real * part_imag + factor_imag * part_real

    filtered = jnp.stack([out_real, out_imag])
    filtered = filtered.reshape(2, frames, share, bands, band_chans)
    filtered = jnp.transpose(filtered, (3, 0, 2, 4, 1)).reshape(
        bands, 2 * share, band_chans * frames
    )
    filtered = jnp.repeat(filtered, owners, axis=0)
    field = lax.all_to_all(filtered, "band", split_axis=0, concat_axis=0, tiled=True)
    field = field.reshape(devices, 2, share, band_chans, frames)
    field = jnp.transpose(field, (1, 0, 2, 3, 4))
    field = field.reshape(2, devices * share, band_chans, frames)
    field = jnp.take(field, dish_order, axis=1)
    power = detect(beam_weights[0], field[0], field[1])
    return power[None]


def solution(mesh):
    devices = mesh.shape["band"]

    def body(samples, prototype, dish_filter, beam_weights, dish_order):
        channels = prototype.shape[1]
        close = (
            channels == LANES
            and beam_weights.shape[1] == 8
            and devices * 8 == channels
            and devices % 2 == 0
            and dish_filter.shape[2] == 12 * devices
            and samples.shape[2] * devices == 32 * channels
        )
        chosen = close_body if close else wide_body
        return chosen(samples, prototype, dish_filter, beam_weights, dish_order)

    placed = (P(None, None, ("grp", "band")), P(), P(), P("band", None, None, None, None), P())
    return jax.shard_map(
        body,
        mesh=mesh,
        in_specs=placed,
        out_specs=P(("grp", "band"), None, None, None),
        check_vma=False,
    )
```

```python
import math

import jax
import jax.numpy as jnp
import numpy as np
from jax import lax
from jax.experimental import pallas as pl
from jax.experimental.pallas import tpu as pltpu
from jax.sharding import PartitionSpec as P

INTEG = 4
EARLY = 2
HIGHEST = lax.Precision.HIGHEST
F32 = jnp.float32
BF16 = jnp.bfloat16
LANES = 128
VMEM = pl.BlockSpec(memory_space=pltpu.VMEM)
HBM = pl.BlockSpec(memory_space=pltpu.HBM)
GRANT = pltpu.CompilerParams(vmem_limit_bytes=16 << 20)


def fourier_tables(length):
    counter = jnp.arange(length, dtype=jnp.int32)
    product = counter[:, None] * counter[None, :] % length
    angles = product.astype(jnp.float32) * (2.0 * math.pi / length)
    factor = 1.0 / math.sqrt(length)
    return (jnp.cos(angles) * factor, jnp.sin(angles) * factor)


held = pltpu.with_memory_space_constraint


def split(value):
    high = value.astype(BF16)
    return high, (value - high.astype(F32)).astype(BF16)


def share_row(part, dish):
    return part * 8 + dish if dish < 8 else 16 + part * 4 + dish - 8


def pieces_kernel(x_ref, out_ref):
    devices, frames_dev = out_ref.shape[:2]
    low = lax.broadcasted_iota(jnp.int32, (8, LANES), 0) < 4
    for frame in range(frames_dev):
        lanes = slice(frame * LANES, (frame + 1) * LANES)
        for dev in range(0, devices, 2):
            for one in (dev, dev + 1):
                for part in range(2):
                    out_ref[one, frame, part * 8 : part * 8 + 8, :] = x_ref[
                        part, one * 8 : one * 8 + 8, lanes
                    ]
            start = devices * 8 + dev * 4
            real = x_ref[0, start : start + 8, lanes]
            imag = x_ref[1, start : start + 8, lanes]
            out_ref[dev, frame, 16:24, :] = jnp.where(low, real, pltpu.roll(imag, 4, 0))
            out_ref[dev + 1, frame, 16:24, :] = jnp.where(low, pltpu.roll(real, 4, 0), imag)


def weights_kernel(
    w_ref, order_ref, slot_ref, table_ref, early_ref, late_ref, table_out_ref, *scratch
):
    buffer, made, sems, table_sem = scratch
    table_copy = pltpu.make_async_copy(table_ref, table_out_ref, table_sem)
    loads = [
        pltpu.make_async_copy(w_ref.at[chan], buffer.at[chan], sems.at[0, chan])
        for chan in range(w_ref.shape[0])
    ]
    stores = [
        pltpu.make_async_copy(made.at[chan], late_ref.at[chan], sems.at[1, chan])
        for chan in range(late_ref.shape[0])
    ]
    ahead = 3
    for load in loads[:ahead]:
        load.start()
    hot = (slot_ref[...] == order_ref[...]).astype(F32).T.astype(BF16)
    beams = w_ref.shape[3]
    for chan, load in enumerate(loads):
        load.wait()
        if chan + ahead < len(loads):
            loads[chan + ahead].start()
        elif chan + ahead == len(loads):
            table_copy.start()
        for part in range(2):
            halves = [
                jnp.dot(half, hot, preferred_element_type=F32).astype(BF16)
                for half in split(buffer[chan, part].T)
            ]
            rows = slice(part * beams, (part + 1) * beams)
            both = jnp.concatenate(halves, axis=1)
            if chan < EARLY:
                early_ref[chan, rows, :] = both
            else:
                made[chan - EARLY, rows, :] = both
        if chan >= EARLY:
            stores[chan - EARLY].start()
    for store in stores:
        store.wait()
    table_copy.wait()


def channel_kernel(
    x_ref, proto_ref, table_ref, taps_ref, out_ref, past, poly, spec, filt
):
    pfb_count = proto_ref.shape[0]
    fir_count = taps_ref.shape[0]
    frames = poly.shape[0]
    group = 8
    low = lax.broadcasted_iota(jnp.int32, (group, 8, LANES), 1) < 4

    past[0 : pfb_count - 1] = jnp.zeros((pfb_count - 1, 24, LANES), F32)
    past[pfb_count - 1 :] = x_ref[...]

    spec[0 : fir_count - 1] = jnp.zeros((fir_count - 1, 24, 2 * LANES), F32)
    for first in range(0, frames, group):
        found = []
        for rows in range(0, 24, 8):
            total = None
            for tap in range(pfb_count):
                begin = first + pfb_count - 1 - tap
                block = past[begin : begin + group, rows : rows + 8, :]
                term = block * proto_ref[tap : tap + 1, :][None]
                total = term if total is None else total + term
            found.append(total)
        turned = pltpu.roll(found[2], 4, 1)
        other = [found[1], -found[0], jnp.where(low, turned, -turned)]
        for index in range(3):
            rows = slice(index * 8, index * 8 + 8)
            poly[first : first + group, rows, 0:LANES] = found[index]
            poly[first : first + group, rows, LANES : 2 * LANES] = other[index]

    for first in range(0, frames, group):
        value = poly[first : first + group].reshape(group * 24, 2 * LANES)
        high, rest = split(value)
        stacked = jnp.concatenate([high, rest, high], axis=1)
        product = jnp.dot(stacked, table_ref[...], preferred_element_type=F32)
        begin = first + fir_count - 1
        spec[begin : begin + group] = product.reshape(group, 24, 2 * LANES)

    for rows in range(0, 24, 8):
        for first in range(0, frames, group):
            total = None
            for tap in range(fir_count):
                begin = first + fir_count - 1 - tap
                near = spec[begin : begin + group, rows : rows + 8, 0:LANES]
                cross = spec[begin : begin + group, rows : rows + 8, LANES : 2 * LANES]
                term = taps_ref[tap, 0, rows : rows + 8, :][None] * near
                term = term + taps_ref[tap, 1, rows : rows + 8, :][None] * cross
                total = term if total is None else total + term
            for frame in range(group):
                begin = (first + frame) * 24 + rows
                filt[begin : begin + 8, :] = total[frame]

    per_band = out_ref.shape[1] // 6
    for pair in range(6):
        rows = [
            filt[pl.ds(share_row(part, pair * 2 + odd), frames, stride=24), :]
            for part in range(2)
            for odd in range(2)
        ]
        turned = jnp.concatenate(rows, axis=0).T
        for dev in range(out_ref.shape[0]):
            out_ref[dev, pair * per_band : (pair + 1) * per_band, :] = turned[
                dev * per_band : (dev + 1) * per_band
            ]


def beams_kernel(x_ref, early_ref, late_hbm, out_ref, late_ref, sems):
    loads = []
    for step in range(late_hbm.shape[0] // 2):
        pair = slice(2 * step, 2 * step + 2)
        loads.append(
            pltpu.make_async_copy(late_hbm.at[pair], late_ref.at[pair], sems.at[step])
        )
        loads[-1].start()
    rows = x_ref.shape[0] // 8
    beams = early_ref.shape[1] // 2
    lane = lax.broadcasted_iota(jnp.int32, (rows, LANES), 1)
    even = lane % 64 < 32
    wide = lax.broadcasted_iota(jnp.int32, (beams, LANES), 1)
    even_wide = wide % 64 < 32
    row = lax.broadcasted_iota(jnp.int32, (16, 2 * LANES), 0)
    column = lax.broadcasted_iota(jnp.int32, (16, 2 * LANES), 1)
    pool = jnp.where(row == column % 64 // INTEG, 1.0 / INTEG, 0.0).astype(BF16)
    steps = range(out_ref.shape[0] // 2)
    fields = []
    for step in steps:
        one = x_ref[pl.ds(2 * step, rows, stride=8), :]
        two = x_ref[pl.ds(2 * step + 1, rows, stride=8), :]
        first = jnp.where(even, one, pltpu.roll(two, 32, 1))
        second = jnp.where(even, pltpu.roll(one, LANES - 32, 1), two)
        both = jnp.concatenate(split(jnp.concatenate([first, second], axis=0)), axis=1)
        fields.append(jnp.concatenate([both, both], axis=0))
    beam_of = []
    for step in steps:
        if 2 * step < EARLY:
            w_ref, begin = early_ref, 2 * step
        else:
            w_ref, begin = late_ref, 2 * step - EARLY
            loads[begin // 2].wait()
        sums = []
        for index in range(2):
            weights = w_ref[begin + index]
            product = jnp.dot(weights, fields[step], preferred_element_type=F32)
            sums.append(product[:, 0:LANES] + product[:, LANES : 2 * LANES])
        by_real = jnp.where(even_wide, sums[0][:beams], sums[1][:beams])
        by_imag = jnp.where(even_wide, sums[0][beams:], sums[1][beams:])
        crossed = pltpu.roll(by_imag, 64, 1)
        beam_of.append(by_real + jnp.where(wide < 64, -crossed, crossed))
    for step in steps:
        power = lax.dot_general(
            pool,
            jnp.concatenate(split(beam_of[step] * beam_of[step]), axis=1),
            (((1,), (1,)), ((), ())),
            preferred_element_type=F32,
        )
        out_ref[2 * step] = power[0:8]
        out_ref[2 * step + 1] = power[8:16]


def slots_of(devices):
    index = np.arange(devices * 12, dtype=np.int32)
    own = index % 6 * 2 + index // (devices * 6)
    source = index // 6 % devices
    dishes = np.where(own < 8, source * 8 + own, devices * 8 + source * 4 + own - 8)
    return dishes.astype(np.int32)[:, None]


def dft_parts(channels):
    index = np.arange(channels)
    angle = 2.0 * np.pi * (index[:, None] * index[None, :] % channels) / channels
    cosine = np.cos(angle) / np.sqrt(channels)
    sine = np.sin(angle) / np.sqrt(channels)
    table = np.block([[cosine, sine], [sine, -cosine]]).astype(np.float32)
    high = table.astype(jnp.bfloat16)
    rest = (table - high.astype(np.float32)).astype(jnp.bfloat16)
    return np.concatenate([high, high, rest], axis=0)


def close_body(samples, prototype, dish_filter, beam_weights, dish_order):
    devices = lax.axis_size("band")
    position = lax.axis_index("band")
    channels = prototype.shape[1]
    fir_count = dish_filter.shape[1]
    dishes = dish_filter.shape[2]
    band_chans = beam_weights.shape[1]
    beams = beam_weights.shape[4]
    frames_dev = samples.shape[2] // channels
    frames = frames_dev * devices

    def exchange(value):
        return lax.all_to_all(value, "band", split_axis=0, concat_axis=0, tiled=True)

    pieces = pl.pallas_call(
        pieces_kernel,
        out_shape=jax.ShapeDtypeStruct((devices, frames_dev, 24, channels), F32),
        in_specs=[VMEM],
        out_specs=VMEM,
        name="pieces",
        compiler_params=GRANT,
    )(samples)
    arrived = exchange(pieces).reshape(frames, 24, channels)

    eight = lax.dynamic_slice_in_dim(dish_filter, position * 8, 8, 2)
    four = lax.dynamic_slice_in_dim(dish_filter, devices * 8 + position * 4, 4, 2)
    taps = jnp.concatenate([eight, eight, four, four], axis=2)
    taps = jnp.transpose(taps, (1, 0, 2, 3))
    table = dft_parts(channels)
    early, late, table = pl.pallas_call(
        weights_kernel,
        out_shape=[
            jax.ShapeDtypeStruct((EARLY, 2 * beams, 2 * dishes), BF16),
            pltpu.HBM((band_chans - EARLY, 2 * beams, 2 * dishes), BF16),
            jax.ShapeDtypeStruct(table.shape, BF16),
        ],
        in_specs=[HBM, VMEM, VMEM, HBM],
        out_specs=[VMEM, HBM, VMEM],
        scratch_shapes=[
            pltpu.VMEM((band_chans, 2, dishes, beams), F32),
            pltpu.VMEM((band_chans - EARLY, 2 * beams, 2 * dishes), BF16),
            pltpu.SemaphoreType.DMA((2, band_chans)),
            pltpu.SemaphoreType.DMA(()),
        ],
        name="weights",
        compiler_params=GRANT,
        cost_estimate=pl.CostEstimate(
            flops=8 * 4 * 2 * 192 * 192 * 384, bytes_accessed=5 << 20, transcendentals=0
        ),
    )(
        held(beam_weights[0], pltpu.HBM),
        dish_order.reshape(1, dishes),
        slots_of(devices),
        held(jnp.asarray(table), pltpu.HBM),
    )
    arrived, early, late, table = lax.optimization_barrier((arrived, early, late, table))

    block = (6 * band_chans, channels)
    filtered = pl.pallas_call(
        channel_kernel,
        out_shape=jax.ShapeDtypeStruct((devices,) + block, F32),
        in_specs=[VMEM] * 4,
        out_specs=VMEM,
        scratch_shapes=[
            pltpu.VMEM((frames + prototype.shape[0] - 1, 24, LANES), F32),
            pltpu.VMEM((frames, 24, 2 * LANES), F32),
            pltpu.VMEM((frames + fir_count - 1, 24, 2 * LANES), F32),
            pltpu.VMEM((frames * 24, LANES), F32),
        ],
        name="channels",
        compiler_params=GRANT,
    )(held(arrived, pltpu.VMEM), prototype, held(table, pltpu.VMEM), taps)
    field = exchange(filtered).reshape(devices * 6 * band_chans, channels)

    power = pl.pallas_call(
        beams_kernel,
        out_shape=jax.ShapeDtypeStruct((band_chans, frames // INTEG, beams), F32),
        in_specs=[VMEM, VMEM, HBM],
        out_specs=VMEM,
        scratch_shapes=[
            pltpu.VMEM(late.shape, BF16),
            pltpu.SemaphoreType.DMA((late.shape[0] // 2,)),
        ],
        name="beams",
        compiler_params=GRANT,
    )(held(field, pltpu.VMEM), held(early, pltpu.VMEM), held(late, pltpu.HBM))
    return jnp.transpose(power, (0, 2, 1))[None]


def detect(weights, field_real, field_imag):
    def contract(weight_part, field_part):
        return jnp.einsum("qds,dqf->qsf", weight_part, field_part, precision=HIGHEST)

    beam_real = contract(weights[:, 0], field_real) - contract(weights[:, 1], field_imag)
    beam_imag = contract(weights[:, 0], field_imag) + contract(weights[:, 1], field_real)
    energy = beam_real * beam_real + beam_imag * beam_imag
    shaped = energy.reshape(energy.shape[:-1] + (energy.shape[-1] // INTEG, INTEG))
    return jnp.mean(shaped, axis=-1)


def wide_body(samples, prototype, dish_filter, beam_weights, dish_order):
    devices = lax.axis_size("band")
    position = lax.axis_index("band")
    pfb_count, channels = prototype.shape
    fir_count = dish_filter.shape[1]
    dishes = dish_filter.shape[2]
    band_chans = beam_weights.shape[1]
    bands = channels // band_chans
    owners = devices // bands
    frames_dev = samples.shape[2] // channels
    frames = frames_dev * devices
    share = -(-dishes // devices)
    extra = share * devices - dishes

    padded = jnp.pad(samples, ((0, 0), (0, extra), (0, 0)))
    pieces = padded.reshape(2, devices, share, frames_dev, channels)
    pieces = jnp.transpose(pieces, (1, 3, 0, 2, 4)).reshape(
        devices, frames_dev, 2 * share, channels
    )
    arrived = lax.all_to_all(pieces, "band", split_axis=0, concat_axis=0, tiled=True)
    blocks = arrived.reshape(frames, 2 * share, channels)

    history = jnp.pad(blocks, ((pfb_count - 1, 0), (0, 0), (0, 0)))
    polyphase = jnp.zeros_like(blocks)
    for tap_index in range(pfb_count):
        offset = pfb_count - 1 - tap_index
        polyphase = polyphase + prototype[tap_index] * history[offset : offset + frames]
    cosine, sine = fourier_tables(channels)
    both = jnp.dot(polyphase, jnp.concatenate([cosine, sine], axis=1), precision=HIGHEST)
    with_cos = both[..., :channels].reshape(frames, 2, share, channels)
    with_sin = both[..., channels:].reshape(frames, 2, share, channels)
    spec_real = with_cos[:, 0] + with_sin[:, 1]
    spec_imag = with_cos[:, 1] - with_sin[:, 0]

    taps = jnp.pad(dish_filter, ((0, 0), (0, 0), (0, extra), (0, 0)))
    taps = lax.dynamic_slice_in_dim(taps, position * share, share, 2)
    lead = ((fir_count - 1, 0), (0, 0), (0, 0))
    past_real, past_imag = jnp.pad(spec_real, lead), jnp.pad(spec_imag, lead)
    out_real = jnp.zeros_like(spec_real)
    out_imag = jnp.zeros_like(spec_imag)
    for tap_index in range(fir_count):
        offset = fir_count - 1 - tap_index
        part_real = past_real[offset : offset + frames]
        part_imag = past_imag[offset : offset + frames]
        factor_real, factor_imag = taps[0, tap_index], taps[1, tap_index]
        out_real = out_real + factor_real * part_real - factor_imag * part_imag
        out_imag = out_imag + factor_real * part_imag + factor_imag * part_real

    filtered = jnp.stack([out_real, out_imag])
    filtered = filtered.reshape(2, frames, share, bands, band_chans)
    filtered = jnp.transpose(filtered, (3, 0, 2, 4, 1)).reshape(
        bands, 2 * share, band_chans * frames
    )
    filtered = jnp.repeat(filtered, owners, axis=0)
    field = lax.all_to_all(filtered, "band", split_axis=0, concat_axis=0, tiled=True)
    field = field.reshape(devices, 2, share, band_chans, frames)
    field = jnp.transpose(field, (1, 0, 2, 3, 4))
    field = field.reshape(2, devices * share, band_chans, frames)
    field = jnp.take(field, dish_order, axis=1)
    power = detect(beam_weights[0], field[0], field[1])
    return power[None]


def solution(mesh):
    devices = mesh.shape["band"]

    def body(samples, prototype, dish_filter, beam_weights, dish_order):
        channels = prototype.shape[1]
        close = (
            channels == LANES
            and beam_weights.shape[1] == 8
            and devices * 8 == channels
            and dish_filter.shape[2] == 12 * devices
            and samples.shape[2] * devices == 32 * channels
        )
        chosen = close_body if close else wide_body
        return chosen(samples, prototype, dish_filter, beam_weights, dish_order)

    placed = (P(None, None, ("grp", "band")), P(), P(), P("band", None, None, None, None), P())
    return jax.shard_map(
        body,
        mesh=mesh,
        in_specs=placed,
        out_specs=P(("grp", "band"), None, None, None),
        check_vma=False,
    )
```

```python
import math

import jax
import jax.numpy as jnp
import numpy as np
from jax import lax
from jax.experimental import pallas as pl
from jax.experimental.pallas import tpu as pltpu
from jax.sharding import PartitionSpec as P

INTEG = 4
EARLY = 2
HIGHEST = lax.Precision.HIGHEST
F32 = jnp.float32
BF16 = jnp.bfloat16
LANES = 128
VMEM = pl.BlockSpec(memory_space=pltpu.VMEM)
HBM = pl.BlockSpec(memory_space=pltpu.HBM)
GRANT = pltpu.CompilerParams(vmem_limit_bytes=16 << 20)


def fourier_tables(length):
    counter = jnp.arange(length, dtype=jnp.int32)
    product = counter[:, None] * counter[None, :] % length
    angles = product.astype(jnp.float32) * (2.0 * math.pi / length)
    factor = 1.0 / math.sqrt(length)
    return (jnp.cos(angles) * factor, jnp.sin(angles) * factor)


held = pltpu.with_memory_space_constraint


def split(value):
    high = value.astype(BF16)
    return high, (value - high.astype(F32)).astype(BF16)


def share_row(part, dish):
    return part * 8 + dish if dish < 8 else 16 + part * 4 + dish - 8


def pieces_kernel(x_hbm, out_hbm, x_ref, out_ref, in_sems, out_sems):
    devices, frames_dev = out_ref.shape[:2]
    low = lax.broadcasted_iota(jnp.int32, (8, LANES), 0) < 4
    half = devices // 2
    loads, stores = [], []
    for part_of in range(2):
        begin = part_of * half
        ranges = [(begin * 8, half * 8), (devices * 8 + begin * 4, half * 4)]
        loads.append([])
        for index, (first, count) in enumerate(ranges):
            rows = slice(first, first + count)
            loads[-1].append(
                pltpu.make_async_copy(
                    x_hbm.at[:, rows], x_ref.at[:, rows], in_sems.at[part_of, index]
                )
            )
        devs = slice(begin, begin + half)
        stores.append(
            pltpu.make_async_copy(out_ref.at[devs], out_hbm.at[devs], out_sems.at[part_of])
        )
    for load in loads[0] + loads[1]:
        load.start()
    for part_of in range(2):
        for load in loads[part_of]:
            load.wait()
        for dev in range(part_of * half, (part_of + 1) * half, 2):
            rest = devices * 8 + dev * 4
            for frame in range(frames_dev):
                lanes = slice(frame * LANES, (frame + 1) * LANES)
                for one in (dev, dev + 1):
                    for part in range(2):
                        out_ref[one, frame, part * 8 : part * 8 + 8, :] = x_ref[
                            part, one * 8 : one * 8 + 8, lanes
                        ]
                real = x_ref[0, rest : rest + 8, lanes]
                imag = x_ref[1, rest : rest + 8, lanes]
                out_ref[dev, frame, 16:24, :] = jnp.where(low, real, pltpu.roll(imag, 4, 0))
                out_ref[dev + 1, frame, 16:24, :] = jnp.where(low, pltpu.roll(real, 4, 0), imag)
        stores[part_of].start()
    for store in stores:
        store.wait()


def weights_kernel(
    w_ref, order_ref, slot_ref, table_ref, early_ref, late_ref, table_out_ref, *scratch
):
    buffer, made, sems, table_sem = scratch
    table_copy = pltpu.make_async_copy(table_ref, table_out_ref, table_sem)
    loads = [
        pltpu.make_async_copy(w_ref.at[chan], buffer.at[chan], sems.at[0, chan])
        for chan in range(w_ref.shape[0])
    ]
    stores = [
        pltpu.make_async_copy(made.at[chan], late_ref.at[chan], sems.at[1, chan])
        for chan in range(late_ref.shape[0])
    ]
    ahead = 3
    for load in loads[:ahead]:
        load.start()
    hot = (slot_ref[...] == order_ref[...]).astype(F32).T.astype(BF16)
    beams = w_ref.shape[3]
    for chan, load in enumerate(loads):
        load.wait()
        if chan + ahead < len(loads):
            loads[chan + ahead].start()
        elif chan + ahead == len(loads):
            table_copy.start()
        for part in range(2):
            halves = [
                jnp.dot(half, hot, preferred_element_type=F32).astype(BF16)
                for half in split(buffer[chan, part].T)
            ]
            rows = slice(part * beams, (part + 1) * beams)
            both = jnp.concatenate(halves, axis=1)
            if chan < EARLY:
                early_ref[chan, rows, :] = both
            else:
                made[chan - EARLY, rows, :] = both
        if chan >= EARLY:
            stores[chan - EARLY].start()
    for store in stores:
        store.wait()
    table_copy.wait()


def channel_kernel(
    x_ref, proto_ref, table_ref, taps_ref, out_ref, past, poly, spec, filt
):
    pfb_count = proto_ref.shape[0]
    fir_count = taps_ref.shape[0]
    frames = poly.shape[0]
    group = 8
    low = lax.broadcasted_iota(jnp.int32, (group, 8, LANES), 1) < 4

    past[0 : pfb_count - 1] = jnp.zeros((pfb_count - 1, 24, LANES), F32)
    past[pfb_count - 1 :] = x_ref[...]

    spec[0 : fir_count - 1] = jnp.zeros((fir_count - 1, 24, 2 * LANES), F32)
    for first in range(0, frames, group):
        found = []
        for rows in range(0, 24, 8):
            total = None
            for tap in range(pfb_count):
                begin = first + pfb_count - 1 - tap
                block = past[begin : begin + group, rows : rows + 8, :]
                term = block * proto_ref[tap : tap + 1, :][None]
                total = term if total is None else total + term
            found.append(total)
        turned = pltpu.roll(found[2], 4, 1)
        other = [found[1], -found[0], jnp.where(low, turned, -turned)]
        for index in range(3):
            rows = slice(index * 8, index * 8 + 8)
            poly[first : first + group, rows, 0:LANES] = found[index]
            poly[first : first + group, rows, LANES : 2 * LANES] = other[index]

    for first in range(0, frames, group):
        value = poly[first : first + group].reshape(group * 24, 2 * LANES)
        high, rest = split(value)
        stacked = jnp.concatenate([high, rest, high], axis=1)
        product = jnp.dot(stacked, table_ref[...], preferred_element_type=F32)
        begin = first + fir_count - 1
        spec[begin : begin + group] = product.reshape(group, 24, 2 * LANES)

    for rows in range(0, 24, 8):
        for first in range(0, frames, group):
            total = None
            for tap in range(fir_count):
                begin = first + fir_count - 1 - tap
                near = spec[begin : begin + group, rows : rows + 8, 0:LANES]
                cross = spec[begin : begin + group, rows : rows + 8, LANES : 2 * LANES]
                term = taps_ref[tap, 0, rows : rows + 8, :][None] * near
                term = term + taps_ref[tap, 1, rows : rows + 8, :][None] * cross
                total = term if total is None else total + term
            for frame in range(group):
                begin = (first + frame) * 24 + rows
                filt[begin : begin + 8, :] = total[frame]

    per_band = out_ref.shape[1] // 6
    for pair in range(6):
        rows = [
            filt[pl.ds(share_row(part, pair * 2 + odd), frames, stride=24), :]
            for part in range(2)
            for odd in range(2)
        ]
        turned = jnp.concatenate(rows, axis=0).T
        for dev in range(out_ref.shape[0]):
            out_ref[dev, pair * per_band : (pair + 1) * per_band, :] = turned[
                dev * per_band : (dev + 1) * per_band
            ]


def beams_kernel(x_ref, early_ref, late_ref, out_ref):
    rows = x_ref.shape[0] // 8
    beams = early_ref.shape[1] // 2
    lane = lax.broadcasted_iota(jnp.int32, (rows, LANES), 1)
    even = lane % 64 < 32
    wide = lax.broadcasted_iota(jnp.int32, (beams, LANES), 1)
    even_wide = wide % 64 < 32
    row = lax.broadcasted_iota(jnp.int32, (16, 2 * LANES), 0)
    column = lax.broadcasted_iota(jnp.int32, (16, 2 * LANES), 1)
    pool = jnp.where(row == column % 64 // INTEG, 1.0 / INTEG, 0.0).astype(BF16)
    steps = range(out_ref.shape[0] // 2)
    fields = []
    for step in steps:
        one = x_ref[pl.ds(2 * step, rows, stride=8), :]
        two = x_ref[pl.ds(2 * step + 1, rows, stride=8), :]
        first = jnp.where(even, one, pltpu.roll(two, 32, 1))
        second = jnp.where(even, pltpu.roll(one, LANES - 32, 1), two)
        both = jnp.concatenate(split(jnp.concatenate([first, second], axis=0)), axis=1)
        fields.append(jnp.concatenate([both, both], axis=0))
    beam_of = []
    for step in steps:
        if 2 * step < EARLY:
            w_ref, begin = early_ref, 2 * step
        else:
            w_ref, begin = late_ref, 2 * step - EARLY
        sums = []
        for index in range(2):
            weights = w_ref[begin + index]
            product = jnp.dot(weights, fields[step], preferred_element_type=F32)
            sums.append(product[:, 0:LANES] + product[:, LANES : 2 * LANES])
        by_real = jnp.where(even_wide, sums[0][:beams], sums[1][:beams])
        by_imag = jnp.where(even_wide, sums[0][beams:], sums[1][beams:])
        crossed = pltpu.roll(by_imag, 64, 1)
        beam_of.append(by_real + jnp.where(wide < 64, -crossed, crossed))
    for step in steps:
        power = lax.dot_general(
            pool,
            jnp.concatenate(split(beam_of[step] * beam_of[step]), axis=1),
            (((1,), (1,)), ((), ())),
            preferred_element_type=F32,
        )
        out_ref[2 * step] = power[0:8]
        out_ref[2 * step + 1] = power[8:16]


def slots_of(devices):
    index = np.arange(devices * 12, dtype=np.int32)
    own = index % 6 * 2 + index // (devices * 6)
    source = index // 6 % devices
    dishes = np.where(own < 8, source * 8 + own, devices * 8 + source * 4 + own - 8)
    return dishes.astype(np.int32)[:, None]


def dft_parts(channels):
    index = np.arange(channels)
    angle = 2.0 * np.pi * (index[:, None] * index[None, :] % channels) / channels
    cosine = np.cos(angle) / np.sqrt(channels)
    sine = np.sin(angle) / np.sqrt(channels)
    table = np.block([[cosine, sine], [sine, -cosine]]).astype(np.float32)
    high = table.astype(jnp.bfloat16)
    rest = (table - high.astype(np.float32)).astype(jnp.bfloat16)
    return np.concatenate([high, high, rest], axis=0)


def close_body(samples, prototype, dish_filter, beam_weights, dish_order):
    devices = lax.axis_size("band")
    position = lax.axis_index("band")
    channels = prototype.shape[1]
    fir_count = dish_filter.shape[1]
    dishes = dish_filter.shape[2]
    band_chans = beam_weights.shape[1]
    beams = beam_weights.shape[4]
    frames_dev = samples.shape[2] // channels
    frames = frames_dev * devices

    def exchange(value):
        return lax.all_to_all(value, "band", split_axis=0, concat_axis=0, tiled=True)

    pieces = pl.pallas_call(
        pieces_kernel,
        out_shape=pltpu.HBM((devices, frames_dev, 24, channels), F32),
        in_specs=[HBM],
        out_specs=HBM,
        scratch_shapes=[
            pltpu.VMEM(samples.shape, F32),
            pltpu.VMEM((devices, frames_dev, 24, channels), F32),
            pltpu.SemaphoreType.DMA((2, 2)),
            pltpu.SemaphoreType.DMA((2,)),
        ],
        name="pieces",
        compiler_params=GRANT,
    )(held(samples, pltpu.HBM))
    arrived = exchange(pieces).reshape(frames, 24, channels)

    eight = lax.dynamic_slice_in_dim(dish_filter, position * 8, 8, 2)
    four = lax.dynamic_slice_in_dim(dish_filter, devices * 8 + position * 4, 4, 2)
    taps = jnp.concatenate([eight, eight, four, four], axis=2)
    taps = jnp.transpose(taps, (1, 0, 2, 3))
    table = dft_parts(channels)
    early, late, table = pl.pallas_call(
        weights_kernel,
        out_shape=[
            jax.ShapeDtypeStruct((EARLY, 2 * beams, 2 * dishes), BF16),
            pltpu.HBM((band_chans - EARLY, 2 * beams, 2 * dishes), BF16),
            jax.ShapeDtypeStruct(table.shape, BF16),
        ],
        in_specs=[HBM, VMEM, VMEM, HBM],
        out_specs=[VMEM, HBM, VMEM],
        scratch_shapes=[
            pltpu.VMEM((band_chans, 2, dishes, beams), F32),
            pltpu.VMEM((band_chans - EARLY, 2 * beams, 2 * dishes), BF16),
            pltpu.SemaphoreType.DMA((2, band_chans)),
            pltpu.SemaphoreType.DMA(()),
        ],
        name="weights",
        compiler_params=GRANT,
        cost_estimate=pl.CostEstimate(
            flops=8 * 4 * 2 * 192 * 192 * 384, bytes_accessed=5 << 20, transcendentals=0
        ),
    )(
        held(beam_weights[0], pltpu.HBM),
        dish_order.reshape(1, dishes),
        slots_of(devices),
        held(jnp.asarray(table), pltpu.HBM),
    )
    arrived, early, late, table = lax.optimization_barrier((arrived, early, late, table))

    block = (6 * band_chans, channels)
    filtered = pl.pallas_call(
        channel_kernel,
        out_shape=jax.ShapeDtypeStruct((devices,) + block, F32),
        in_specs=[VMEM] * 4,
        out_specs=VMEM,
        scratch_shapes=[
            pltpu.VMEM((frames + prototype.shape[0] - 1, 24, LANES), F32),
            pltpu.VMEM((frames, 24, 2 * LANES), F32),
            pltpu.VMEM((frames + fir_count - 1, 24, 2 * LANES), F32),
            pltpu.VMEM((frames * 24, LANES), F32),
        ],
        name="channels",
        compiler_params=GRANT,
    )(held(arrived, pltpu.VMEM), prototype, held(table, pltpu.VMEM), taps)
    field = exchange(filtered).reshape(devices * 6 * band_chans, channels)

    power = pl.pallas_call(
        beams_kernel,
        out_shape=jax.ShapeDtypeStruct((band_chans, frames // INTEG, beams), F32),
        in_specs=[VMEM] * 3,
        out_specs=VMEM,
        name="beams",
        compiler_params=GRANT,
    )(held(field, pltpu.VMEM), held(early, pltpu.VMEM), late)
    return jnp.transpose(power, (0, 2, 1))[None]


def detect(weights, field_real, field_imag):
    def contract(weight_part, field_part):
        return jnp.einsum("qds,dqf->qsf", weight_part, field_part, precision=HIGHEST)

    beam_real = contract(weights[:, 0], field_real) - contract(weights[:, 1], field_imag)
    beam_imag = contract(weights[:, 0], field_imag) + contract(weights[:, 1], field_real)
    energy = beam_real * beam_real + beam_imag * beam_imag
    shaped = energy.reshape(energy.shape[:-1] + (energy.shape[-1] // INTEG, INTEG))
    return jnp.mean(shaped, axis=-1)


def wide_body(samples, prototype, dish_filter, beam_weights, dish_order):
    devices = lax.axis_size("band")
    position = lax.axis_index("band")
    pfb_count, channels = prototype.shape
    fir_count = dish_filter.shape[1]
    dishes = dish_filter.shape[2]
    band_chans = beam_weights.shape[1]
    bands = channels // band_chans
    owners = devices // bands
    frames_dev = samples.shape[2] // channels
    frames = frames_dev * devices
    share = -(-dishes // devices)
    extra = share * devices - dishes

    padded = jnp.pad(samples, ((0, 0), (0, extra), (0, 0)))
    pieces = padded.reshape(2, devices, share, frames_dev, channels)
    pieces = jnp.transpose(pieces, (1, 3, 0, 2, 4)).reshape(
        devices, frames_dev, 2 * share, channels
    )
    arrived = lax.all_to_all(pieces, "band", split_axis=0, concat_axis=0, tiled=True)
    blocks = arrived.reshape(frames, 2 * share, channels)

    history = jnp.pad(blocks, ((pfb_count - 1, 0), (0, 0), (0, 0)))
    polyphase = jnp.zeros_like(blocks)
    for tap_index in range(pfb_count):
        offset = pfb_count - 1 - tap_index
        polyphase = polyphase + prototype[tap_index] * history[offset : offset + frames]
    cosine, sine = fourier_tables(channels)
    both = jnp.dot(polyphase, jnp.concatenate([cosine, sine], axis=1), precision=HIGHEST)
    with_cos = both[..., :channels].reshape(frames, 2, share, channels)
    with_sin = both[..., channels:].reshape(frames, 2, share, channels)
    spec_real = with_cos[:, 0] + with_sin[:, 1]
    spec_imag = with_cos[:, 1] - with_sin[:, 0]

    taps = jnp.pad(dish_filter, ((0, 0), (0, 0), (0, extra), (0, 0)))
    taps = lax.dynamic_slice_in_dim(taps, position * share, share, 2)
    lead = ((fir_count - 1, 0), (0, 0), (0, 0))
    past_real, past_imag = jnp.pad(spec_real, lead), jnp.pad(spec_imag, lead)
    out_real = jnp.zeros_like(spec_real)
    out_imag = jnp.zeros_like(spec_imag)
    for tap_index in range(fir_count):
        offset = fir_count - 1 - tap_index
        part_real = past_real[offset : offset + frames]
        part_imag = past_imag[offset : offset + frames]
        factor_real, factor_imag = taps[0, tap_index], taps[1, tap_index]
        out_real = out_real + factor_real * part_real - factor_imag * part_imag
        out_imag = out_imag + factor_real * part_imag + factor_imag * part_real

    filtered = jnp.stack([out_real, out_imag])
    filtered = filtered.reshape(2, frames, share, bands, band_chans)
    filtered = jnp.transpose(filtered, (3, 0, 2, 4, 1)).reshape(
        bands, 2 * share, band_chans * frames
    )
    filtered = jnp.repeat(filtered, owners, axis=0)
    field = lax.all_to_all(filtered, "band", split_axis=0, concat_axis=0, tiled=True)
    field = field.reshape(devices, 2, share, band_chans, frames)
    field = jnp.transpose(field, (1, 0, 2, 3, 4))
    field = field.reshape(2, devices * share, band_chans, frames)
    field = jnp.take(field, dish_order, axis=1)
    power = detect(beam_weights[0], field[0], field[1])
    return power[None]


def solution(mesh):
    devices = mesh.shape["band"]

    def body(samples, prototype, dish_filter, beam_weights, dish_order):
        channels = prototype.shape[1]
        close = (
            channels == LANES
            and beam_weights.shape[1] == 8
            and devices * 8 == channels
            and dish_filter.shape[2] == 12 * devices
            and samples.shape[2] * devices == 32 * channels
        )
        chosen = close_body if close else wide_body
        return chosen(samples, prototype, dish_filter, beam_weights, dish_order)

    placed = (P(None, None, ("grp", "band")), P(), P(), P("band", None, None, None, None), P())
    return jax.shard_map(
        body,
        mesh=mesh,
        in_specs=placed,
        out_specs=P(("grp", "band"), None, None, None),
        check_vma=False,
    )
```

```python
import math

import jax
import jax.numpy as jnp
import numpy as np
from jax import lax
from jax.experimental import pallas as pl
from jax.experimental.pallas import tpu as pltpu
from jax.sharding import PartitionSpec as P

INTEG = 4
HIGHEST = lax.Precision.HIGHEST
F32 = jnp.float32
BF16 = jnp.bfloat16
LANES = 128
VMEM = pl.BlockSpec(memory_space=pltpu.VMEM)
HBM = pl.BlockSpec(memory_space=pltpu.HBM)
GRANT = pltpu.CompilerParams(vmem_limit_bytes=16 << 20)


def fourier_tables(length):
    counter = jnp.arange(length, dtype=jnp.int32)
    product = counter[:, None] * counter[None, :] % length
    angles = product.astype(jnp.float32) * (2.0 * math.pi / length)
    factor = 1.0 / math.sqrt(length)
    return (jnp.cos(angles) * factor, jnp.sin(angles) * factor)


held = pltpu.with_memory_space_constraint


def split(value):
    high = value.astype(BF16)
    return high, (value - high.astype(F32)).astype(BF16)


def share_row(part, dish):
    return part * 8 + dish if dish < 8 else 16 + part * 4 + dish - 8


def pieces_kernel(x_ref, out_ref):
    devices, frames_dev = out_ref.shape[:2]
    low = lax.broadcasted_iota(jnp.int32, (8, LANES), 0) < 4
    for frame in range(frames_dev):
        lanes = slice(frame * LANES, (frame + 1) * LANES)
        for dev in range(0, devices, 2):
            for one in (dev, dev + 1):
                for part in range(2):
                    out_ref[one, frame, part * 8 : part * 8 + 8, :] = x_ref[
                        part, one * 8 : one * 8 + 8, lanes
                    ]
            start = devices * 8 + dev * 4
            real = x_ref[0, start : start + 8, lanes]
            imag = x_ref[1, start : start + 8, lanes]
            out_ref[dev, frame, 16:24, :] = jnp.where(low, real, pltpu.roll(imag, 4, 0))
            out_ref[dev + 1, frame, 16:24, :] = jnp.where(low, pltpu.roll(real, 4, 0), imag)


def weights_kernel(
    w_ref, order_ref, slot_ref, table_ref, out_ref, table_out_ref, buffer, made, sems, table_sem
):
    table_copy = pltpu.make_async_copy(table_ref, table_out_ref, table_sem)
    loads = [
        pltpu.make_async_copy(w_ref.at[chan], buffer.at[chan], sems.at[0, chan])
        for chan in range(w_ref.shape[0])
    ]
    stores = [
        pltpu.make_async_copy(made.at[chan], out_ref.at[chan], sems.at[1, chan])
        for chan in range(w_ref.shape[0])
    ]
    ahead = 3
    for load in loads[:ahead]:
        load.start()
    hot = (slot_ref[...] == order_ref[...]).astype(F32).T.astype(BF16)
    beams = w_ref.shape[3]
    for chan, load in enumerate(loads):
        load.wait()
        if chan + ahead < len(loads):
            loads[chan + ahead].start()
        elif chan + ahead == len(loads):
            table_copy.start()
        for part in range(2):
            halves = [
                jnp.dot(half, hot, preferred_element_type=F32).astype(BF16)
                for half in split(buffer[chan, part].T)
            ]
            rows = slice(part * beams, (part + 1) * beams)
            made[chan, rows, :] = jnp.concatenate(halves, axis=1)
        stores[chan].start()
    for store in stores:
        store.wait()
    table_copy.wait()


def channel_kernel(
    x_ref, proto_ref, table_ref, taps_ref, out_ref, past, poly, spec, filt
):
    pfb_count = proto_ref.shape[0]
    fir_count = taps_ref.shape[0]
    frames = poly.shape[0]
    group = 8
    low = lax.broadcasted_iota(jnp.int32, (group, 8, LANES), 1) < 4

    past[0 : pfb_count - 1] = jnp.zeros((pfb_count - 1, 24, LANES), F32)
    past[pfb_count - 1 :] = x_ref[...]

    spec[0 : fir_count - 1] = jnp.zeros((fir_count - 1, 24, 2 * LANES), F32)
    for first in range(0, frames, group):
        found = []
        for rows in range(0, 24, 8):
            total = None
            for tap in range(pfb_count):
                begin = first + pfb_count - 1 - tap
                block = past[begin : begin + group, rows : rows + 8, :]
                term = block * proto_ref[tap : tap + 1, :][None]
                total = term if total is None else total + term
            found.append(total)
        turned = pltpu.roll(found[2], 4, 1)
        other = [found[1], -found[0], jnp.where(low, turned, -turned)]
        for index in range(3):
            rows = slice(index * 8, index * 8 + 8)
            poly[first : first + group, rows, 0:LANES] = found[index]
            poly[first : first + group, rows, LANES : 2 * LANES] = other[index]

    for first in range(0, frames, group):
        value = poly[first : first + group].reshape(group * 24, 2 * LANES)
        high, rest = split(value)
        stacked = jnp.concatenate([high, rest, high], axis=1)
        product = jnp.dot(stacked, table_ref[...], preferred_element_type=F32)
        begin = first + fir_count - 1
        spec[begin : begin + group] = product.reshape(group, 24, 2 * LANES)

    for rows in range(0, 24, 8):
        for first in range(0, frames, group):
            total = None
            for tap in range(fir_count):
                begin = first + fir_count - 1 - tap
                near = spec[begin : begin + group, rows : rows + 8, 0:LANES]
                cross = spec[begin : begin + group, rows : rows + 8, LANES : 2 * LANES]
                term = taps_ref[tap, 0, rows : rows + 8, :][None] * near
                term = term + taps_ref[tap, 1, rows : rows + 8, :][None] * cross
                total = term if total is None else total + term
            for frame in range(group):
                begin = (first + frame) * 24 + rows
                filt[begin : begin + 8, :] = total[frame]

    per_band = out_ref.shape[1] // 6
    for pair in range(6):
        rows = [
            filt[pl.ds(share_row(part, pair * 2 + odd), frames, stride=24), :]
            for part in range(2)
            for odd in range(2)
        ]
        turned = jnp.concatenate(rows, axis=0).T
        for dev in range(out_ref.shape[0]):
            out_ref[dev, pair * per_band : (pair + 1) * per_band, :] = turned[
                dev * per_band : (dev + 1) * per_band
            ]


def beams_kernel(x_ref, w_ref, out_ref):
    rows = x_ref.shape[0] // 8
    beams = w_ref.shape[1] // 2
    lane = lax.broadcasted_iota(jnp.int32, (rows, LANES), 1)
    even = lane % 64 < 32
    wide = lax.broadcasted_iota(jnp.int32, (beams, LANES), 1)
    even_wide = wide % 64 < 32
    row = lax.broadcasted_iota(jnp.int32, (16, 2 * LANES), 0)
    column = lax.broadcasted_iota(jnp.int32, (16, 2 * LANES), 1)
    pool = jnp.where(row == column % 64 // INTEG, 1.0 / INTEG, 0.0).astype(BF16)
    steps = range(out_ref.shape[0] // 2)
    fields = []
    for step in steps:
        one = x_ref[pl.ds(2 * step, rows, stride=8), :]
        two = x_ref[pl.ds(2 * step + 1, rows, stride=8), :]
        first = jnp.where(even, one, pltpu.roll(two, 32, 1))
        second = jnp.where(even, pltpu.roll(one, LANES - 32, 1), two)
        both = jnp.concatenate(split(jnp.concatenate([first, second], axis=0)), axis=1)
        fields.append(jnp.concatenate([both, both], axis=0))
    beam_of = []
    for step in steps:
        sums = []
        for index in range(2):
            product = jnp.dot(w_ref[2 * step + index], fields[step], preferred_element_type=F32)
            sums.append(product[:, 0:LANES] + product[:, LANES : 2 * LANES])
        by_real = jnp.where(even_wide, sums[0][:beams], sums[1][:beams])
        by_imag = jnp.where(even_wide, sums[0][beams:], sums[1][beams:])
        crossed = pltpu.roll(by_imag, 64, 1)
        beam_of.append(by_real + jnp.where(wide < 64, -crossed, crossed))
    for step in steps:
        power = lax.dot_general(
            pool,
            jnp.concatenate(split(beam_of[step] * beam_of[step]), axis=1),
            (((1,), (1,)), ((), ())),
            preferred_element_type=F32,
        )
        out_ref[2 * step] = power[0:8]
        out_ref[2 * step + 1] = power[8:16]


def slots_of(devices):
    index = np.arange(devices * 12, dtype=np.int32)
    own = index % 6 * 2 + index // (devices * 6)
    source = index // 6 % devices
    dishes = np.where(own < 8, source * 8 + own, devices * 8 + source * 4 + own - 8)
    return dishes.astype(np.int32)[:, None]


def dft_parts(channels):
    index = np.arange(channels)
    angle = 2.0 * np.pi * (index[:, None] * index[None, :] % channels) / channels
    cosine = np.cos(angle) / np.sqrt(channels)
    sine = np.sin(angle) / np.sqrt(channels)
    table = np.block([[cosine, sine], [sine, -cosine]]).astype(np.float32)
    high = table.astype(jnp.bfloat16)
    rest = (table - high.astype(np.float32)).astype(jnp.bfloat16)
    return np.concatenate([high, high, rest], axis=0)


def close_body(samples, prototype, dish_filter, beam_weights, dish_order):
    devices = lax.axis_size("band")
    position = lax.axis_index("band")
    channels = prototype.shape[1]
    fir_count = dish_filter.shape[1]
    dishes = dish_filter.shape[2]
    band_chans = beam_weights.shape[1]
    beams = beam_weights.shape[4]
    frames_dev = samples.shape[2] // channels
    frames = frames_dev * devices

    def exchange(value):
        return lax.all_to_all(value, "band", split_axis=0, concat_axis=0, tiled=True)

    pieces = pl.pallas_call(
        pieces_kernel,
        out_shape=jax.ShapeDtypeStruct((devices, frames_dev, 24, channels), F32),
        in_specs=[VMEM],
        out_specs=VMEM,
        name="pieces",
        compiler_params=GRANT,
    )(samples)
    arrived = exchange(pieces).reshape(frames, 24, channels)

    eight = lax.dynamic_slice_in_dim(dish_filter, position * 8, 8, 2)
    four = lax.dynamic_slice_in_dim(dish_filter, devices * 8 + position * 4, 4, 2)
    taps = jnp.concatenate([eight, eight, four, four], axis=2)
    taps = jnp.transpose(taps, (1, 0, 2, 3))
    table = dft_parts(channels)
    weights, table = pl.pallas_call(
        weights_kernel,
        out_shape=[
            pltpu.HBM((band_chans, 2 * beams, 2 * dishes), BF16),
            jax.ShapeDtypeStruct(table.shape, BF16),
        ],
        in_specs=[HBM, VMEM, VMEM, HBM],
        out_specs=[HBM, VMEM],
        scratch_shapes=[
            pltpu.VMEM((band_chans, 2, dishes, beams), F32),
            pltpu.VMEM((band_chans, 2 * beams, 2 * dishes), BF16),
            pltpu.SemaphoreType.DMA((2, band_chans)),
            pltpu.SemaphoreType.DMA(()),
        ],
        name="weights",
        compiler_params=GRANT,
        cost_estimate=pl.CostEstimate(
            flops=8 * 4 * 2 * 192 * 192 * 384, bytes_accessed=5 << 20, transcendentals=0
        ),
    )(
        held(beam_weights[0], pltpu.HBM),
        dish_order.reshape(1, dishes),
        slots_of(devices),
        held(jnp.asarray(table), pltpu.HBM),
    )
    arrived, weights, table = lax.optimization_barrier((arrived, weights, table))

    block = (6 * band_chans, channels)
    filtered = pl.pallas_call(
        channel_kernel,
        out_shape=jax.ShapeDtypeStruct((devices,) + block, F32),
        in_specs=[VMEM] * 4,
        out_specs=VMEM,
        scratch_shapes=[
            pltpu.VMEM((frames + prototype.shape[0] - 1, 24, LANES), F32),
            pltpu.VMEM((frames, 24, 2 * LANES), F32),
            pltpu.VMEM((frames + fir_count - 1, 24, 2 * LANES), F32),
            pltpu.VMEM((frames * 24, LANES), F32),
        ],
        name="channels",
        compiler_params=GRANT,
    )(held(arrived, pltpu.VMEM), prototype, held(table, pltpu.VMEM), taps)
    filtered, weights = lax.optimization_barrier((filtered, weights))
    field = exchange(filtered).reshape(devices * 6 * band_chans, channels)

    power = pl.pallas_call(
        beams_kernel,
        out_shape=jax.ShapeDtypeStruct((band_chans, frames // INTEG, beams), F32),
        in_specs=[VMEM] * 2,
        out_specs=VMEM,
        name="beams",
        compiler_params=GRANT,
    )(held(field, pltpu.VMEM), weights)
    return jnp.transpose(power, (0, 2, 1))[None]


def detect(weights, field_real, field_imag):
    def contract(weight_part, field_part):
        return jnp.einsum("qds,dqf->qsf", weight_part, field_part, precision=HIGHEST)

    beam_real = contract(weights[:, 0], field_real) - contract(weights[:, 1], field_imag)
    beam_imag = contract(weights[:, 0], field_imag) + contract(weights[:, 1], field_real)
    energy = beam_real * beam_real + beam_imag * beam_imag
    shaped = energy.reshape(energy.shape[:-1] + (energy.shape[-1] // INTEG, INTEG))
    return jnp.mean(shaped, axis=-1)


def wide_body(samples, prototype, dish_filter, beam_weights, dish_order):
    devices = lax.axis_size("band")
    position = lax.axis_index("band")
    pfb_count, channels = prototype.shape
    fir_count = dish_filter.shape[1]
    dishes = dish_filter.shape[2]
    band_chans = beam_weights.shape[1]
    bands = channels // band_chans
    owners = devices // bands
    frames_dev = samples.shape[2] // channels
    frames = frames_dev * devices
    share = -(-dishes // devices)
    extra = share * devices - dishes

    padded = jnp.pad(samples, ((0, 0), (0, extra), (0, 0)))
    pieces = padded.reshape(2, devices, share, frames_dev, channels)
    pieces = jnp.transpose(pieces, (1, 3, 0, 2, 4)).reshape(
        devices, frames_dev, 2 * share, channels
    )
    arrived = lax.all_to_all(pieces, "band", split_axis=0, concat_axis=0, tiled=True)
    blocks = arrived.reshape(frames, 2 * share, channels)

    history = jnp.pad(blocks, ((pfb_count - 1, 0), (0, 0), (0, 0)))
    polyphase = jnp.zeros_like(blocks)
    for tap_index in range(pfb_count):
        offset = pfb_count - 1 - tap_index
        polyphase = polyphase + prototype[tap_index] * history[offset : offset + frames]
    cosine, sine = fourier_tables(channels)
    both = jnp.dot(polyphase, jnp.concatenate([cosine, sine], axis=1), precision=HIGHEST)
    with_cos = both[..., :channels].reshape(frames, 2, share, channels)
    with_sin = both[..., channels:].reshape(frames, 2, share, channels)
    spec_real = with_cos[:, 0] + with_sin[:, 1]
    spec_imag = with_cos[:, 1] - with_sin[:, 0]

    taps = jnp.pad(dish_filter, ((0, 0), (0, 0), (0, extra), (0, 0)))
    taps = lax.dynamic_slice_in_dim(taps, position * share, share, 2)
    lead = ((fir_count - 1, 0), (0, 0), (0, 0))
    past_real, past_imag = jnp.pad(spec_real, lead), jnp.pad(spec_imag, lead)
    out_real = jnp.zeros_like(spec_real)
    out_imag = jnp.zeros_like(spec_imag)
    for tap_index in range(fir_count):
        offset = fir_count - 1 - tap_index
        part_real = past_real[offset : offset + frames]
        part_imag = past_imag[offset : offset + frames]
        factor_real, factor_imag = taps[0, tap_index], taps[1, tap_index]
        out_real = out_real + factor_real * part_real - factor_imag * part_imag
        out_imag = out_imag + factor_real * part_imag + factor_imag * part_real

    filtered = jnp.stack([out_real, out_imag])
    filtered = filtered.reshape(2, frames, share, bands, band_chans)
    filtered = jnp.transpose(filtered, (3, 0, 2, 4, 1)).reshape(
        bands, 2 * share, band_chans * frames
    )
    filtered = jnp.repeat(filtered, owners, axis=0)
    field = lax.all_to_all(filtered, "band", split_axis=0, concat_axis=0, tiled=True)
    field = field.reshape(devices, 2, share, band_chans, frames)
    field = jnp.transpose(field, (1, 0, 2, 3, 4))
    field = field.reshape(2, devices * share, band_chans, frames)
    field = jnp.take(field, dish_order, axis=1)
    power = detect(beam_weights[0], field[0], field[1])
    return power[None]


def solution(mesh):
    devices = mesh.shape["band"]

    def body(samples, prototype, dish_filter, beam_weights, dish_order):
        channels = prototype.shape[1]
        close = (
            channels == LANES
            and beam_weights.shape[1] == 8
            and devices * 8 == channels
            and dish_filter.shape[2] == 12 * devices
            and samples.shape[2] * devices == 32 * channels
        )
        chosen = close_body if close else wide_body
        return chosen(samples, prototype, dish_filter, beam_weights, dish_order)

    placed = (P(None, None, ("grp", "band")), P(), P(), P("band", None, None, None, None), P())
    return jax.shard_map(
        body,
        mesh=mesh,
        in_specs=placed,
        out_specs=P(("grp", "band"), None, None, None),
        check_vma=False,
    )
```

```python
import math

import jax
import jax.numpy as jnp
import numpy as np
from jax import lax
from jax.experimental import pallas as pl
from jax.experimental.pallas import tpu as pltpu
from jax.sharding import PartitionSpec as P

INTEG = 4
EARLY = 2
HIGHEST = lax.Precision.HIGHEST
F32 = jnp.float32
BF16 = jnp.bfloat16
LANES = 128
VMEM = pl.BlockSpec(memory_space=pltpu.VMEM)
HBM = pl.BlockSpec(memory_space=pltpu.HBM)
GRANT = pltpu.CompilerParams(vmem_limit_bytes=16 << 20)


def fourier_tables(length):
    counter = jnp.arange(length, dtype=jnp.int32)
    product = counter[:, None] * counter[None, :] % length
    angles = product.astype(jnp.float32) * (2.0 * math.pi / length)
    factor = 1.0 / math.sqrt(length)
    return (jnp.cos(angles) * factor, jnp.sin(angles) * factor)


held = pltpu.with_memory_space_constraint


def split(value):
    high = value.astype(BF16)
    return high, (value - high.astype(F32)).astype(BF16)


def share_row(part, dish):
    return part * 8 + dish if dish < 8 else 16 + part * 4 + dish - 8


def pieces_kernel(x_ref, out_ref):
    devices, frames_dev = out_ref.shape[:2]
    low = lax.broadcasted_iota(jnp.int32, (8, LANES), 0) < 4
    for frame in range(frames_dev):
        lanes = slice(frame * LANES, (frame + 1) * LANES)
        for dev in range(0, devices, 2):
            for one in (dev, dev + 1):
                for part in range(2):
                    out_ref[one, frame, part * 8 : part * 8 + 8, :] = x_ref[
                        part, one * 8 : one * 8 + 8, lanes
                    ]
            start = devices * 8 + dev * 4
            real = x_ref[0, start : start + 8, lanes]
            imag = x_ref[1, start : start + 8, lanes]
            out_ref[dev, frame, 16:24, :] = jnp.where(low, real, pltpu.roll(imag, 4, 0))
            out_ref[dev + 1, frame, 16:24, :] = jnp.where(low, pltpu.roll(real, 4, 0), imag)


def weights_kernel(
    w_ref, order_ref, slot_ref, table_ref, early_ref, late_ref, table_out_ref, *scratch
):
    buffer, made, sems, table_sem = scratch
    table_copy = pltpu.make_async_copy(table_ref, table_out_ref, table_sem)
    loads = [
        pltpu.make_async_copy(w_ref.at[chan], buffer.at[chan], sems.at[0, chan])
        for chan in range(w_ref.shape[0])
    ]
    stores = [
        pltpu.make_async_copy(made.at[chan], late_ref.at[chan], sems.at[1, chan])
        for chan in range(late_ref.shape[0])
    ]
    ahead = 3
    for load in loads[:ahead]:
        load.start()
    hot = (slot_ref[...] == order_ref[...]).astype(F32).T.astype(BF16)
    beams = w_ref.shape[3]
    for chan, load in enumerate(loads):
        load.wait()
        if chan + ahead < len(loads):
            loads[chan + ahead].start()
        elif chan + ahead == len(loads):
            table_copy.start()
        for part in range(2):
            halves = [
                jnp.dot(half, hot, preferred_element_type=F32).astype(BF16)
                for half in split(buffer[chan, part].T)
            ]
            rows = slice(part * beams, (part + 1) * beams)
            both = jnp.concatenate(halves, axis=1)
            if chan < EARLY:
                early_ref[chan, rows, :] = both
            else:
                made[chan - EARLY, rows, :] = both
        if chan >= EARLY:
            stores[chan - EARLY].start()
    for store in stores:
        store.wait()
    table_copy.wait()


def channel_kernel(
    x_ref, proto_ref, table_ref, taps_ref, late_ref, out_ref, late_out_ref, *scratch
):
    past, poly, spec, filt, late_sem = scratch
    late_copy = pltpu.make_async_copy(late_ref, late_out_ref, late_sem)
    late_copy.start()
    pfb_count = proto_ref.shape[0]
    fir_count = taps_ref.shape[0]
    frames = poly.shape[0]
    group = 8
    low = lax.broadcasted_iota(jnp.int32, (group, 8, LANES), 1) < 4

    past[0 : pfb_count - 1] = jnp.zeros((pfb_count - 1, 24, LANES), F32)
    past[pfb_count - 1 :] = x_ref[...]

    spec[0 : fir_count - 1] = jnp.zeros((fir_count - 1, 24, 2 * LANES), F32)
    for first in range(0, frames, group):
        found = []
        for rows in range(0, 24, 8):
            total = None
            for tap in range(pfb_count):
                begin = first + pfb_count - 1 - tap
                block = past[begin : begin + group, rows : rows + 8, :]
                term = block * proto_ref[tap : tap + 1, :][None]
                total = term if total is None else total + term
            found.append(total)
        turned = pltpu.roll(found[2], 4, 1)
        other = [found[1], -found[0], jnp.where(low, turned, -turned)]
        for index in range(3):
            rows = slice(index * 8, index * 8 + 8)
            poly[first : first + group, rows, 0:LANES] = found[index]
            poly[first : first + group, rows, LANES : 2 * LANES] = other[index]

    for first in range(0, frames, group):
        value = poly[first : first + group].reshape(group * 24, 2 * LANES)
        high, rest = split(value)
        stacked = jnp.concatenate([high, rest, high], axis=1)
        product = jnp.dot(stacked, table_ref[...], preferred_element_type=F32)
        begin = first + fir_count - 1
        spec[begin : begin + group] = product.reshape(group, 24, 2 * LANES)

    for rows in range(0, 24, 8):
        for first in range(0, frames, group):
            total = None
            for tap in range(fir_count):
                begin = first + fir_count - 1 - tap
                near = spec[begin : begin + group, rows : rows + 8, 0:LANES]
                cross = spec[begin : begin + group, rows : rows + 8, LANES : 2 * LANES]
                term = taps_ref[tap, 0, rows : rows + 8, :][None] * near
                term = term + taps_ref[tap, 1, rows : rows + 8, :][None] * cross
                total = term if total is None else total + term
            for frame in range(group):
                begin = (first + frame) * 24 + rows
                filt[begin : begin + 8, :] = total[frame]

    per_band = out_ref.shape[1] // 6
    for pair in range(6):
        rows = [
            filt[pl.ds(share_row(part, pair * 2 + odd), frames, stride=24), :]
            for part in range(2)
            for odd in range(2)
        ]
        turned = jnp.concatenate(rows, axis=0).T
        for dev in range(out_ref.shape[0]):
            out_ref[dev, pair * per_band : (pair + 1) * per_band, :] = turned[
                dev * per_band : (dev + 1) * per_band
            ]
    late_copy.wait()


def beams_kernel(x_ref, early_ref, late_ref, out_ref):
    rows = x_ref.shape[0] // 8
    beams = early_ref.shape[1] // 2
    lane = lax.broadcasted_iota(jnp.int32, (rows, LANES), 1)
    even = lane % 64 < 32
    wide = lax.broadcasted_iota(jnp.int32, (beams, LANES), 1)
    even_wide = wide % 64 < 32
    row = lax.broadcasted_iota(jnp.int32, (16, 2 * LANES), 0)
    column = lax.broadcasted_iota(jnp.int32, (16, 2 * LANES), 1)
    pool = jnp.where(row == column % 64 // INTEG, 1.0 / INTEG, 0.0).astype(BF16)
    steps = range(out_ref.shape[0] // 2)
    fields = []
    for step in steps:
        one = x_ref[pl.ds(2 * step, rows, stride=8), :]
        two = x_ref[pl.ds(2 * step + 1, rows, stride=8), :]
        first = jnp.where(even, one, pltpu.roll(two, 32, 1))
        second = jnp.where(even, pltpu.roll(one, LANES - 32, 1), two)
        both = jnp.concatenate(split(jnp.concatenate([first, second], axis=0)), axis=1)
        fields.append(jnp.concatenate([both, both], axis=0))
    beam_of = []
    for step in steps:
        if 2 * step < EARLY:
            w_ref, begin = early_ref, 2 * step
        else:
            w_ref, begin = late_ref, 2 * step - EARLY
        sums = []
        for index in range(2):
            weights = w_ref[begin + index]
            product = jnp.dot(weights, fields[step], preferred_element_type=F32)
            sums.append(product[:, 0:LANES] + product[:, LANES : 2 * LANES])
        by_real = jnp.where(even_wide, sums[0][:beams], sums[1][:beams])
        by_imag = jnp.where(even_wide, sums[0][beams:], sums[1][beams:])
        crossed = pltpu.roll(by_imag, 64, 1)
        beam_of.append(by_real + jnp.where(wide < 64, -crossed, crossed))
    for step in steps:
        power = lax.dot_general(
            pool,
            jnp.concatenate(split(beam_of[step] * beam_of[step]), axis=1),
            (((1,), (1,)), ((), ())),
            preferred_element_type=F32,
        )
        out_ref[2 * step] = power[0:8]
        out_ref[2 * step + 1] = power[8:16]


def slots_of(devices):
    index = np.arange(devices * 12, dtype=np.int32)
    own = index % 6 * 2 + index // (devices * 6)
    source = index // 6 % devices
    dishes = np.where(own < 8, source * 8 + own, devices * 8 + source * 4 + own - 8)
    return dishes.astype(np.int32)[:, None]


def dft_parts(channels):
    index = np.arange(channels)
    angle = 2.0 * np.pi * (index[:, None] * index[None, :] % channels) / channels
    cosine = np.cos(angle) / np.sqrt(channels)
    sine = np.sin(angle) / np.sqrt(channels)
    table = np.block([[cosine, sine], [sine, -cosine]]).astype(np.float32)
    high = table.astype(jnp.bfloat16)
    rest = (table - high.astype(np.float32)).astype(jnp.bfloat16)
    return np.concatenate([high, high, rest], axis=0)


def close_body(samples, prototype, dish_filter, beam_weights, dish_order):
    devices = lax.axis_size("band")
    position = lax.axis_index("band")
    channels = prototype.shape[1]
    fir_count = dish_filter.shape[1]
    dishes = dish_filter.shape[2]
    band_chans = beam_weights.shape[1]
    beams = beam_weights.shape[4]
    frames_dev = samples.shape[2] // channels
    frames = frames_dev * devices

    def exchange(value):
        return lax.all_to_all(value, "band", split_axis=0, concat_axis=0, tiled=True)

    pieces = pl.pallas_call(
        pieces_kernel,
        out_shape=jax.ShapeDtypeStruct((devices, frames_dev, 24, channels), F32),
        in_specs=[VMEM],
        out_specs=VMEM,
        name="pieces",
        compiler_params=GRANT,
    )(samples)
    arrived = exchange(pieces).reshape(frames, 24, channels)

    eight = lax.dynamic_slice_in_dim(dish_filter, position * 8, 8, 2)
    four = lax.dynamic_slice_in_dim(dish_filter, devices * 8 + position * 4, 4, 2)
    taps = jnp.concatenate([eight, eight, four, four], axis=2)
    taps = jnp.transpose(taps, (1, 0, 2, 3))
    table = dft_parts(channels)
    early, late, table = pl.pallas_call(
        weights_kernel,
        out_shape=[
            jax.ShapeDtypeStruct((EARLY, 2 * beams, 2 * dishes), BF16),
            pltpu.HBM((band_chans - EARLY, 2 * beams, 2 * dishes), BF16),
            jax.ShapeDtypeStruct(table.shape, BF16),
        ],
        in_specs=[HBM, VMEM, VMEM, HBM],
        out_specs=[VMEM, HBM, VMEM],
        scratch_shapes=[
            pltpu.VMEM((band_chans, 2, dishes, beams), F32),
            pltpu.VMEM((band_chans - EARLY, 2 * beams, 2 * dishes), BF16),
            pltpu.SemaphoreType.DMA((2, band_chans)),
            pltpu.SemaphoreType.DMA(()),
        ],
        name="weights",
        compiler_params=GRANT,
        cost_estimate=pl.CostEstimate(
            flops=8 * 4 * 2 * 192 * 192 * 384, bytes_accessed=5 << 20, transcendentals=0
        ),
    )(
        held(beam_weights[0], pltpu.HBM),
        dish_order.reshape(1, dishes),
        slots_of(devices),
        held(jnp.asarray(table), pltpu.HBM),
    )
    arrived, early, late, table = lax.optimization_barrier((arrived, early, late, table))

    block = (6 * band_chans, channels)
    filtered, late = pl.pallas_call(
        channel_kernel,
        out_shape=[
            jax.ShapeDtypeStruct((devices,) + block, F32),
            jax.ShapeDtypeStruct(late.shape, BF16),
        ],
        in_specs=[VMEM] * 4 + [HBM],
        out_specs=[VMEM] * 2,
        scratch_shapes=[
            pltpu.VMEM((frames + prototype.shape[0] - 1, 24, LANES), F32),
            pltpu.VMEM((frames, 24, 2 * LANES), F32),
            pltpu.VMEM((frames + fir_count - 1, 24, 2 * LANES), F32),
            pltpu.VMEM((frames * 24, LANES), F32),
            pltpu.SemaphoreType.DMA(()),
        ],
        name="channels",
        compiler_params=GRANT,
    )(
        held(arrived, pltpu.VMEM),
        prototype,
        held(table, pltpu.VMEM),
        taps,
        held(late, pltpu.HBM),
    )
    field = exchange(filtered).reshape(devices * 6 * band_chans, channels)

    power = pl.pallas_call(
        beams_kernel,
        out_shape=jax.ShapeDtypeStruct((band_chans, frames // INTEG, beams), F32),
        in_specs=[VMEM] * 3,
        out_specs=VMEM,
        name="beams",
        compiler_params=GRANT,
    )(held(field, pltpu.VMEM), held(early, pltpu.VMEM), held(late, pltpu.VMEM))
    return jnp.transpose(power, (0, 2, 1))[None]


def detect(weights, field_real, field_imag):
    def contract(weight_part, field_part):
        return jnp.einsum("qds,dqf->qsf", weight_part, field_part, precision=HIGHEST)

    beam_real = contract(weights[:, 0], field_real) - contract(weights[:, 1], field_imag)
    beam_imag = contract(weights[:, 0], field_imag) + contract(weights[:, 1], field_real)
    energy = beam_real * beam_real + beam_imag * beam_imag
    shaped = energy.reshape(energy.shape[:-1] + (energy.shape[-1] // INTEG, INTEG))
    return jnp.mean(shaped, axis=-1)


def wide_body(samples, prototype, dish_filter, beam_weights, dish_order):
    devices = lax.axis_size("band")
    position = lax.axis_index("band")
    pfb_count, channels = prototype.shape
    fir_count = dish_filter.shape[1]
    dishes = dish_filter.shape[2]
    band_chans = beam_weights.shape[1]
    bands = channels // band_chans
    owners = devices // bands
    frames_dev = samples.shape[2] // channels
    frames = frames_dev * devices
    share = -(-dishes // devices)
    extra = share * devices - dishes

    padded = jnp.pad(samples, ((0, 0), (0, extra), (0, 0)))
    pieces = padded.reshape(2, devices, share, frames_dev, channels)
    pieces = jnp.transpose(pieces, (1, 3, 0, 2, 4)).reshape(
        devices, frames_dev, 2 * share, channels
    )
    arrived = lax.all_to_all(pieces, "band", split_axis=0, concat_axis=0, tiled=True)
    blocks = arrived.reshape(frames, 2 * share, channels)

    history = jnp.pad(blocks, ((pfb_count - 1, 0), (0, 0), (0, 0)))
    polyphase = jnp.zeros_like(blocks)
    for tap_index in range(pfb_count):
        offset = pfb_count - 1 - tap_index
        polyphase = polyphase + prototype[tap_index] * history[offset : offset + frames]
    cosine, sine = fourier_tables(channels)
    both = jnp.dot(polyphase, jnp.concatenate([cosine, sine], axis=1), precision=HIGHEST)
    with_cos = both[..., :channels].reshape(frames, 2, share, channels)
    with_sin = both[..., channels:].reshape(frames, 2, share, channels)
    spec_real = with_cos[:, 0] + with_sin[:, 1]
    spec_imag = with_cos[:, 1] - with_sin[:, 0]

    taps = jnp.pad(dish_filter, ((0, 0), (0, 0), (0, extra), (0, 0)))
    taps = lax.dynamic_slice_in_dim(taps, position * share, share, 2)
    lead = ((fir_count - 1, 0), (0, 0), (0, 0))
    past_real, past_imag = jnp.pad(spec_real, lead), jnp.pad(spec_imag, lead)
    out_real = jnp.zeros_like(spec_real)
    out_imag = jnp.zeros_like(spec_imag)
    for tap_index in range(fir_count):
        offset = fir_count - 1 - tap_index
        part_real = past_real[offset : offset + frames]
        part_imag = past_imag[offset : offset + frames]
        factor_real, factor_imag = taps[0, tap_index], taps[1, tap_index]
        out_real = out_real + factor_real * part_real - factor_imag * part_imag
        out_imag = out_imag + factor_real * part_imag + factor_imag * part_real

    filtered = jnp.stack([out_real, out_imag])
    filtered = filtered.reshape(2, frames, share, bands, band_chans)
    filtered = jnp.transpose(filtered, (3, 0, 2, 4, 1)).reshape(
        bands, 2 * share, band_chans * frames
    )
    filtered = jnp.repeat(filtered, owners, axis=0)
    field = lax.all_to_all(filtered, "band", split_axis=0, concat_axis=0, tiled=True)
    field = field.reshape(devices, 2, share, band_chans, frames)
    field = jnp.transpose(field, (1, 0, 2, 3, 4))
    field = field.reshape(2, devices * share, band_chans, frames)
    field = jnp.take(field, dish_order, axis=1)
    power = detect(beam_weights[0], field[0], field[1])
    return power[None]


def solution(mesh):
    devices = mesh.shape["band"]

    def body(samples, prototype, dish_filter, beam_weights, dish_order):
        channels = prototype.shape[1]
        close = (
            channels == LANES
            and beam_weights.shape[1] == 8
            and devices * 8 == channels
            and dish_filter.shape[2] == 12 * devices
            and samples.shape[2] * devices == 32 * channels
        )
        chosen = close_body if close else wide_body
        return chosen(samples, prototype, dish_filter, beam_weights, dish_order)

    placed = (P(None, None, ("grp", "band")), P(), P(), P("band", None, None, None, None), P())
    return jax.shard_map(
        body,
        mesh=mesh,
        in_specs=placed,
        out_specs=P(("grp", "band"), None, None, None),
        check_vma=False,
    )
```

```python
import math

import jax
import jax.numpy as jnp
import numpy as np
from jax import lax
from jax.experimental import pallas as pl
from jax.experimental.pallas import tpu as pltpu
from jax.sharding import PartitionSpec as P

INTEG = 4
EARLY = 2
HIGHEST = lax.Precision.HIGHEST
F32 = jnp.float32
BF16 = jnp.bfloat16
LANES = 128
VMEM = pl.BlockSpec(memory_space=pltpu.VMEM)
HBM = pl.BlockSpec(memory_space=pltpu.HBM)
GRANT = pltpu.CompilerParams(vmem_limit_bytes=16 << 20)


def fourier_tables(length):
    counter = jnp.arange(length, dtype=jnp.int32)
    product = counter[:, None] * counter[None, :] % length
    angles = product.astype(jnp.float32) * (2.0 * math.pi / length)
    factor = 1.0 / math.sqrt(length)
    return (jnp.cos(angles) * factor, jnp.sin(angles) * factor)


held = pltpu.with_memory_space_constraint


def split(value):
    high = value.astype(BF16)
    return high, (value - high.astype(F32)).astype(BF16)


def share_row(part, dish):
    return part * 8 + dish if dish < 8 else 16 + part * 4 + dish - 8


def pieces_kernel(x_ref, out_ref):
    devices, frames_dev = out_ref.shape[:2]
    low = lax.broadcasted_iota(jnp.int32, (8, LANES), 0) < 4
    for frame in range(frames_dev):
        lanes = slice(frame * LANES, (frame + 1) * LANES)
        for dev in range(0, devices, 2):
            for one in (dev, dev + 1):
                for part in range(2):
                    out_ref[one, frame, part * 8 : part * 8 + 8, :] = x_ref[
                        part, one * 8 : one * 8 + 8, lanes
                    ]
            start = devices * 8 + dev * 4
            real = x_ref[0, start : start + 8, lanes]
            imag = x_ref[1, start : start + 8, lanes]
            out_ref[dev, frame, 16:24, :] = jnp.where(low, real, pltpu.roll(imag, 4, 0))
            out_ref[dev + 1, frame, 16:24, :] = jnp.where(low, pltpu.roll(real, 4, 0), imag)


def weights_kernel(
    w_ref, order_ref, slot_ref, early_ref, late_ref, buffer, made, sems
):
    loads = [
        pltpu.make_async_copy(w_ref.at[chan], buffer.at[chan], sems.at[0, chan])
        for chan in range(w_ref.shape[0])
    ]
    stores = [
        pltpu.make_async_copy(made.at[chan], late_ref.at[chan], sems.at[1, chan])
        for chan in range(late_ref.shape[0])
    ]
    ahead = 3
    for load in loads[:ahead]:
        load.start()
    hot = (slot_ref[...] == order_ref[...]).astype(F32).T.astype(BF16)
    beams = w_ref.shape[3]
    for chan, load in enumerate(loads):
        load.wait()
        if chan + ahead < len(loads):
            loads[chan + ahead].start()
        for part in range(2):
            halves = [
                jnp.dot(half, hot, preferred_element_type=F32).astype(BF16)
                for half in split(buffer[chan, part].T)
            ]
            rows = slice(part * beams, (part + 1) * beams)
            both = jnp.concatenate(halves, axis=1)
            if chan < EARLY:
                early_ref[chan, rows, :] = both
            else:
                made[chan - EARLY, rows, :] = both
        if chan >= EARLY:
            stores[chan - EARLY].start()
    for store in stores:
        store.wait()


def channel_kernel(
    x_ref, proto_ref, table_hbm, taps_hbm, late_ref, out_ref, late_out_ref, *scratch
):
    past, poly, spec, filt, table_ref, taps_ref, sems = scratch
    place = lax.axis_index("band")
    devices = out_ref.shape[0]
    eight = pl.ds(pl.multiple_of(place * 8, 8), 8)
    pair_rows = pl.ds(pl.multiple_of(devices * 8 + place // 2 * 8, 8), 8)
    loads = [
        pltpu.make_async_copy(taps_hbm.at[:, :, eight, :], taps_ref.at[:, :, 0:8], sems.at[0]),
        pltpu.make_async_copy(taps_hbm.at[:, :, pair_rows, :], taps_ref.at[:, :, 8:16], sems.at[1]),
        pltpu.make_async_copy(table_hbm, table_ref, sems.at[2]),
    ]
    for load in loads:
        load.start()
    late_copy = pltpu.make_async_copy(late_ref, late_out_ref, sems.at[3])
    late_copy.start()
    pfb_count = proto_ref.shape[0]
    fir_count = taps_ref.shape[1]
    frames = poly.shape[0]
    group = 8
    low = lax.broadcasted_iota(jnp.int32, (group, 8, LANES), 1) < 4

    past[0 : pfb_count - 1] = jnp.zeros((pfb_count - 1, 24, LANES), F32)
    past[pfb_count - 1 :] = x_ref[...]

    spec[0 : fir_count - 1] = jnp.zeros((fir_count - 1, 24, 2 * LANES), F32)
    for first in range(0, frames, group):
        found = []
        for rows in range(0, 24, 8):
            total = None
            for tap in range(pfb_count):
                begin = first + pfb_count - 1 - tap
                block = past[begin : begin + group, rows : rows + 8, :]
                term = block * proto_ref[tap : tap + 1, :][None]
                total = term if total is None else total + term
            found.append(total)
        turned = pltpu.roll(found[2], 4, 1)
        other = [found[1], -found[0], jnp.where(low, turned, -turned)]
        for index in range(3):
            rows = slice(index * 8, index * 8 + 8)
            poly[first : first + group, rows, 0:LANES] = found[index]
            poly[first : first + group, rows, LANES : 2 * LANES] = other[index]

    for load in loads:
        load.wait()

    for first in range(0, frames, group):
        value = poly[first : first + group].reshape(group * 24, 2 * LANES)
        high, rest = split(value)
        stacked = jnp.concatenate([high, rest, high], axis=1)
        product = jnp.dot(stacked, table_ref[...], preferred_element_type=F32)
        begin = first + fir_count - 1
        spec[begin : begin + group] = product.reshape(group, 24, 2 * LANES)

    for rows in range(0, 24, 8):
        taps = []
        for tap in range(fir_count):
            for part in range(2):
                if rows < 16:
                    taps.append(taps_ref[part, tap, 0:8][None])
                    continue
                four = taps_ref[part, tap, 8:16]
                turned = pltpu.roll(four, 4, 0)
                even = jnp.where(low[0], four, turned)
                odd = jnp.where(low[0], turned, four)
                taps.append(jnp.where(place % 2 == 0, even, odd)[None])
        for first in range(0, frames, group):
            total = None
            for tap in range(fir_count):
                begin = first + fir_count - 1 - tap
                near = spec[begin : begin + group, rows : rows + 8, 0:LANES]
                cross = spec[begin : begin + group, rows : rows + 8, LANES : 2 * LANES]
                term = taps[2 * tap] * near + taps[2 * tap + 1] * cross
                total = term if total is None else total + term
            for frame in range(group):
                begin = (first + frame) * 24 + rows
                filt[begin : begin + 8, :] = total[frame]

    per_band = out_ref.shape[1] // 6
    for pair in range(6):
        rows = [
            filt[pl.ds(share_row(part, pair * 2 + odd), frames, stride=24), :]
            for part in range(2)
            for odd in range(2)
        ]
        turned = jnp.concatenate(rows, axis=0).T
        for dev in range(out_ref.shape[0]):
            out_ref[dev, pair * per_band : (pair + 1) * per_band, :] = turned[
                dev * per_band : (dev + 1) * per_band
            ]
    late_copy.wait()


def beams_kernel(x_ref, early_ref, late_ref, out_ref):
    rows = x_ref.shape[0] // 8
    beams = early_ref.shape[1] // 2
    lane = lax.broadcasted_iota(jnp.int32, (rows, LANES), 1)
    even = lane % 64 < 32
    wide = lax.broadcasted_iota(jnp.int32, (beams, LANES), 1)
    even_wide = wide % 64 < 32
    row = lax.broadcasted_iota(jnp.int32, (16, 2 * LANES), 0)
    column = lax.broadcasted_iota(jnp.int32, (16, 2 * LANES), 1)
    pool = jnp.where(row == column % 64 // INTEG, 1.0 / INTEG, 0.0).astype(BF16)
    steps = range(out_ref.shape[0] // 2)
    fields = []
    for step in steps:
        one = x_ref[pl.ds(2 * step, rows, stride=8), :]
        two = x_ref[pl.ds(2 * step + 1, rows, stride=8), :]
        first = jnp.where(even, one, pltpu.roll(two, 32, 1))
        second = jnp.where(even, pltpu.roll(one, LANES - 32, 1), two)
        both = jnp.concatenate(split(jnp.concatenate([first, second], axis=0)), axis=1)
        fields.append(jnp.concatenate([both, both], axis=0))
    beam_of = []
    for step in steps:
        if 2 * step < EARLY:
            w_ref, begin = early_ref, 2 * step
        else:
            w_ref, begin = late_ref, 2 * step - EARLY
        sums = []
        for index in range(2):
            weights = w_ref[begin + index]
            product = jnp.dot(weights, fields[step], preferred_element_type=F32)
            sums.append(product[:, 0:LANES] + product[:, LANES : 2 * LANES])
        by_real = jnp.where(even_wide, sums[0][:beams], sums[1][:beams])
        by_imag = jnp.where(even_wide, sums[0][beams:], sums[1][beams:])
        crossed = pltpu.roll(by_imag, 64, 1)
        beam_of.append(by_real + jnp.where(wide < 64, -crossed, crossed))
    for step in steps:
        power = lax.dot_general(
            pool,
            jnp.concatenate(split(beam_of[step] * beam_of[step]), axis=1),
            (((1,), (1,)), ((), ())),
            preferred_element_type=F32,
        )
        out_ref[2 * step] = power[0:8]
        out_ref[2 * step + 1] = power[8:16]


def slots_of(devices):
    index = np.arange(devices * 12, dtype=np.int32)
    own = index % 6 * 2 + index // (devices * 6)
    source = index // 6 % devices
    dishes = np.where(own < 8, source * 8 + own, devices * 8 + source * 4 + own - 8)
    return dishes.astype(np.int32)[:, None]


def dft_parts(channels):
    index = np.arange(channels)
    angle = 2.0 * np.pi * (index[:, None] * index[None, :] % channels) / channels
    cosine = np.cos(angle) / np.sqrt(channels)
    sine = np.sin(angle) / np.sqrt(channels)
    table = np.block([[cosine, sine], [sine, -cosine]]).astype(np.float32)
    high = table.astype(jnp.bfloat16)
    rest = (table - high.astype(np.float32)).astype(jnp.bfloat16)
    return np.concatenate([high, high, rest], axis=0)


def close_body(samples, prototype, dish_filter, beam_weights, dish_order):
    devices = lax.axis_size("band")
    channels = prototype.shape[1]
    fir_count = dish_filter.shape[1]
    dishes = dish_filter.shape[2]
    band_chans = beam_weights.shape[1]
    beams = beam_weights.shape[4]
    frames_dev = samples.shape[2] // channels
    frames = frames_dev * devices

    def exchange(value):
        return lax.all_to_all(value, "band", split_axis=0, concat_axis=0, tiled=True)

    pieces = pl.pallas_call(
        pieces_kernel,
        out_shape=jax.ShapeDtypeStruct((devices, frames_dev, 24, channels), F32),
        in_specs=[VMEM],
        out_specs=VMEM,
        name="pieces",
        compiler_params=GRANT,
    )(samples)
    arrived = exchange(pieces).reshape(frames, 24, channels)

    table = dft_parts(channels)
    early, late = pl.pallas_call(
        weights_kernel,
        out_shape=[
            jax.ShapeDtypeStruct((EARLY, 2 * beams, 2 * dishes), BF16),
            pltpu.HBM((band_chans - EARLY, 2 * beams, 2 * dishes), BF16),
        ],
        in_specs=[HBM, VMEM, VMEM],
        out_specs=[VMEM, HBM],
        scratch_shapes=[
            pltpu.VMEM((band_chans, 2, dishes, beams), F32),
            pltpu.VMEM((band_chans - EARLY, 2 * beams, 2 * dishes), BF16),
            pltpu.SemaphoreType.DMA((2, band_chans)),
        ],
        name="weights",
        compiler_params=GRANT,
        cost_estimate=pl.CostEstimate(
            flops=8 * 4 * 2 * 192 * 192 * 384, bytes_accessed=5 << 20, transcendentals=0
        ),
    )(
        held(beam_weights[0], pltpu.HBM),
        dish_order.reshape(1, dishes),
        slots_of(devices),
    )
    arrived, early, late = lax.optimization_barrier((arrived, early, late))

    block = (6 * band_chans, channels)
    filtered, late = pl.pallas_call(
        channel_kernel,
        out_shape=[
            jax.ShapeDtypeStruct((devices,) + block, F32),
            jax.ShapeDtypeStruct(late.shape, BF16),
        ],
        in_specs=[VMEM] * 2 + [HBM] * 3,
        out_specs=[VMEM] * 2,
        scratch_shapes=[
            pltpu.VMEM((frames + prototype.shape[0] - 1, 24, LANES), F32),
            pltpu.VMEM((frames, 24, 2 * LANES), F32),
            pltpu.VMEM((frames + fir_count - 1, 24, 2 * LANES), F32),
            pltpu.VMEM((frames * 24, LANES), F32),
            pltpu.VMEM(table.shape, BF16),
            pltpu.VMEM((2, fir_count, 16, LANES), F32),
            pltpu.SemaphoreType.DMA((4,)),
        ],
        name="channels",
        compiler_params=GRANT,
    )(
        held(arrived, pltpu.VMEM),
        prototype,
        held(jnp.asarray(table), pltpu.HBM),
        held(dish_filter, pltpu.HBM),
        held(late, pltpu.HBM),
    )
    field = exchange(filtered).reshape(devices * 6 * band_chans, channels)

    power = pl.pallas_call(
        beams_kernel,
        out_shape=jax.ShapeDtypeStruct((band_chans, frames // INTEG, beams), F32),
        in_specs=[VMEM] * 3,
        out_specs=VMEM,
        name="beams",
        compiler_params=GRANT,
    )(held(field, pltpu.VMEM), held(early, pltpu.VMEM), held(late, pltpu.VMEM))
    return jnp.transpose(power, (0, 2, 1))[None]


def detect(weights, field_real, field_imag):
    def contract(weight_part, field_part):
        return jnp.einsum("qds,dqf->qsf", weight_part, field_part, precision=HIGHEST)

    beam_real = contract(weights[:, 0], field_real) - contract(weights[:, 1], field_imag)
    beam_imag = contract(weights[:, 0], field_imag) + contract(weights[:, 1], field_real)
    energy = beam_real * beam_real + beam_imag * beam_imag
    shaped = energy.reshape(energy.shape[:-1] + (energy.shape[-1] // INTEG, INTEG))
    return jnp.mean(shaped, axis=-1)


def wide_body(samples, prototype, dish_filter, beam_weights, dish_order):
    devices = lax.axis_size("band")
    position = lax.axis_index("band")
    pfb_count, channels = prototype.shape
    fir_count = dish_filter.shape[1]
    dishes = dish_filter.shape[2]
    band_chans = beam_weights.shape[1]
    bands = channels // band_chans
    owners = devices // bands
    frames_dev = samples.shape[2] // channels
    frames = frames_dev * devices
    share = -(-dishes // devices)
    extra = share * devices - dishes

    padded = jnp.pad(samples, ((0, 0), (0, extra), (0, 0)))
    pieces = padded.reshape(2, devices, share, frames_dev, channels)
    pieces = jnp.transpose(pieces, (1, 3, 0, 2, 4)).reshape(
        devices, frames_dev, 2 * share, channels
    )
    arrived = lax.all_to_all(pieces, "band", split_axis=0, concat_axis=0, tiled=True)
    blocks = arrived.reshape(frames, 2 * share, channels)

    history = jnp.pad(blocks, ((pfb_count - 1, 0), (0, 0), (0, 0)))
    polyphase = jnp.zeros_like(blocks)
    for tap_index in range(pfb_count):
        offset = pfb_count - 1 - tap_index
        polyphase = polyphase + prototype[tap_index] * history[offset : offset + frames]
    cosine, sine = fourier_tables(channels)
    both = jnp.dot(polyphase, jnp.concatenate([cosine, sine], axis=1), precision=HIGHEST)
    with_cos = both[..., :channels].reshape(frames, 2, share, channels)
    with_sin = both[..., channels:].reshape(frames, 2, share, channels)
    spec_real = with_cos[:, 0] + with_sin[:, 1]
    spec_imag = with_cos[:, 1] - with_sin[:, 0]

    taps = jnp.pad(dish_filter, ((0, 0), (0, 0), (0, extra), (0, 0)))
    taps = lax.dynamic_slice_in_dim(taps, position * share, share, 2)
    lead = ((fir_count - 1, 0), (0, 0), (0, 0))
    past_real, past_imag = jnp.pad(spec_real, lead), jnp.pad(spec_imag, lead)
    out_real = jnp.zeros_like(spec_real)
    out_imag = jnp.zeros_like(spec_imag)
    for tap_index in range(fir_count):
        offset = fir_count - 1 - tap_index
        part_real = past_real[offset : offset + frames]
        part_imag = past_imag[offset : offset + frames]
        factor_real, factor_imag = taps[0, tap_index], taps[1, tap_index]
        out_real = out_real + factor_real * part_real - factor_imag * part_imag
        out_imag = out_imag + factor_real * part_imag + factor_imag * part_real

    filtered = jnp.stack([out_real, out_imag])
    filtered = filtered.reshape(2, frames, share, bands, band_chans)
    filtered = jnp.transpose(filtered, (3, 0, 2, 4, 1)).reshape(
        bands, 2 * share, band_chans * frames
    )
    filtered = jnp.repeat(filtered, owners, axis=0)
    field = lax.all_to_all(filtered, "band", split_axis=0, concat_axis=0, tiled=True)
    field = field.reshape(devices, 2, share, band_chans, frames)
    field = jnp.transpose(field, (1, 0, 2, 3, 4))
    field = field.reshape(2, devices * share, band_chans, frames)
    field = jnp.take(field, dish_order, axis=1)
    power = detect(beam_weights[0], field[0], field[1])
    return power[None]


def solution(mesh):
    devices = mesh.shape["band"]

    def body(samples, prototype, dish_filter, beam_weights, dish_order):
        channels = prototype.shape[1]
        close = (
            channels == LANES
            and beam_weights.shape[1] == 8
            and devices * 8 == channels
            and dish_filter.shape[2] == 12 * devices
            and samples.shape[2] * devices == 32 * channels
        )
        chosen = close_body if close else wide_body
        return chosen(samples, prototype, dish_filter, beam_weights, dish_order)

    placed = (P(None, None, ("grp", "band")), P(), P(), P("band", None, None, None, None), P())
    return jax.shard_map(
        body,
        mesh=mesh,
        in_specs=placed,
        out_specs=P(("grp", "band"), None, None, None),
        check_vma=False,
    )
```

```python
import math

import jax
import jax.numpy as jnp
import numpy as np
from jax import lax
from jax.experimental import pallas as pl
from jax.experimental.pallas import tpu as pltpu
from jax.sharding import PartitionSpec as P

INTEG = 4
HIGHEST = lax.Precision.HIGHEST
F32 = jnp.float32
BF16 = jnp.bfloat16
LANES = 128
VMEM = pl.BlockSpec(memory_space=pltpu.VMEM)
HBM = pl.BlockSpec(memory_space=pltpu.HBM)
GRANT = pltpu.CompilerParams(vmem_limit_bytes=16 << 20)


def fourier_tables(length):
    counter = jnp.arange(length, dtype=jnp.int32)
    product = counter[:, None] * counter[None, :] % length
    angles = product.astype(jnp.float32) * (2.0 * math.pi / length)
    factor = 1.0 / math.sqrt(length)
    return (jnp.cos(angles) * factor, jnp.sin(angles) * factor)


held = pltpu.with_memory_space_constraint


def split(value):
    high = value.astype(BF16)
    return high, (value - high.astype(F32)).astype(BF16)


def share_row(part, dish):
    return part * 8 + dish if dish < 8 else 16 + part * 4 + dish - 8


def pieces_kernel(x_ref, out_ref):
    devices, frames_dev = out_ref.shape[:2]
    low = lax.broadcasted_iota(jnp.int32, (8, LANES), 0) < 4
    for frame in range(frames_dev):
        lanes = slice(frame * LANES, (frame + 1) * LANES)
        for dev in range(0, devices, 2):
            for one in (dev, dev + 1):
                for part in range(2):
                    out_ref[one, frame, part * 8 : part * 8 + 8, :] = x_ref[
                        part, one * 8 : one * 8 + 8, lanes
                    ]
            start = devices * 8 + dev * 4
            real = x_ref[0, start : start + 8, lanes]
            imag = x_ref[1, start : start + 8, lanes]
            out_ref[dev, frame, 16:24, :] = jnp.where(low, real, pltpu.roll(imag, 4, 0))
            out_ref[dev + 1, frame, 16:24, :] = jnp.where(low, pltpu.roll(real, 4, 0), imag)


def make_weights(w_ref, hot, out_ref, chan):
    beams = w_ref.shape[3]
    for part in range(2):
        halves = [
            jnp.dot(half, hot, preferred_element_type=F32).astype(BF16)
            for half in split(w_ref[chan, part].T)
        ]
        rows = slice(part * beams, (part + 1) * beams)
        out_ref[chan, rows, :] = jnp.concatenate(halves, axis=1)


def channel_kernel(
    x_ref, proto_ref, w_ref, order_ref, slot_ref, table_hbm, taps_hbm, out_ref, w_out_ref, *scratch
):
    past, poly, spec, filt, table_ref, taps_ref, sems = scratch
    place = lax.axis_index("band")
    devices = out_ref.shape[0]
    eight = pl.ds(pl.multiple_of(place * 8, 8), 8)
    pair_rows = pl.ds(pl.multiple_of(devices * 8 + place // 2 * 8, 8), 8)
    loads = [
        pltpu.make_async_copy(taps_hbm.at[:, :, eight, :], taps_ref.at[:, :, 0:8], sems.at[0]),
        pltpu.make_async_copy(taps_hbm.at[:, :, pair_rows, :], taps_ref.at[:, :, 8:16], sems.at[1]),
        pltpu.make_async_copy(table_hbm, table_ref, sems.at[2]),
    ]
    for load in loads:
        load.start()
    hot = (slot_ref[...] == order_ref[...]).astype(F32).T.astype(BF16)
    chans = w_ref.shape[0]
    pfb_count = proto_ref.shape[0]
    fir_count = taps_ref.shape[1]
    frames = poly.shape[0]
    group = 8
    low = lax.broadcasted_iota(jnp.int32, (group, 8, LANES), 1) < 4

    past[0 : pfb_count - 1] = jnp.zeros((pfb_count - 1, 24, LANES), F32)
    past[pfb_count - 1 :] = x_ref[...]

    spec[0 : fir_count - 1] = jnp.zeros((fir_count - 1, 24, 2 * LANES), F32)
    for first in range(0, frames, group):
        found = []
        for rows in range(0, 24, 8):
            total = None
            for tap in range(pfb_count):
                begin = first + pfb_count - 1 - tap
                block = past[begin : begin + group, rows : rows + 8, :]
                term = block * proto_ref[tap : tap + 1, :][None]
                total = term if total is None else total + term
            found.append(total)
        turned = pltpu.roll(found[2], 4, 1)
        other = [found[1], -found[0], jnp.where(low, turned, -turned)]
        for index in range(3):
            rows = slice(index * 8, index * 8 + 8)
            poly[first : first + group, rows, 0:LANES] = found[index]
            poly[first : first + group, rows, LANES : 2 * LANES] = other[index]
        for chan in range(first * chans // frames, (first + group) * chans // frames):
            make_weights(w_ref, hot, w_out_ref, chan)

    for load in loads:
        load.wait()

    for first in range(0, frames, group):
        value = poly[first : first + group].reshape(group * 24, 2 * LANES)
        high, rest = split(value)
        stacked = jnp.concatenate([high, rest, high], axis=1)
        product = jnp.dot(stacked, table_ref[...], preferred_element_type=F32)
        begin = first + fir_count - 1
        spec[begin : begin + group] = product.reshape(group, 24, 2 * LANES)

    for rows in range(0, 24, 8):
        taps = []
        for tap in range(fir_count):
            for part in range(2):
                if rows < 16:
                    taps.append(taps_ref[part, tap, 0:8][None])
                    continue
                four = taps_ref[part, tap, 8:16]
                turned = pltpu.roll(four, 4, 0)
                even = jnp.where(low[0], four, turned)
                odd = jnp.where(low[0], turned, four)
                taps.append(jnp.where(place % 2 == 0, even, odd)[None])
        for first in range(0, frames, group):
            total = None
            for tap in range(fir_count):
                begin = first + fir_count - 1 - tap
                near = spec[begin : begin + group, rows : rows + 8, 0:LANES]
                cross = spec[begin : begin + group, rows : rows + 8, LANES : 2 * LANES]
                term = taps[2 * tap] * near + taps[2 * tap + 1] * cross
                total = term if total is None else total + term
            for frame in range(group):
                begin = (first + frame) * 24 + rows
                filt[begin : begin + 8, :] = total[frame]

    per_band = out_ref.shape[1] // 6
    for pair in range(6):
        rows = [
            filt[pl.ds(share_row(part, pair * 2 + odd), frames, stride=24), :]
            for part in range(2)
            for odd in range(2)
        ]
        turned = jnp.concatenate(rows, axis=0).T
        for dev in range(out_ref.shape[0]):
            out_ref[dev, pair * per_band : (pair + 1) * per_band, :] = turned[
                dev * per_band : (dev + 1) * per_band
            ]


def beams_kernel(x_ref, w_ref, out_ref):
    rows = x_ref.shape[0] // 8
    beams = w_ref.shape[1] // 2
    lane = lax.broadcasted_iota(jnp.int32, (rows, LANES), 1)
    even = lane % 64 < 32
    wide = lax.broadcasted_iota(jnp.int32, (beams, LANES), 1)
    even_wide = wide % 64 < 32
    row = lax.broadcasted_iota(jnp.int32, (16, 2 * LANES), 0)
    column = lax.broadcasted_iota(jnp.int32, (16, 2 * LANES), 1)
    pool = jnp.where(row == column % 64 // INTEG, 1.0 / INTEG, 0.0).astype(BF16)
    steps = range(out_ref.shape[0] // 2)
    fields = []
    for step in steps:
        one = x_ref[pl.ds(2 * step, rows, stride=8), :]
        two = x_ref[pl.ds(2 * step + 1, rows, stride=8), :]
        first = jnp.where(even, one, pltpu.roll(two, 32, 1))
        second = jnp.where(even, pltpu.roll(one, LANES - 32, 1), two)
        both = jnp.concatenate(split(jnp.concatenate([first, second], axis=0)), axis=1)
        fields.append(jnp.concatenate([both, both], axis=0))
    beam_of = []
    for step in steps:
        sums = []
        for index in range(2):
            product = jnp.dot(w_ref[2 * step + index], fields[step], preferred_element_type=F32)
            sums.append(product[:, 0:LANES] + product[:, LANES : 2 * LANES])
        by_real = jnp.where(even_wide, sums[0][:beams], sums[1][:beams])
        by_imag = jnp.where(even_wide, sums[0][beams:], sums[1][beams:])
        crossed = pltpu.roll(by_imag, 64, 1)
        beam_of.append(by_real + jnp.where(wide < 64, -crossed, crossed))
    for step in steps:
        power = lax.dot_general(
            pool,
            jnp.concatenate(split(beam_of[step] * beam_of[step]), axis=1),
            (((1,), (1,)), ((), ())),
            preferred_element_type=F32,
        )
        out_ref[2 * step] = power[0:8]
        out_ref[2 * step + 1] = power[8:16]


def slots_of(devices):
    index = np.arange(devices * 12, dtype=np.int32)
    own = index % 6 * 2 + index // (devices * 6)
    source = index // 6 % devices
    dishes = np.where(own < 8, source * 8 + own, devices * 8 + source * 4 + own - 8)
    return dishes.astype(np.int32)[:, None]


def dft_parts(channels):
    index = np.arange(channels)
    angle = 2.0 * np.pi * (index[:, None] * index[None, :] % channels) / channels
    cosine = np.cos(angle) / np.sqrt(channels)
    sine = np.sin(angle) / np.sqrt(channels)
    table = np.block([[cosine, sine], [sine, -cosine]]).astype(np.float32)
    high = table.astype(jnp.bfloat16)
    rest = (table - high.astype(np.float32)).astype(jnp.bfloat16)
    return np.concatenate([high, high, rest], axis=0)


def close_body(samples, prototype, dish_filter, beam_weights, dish_order):
    devices = lax.axis_size("band")
    channels = prototype.shape[1]
    fir_count = dish_filter.shape[1]
    dishes = dish_filter.shape[2]
    band_chans = beam_weights.shape[1]
    beams = beam_weights.shape[4]
    frames_dev = samples.shape[2] // channels
    frames = frames_dev * devices

    def exchange(value):
        return lax.all_to_all(value, "band", split_axis=0, concat_axis=0, tiled=True)

    pieces = pl.pallas_call(
        pieces_kernel,
        out_shape=jax.ShapeDtypeStruct((devices, frames_dev, 24, channels), F32),
        in_specs=[VMEM],
        out_specs=VMEM,
        name="pieces",
        compiler_params=GRANT,
    )(samples)
    arrived = exchange(pieces).reshape(frames, 24, channels)

    table = dft_parts(channels)
    block = (6 * band_chans, channels)
    filtered, weights = pl.pallas_call(
        channel_kernel,
        out_shape=[
            jax.ShapeDtypeStruct((devices,) + block, F32),
            jax.ShapeDtypeStruct((band_chans, 2 * beams, 2 * dishes), BF16),
        ],
        in_specs=[VMEM] * 5 + [HBM] * 2,
        out_specs=[VMEM] * 2,
        scratch_shapes=[
            pltpu.VMEM((frames + prototype.shape[0] - 1, 24, LANES), F32),
            pltpu.VMEM((frames, 24, 2 * LANES), F32),
            pltpu.VMEM((frames + fir_count - 1, 24, 2 * LANES), F32),
            pltpu.VMEM((frames * 24, LANES), F32),
            pltpu.VMEM(table.shape, BF16),
            pltpu.VMEM((2, fir_count, 16, LANES), F32),
            pltpu.SemaphoreType.DMA((3,)),
        ],
        name="channels",
        compiler_params=GRANT,
    )(
        held(arrived, pltpu.VMEM),
        prototype,
        beam_weights[0],
        dish_order.reshape(1, dishes),
        slots_of(devices),
        held(jnp.asarray(table), pltpu.HBM),
        held(dish_filter, pltpu.HBM),
    )
    field = exchange(filtered).reshape(devices * 6 * band_chans, channels)

    power = pl.pallas_call(
        beams_kernel,
        out_shape=jax.ShapeDtypeStruct((band_chans, frames // INTEG, beams), F32),
        in_specs=[VMEM] * 2,
        out_specs=VMEM,
        name="beams",
        compiler_params=GRANT,
    )(held(field, pltpu.VMEM), held(weights, pltpu.VMEM))
    return jnp.transpose(power, (0, 2, 1))[None]


def detect(weights, field_real, field_imag):
    def contract(weight_part, field_part):
        return jnp.einsum("qds,dqf->qsf", weight_part, field_part, precision=HIGHEST)

    beam_real = contract(weights[:, 0], field_real) - contract(weights[:, 1], field_imag)
    beam_imag = contract(weights[:, 0], field_imag) + contract(weights[:, 1], field_real)
    energy = beam_real * beam_real + beam_imag * beam_imag
    shaped = energy.reshape(energy.shape[:-1] + (energy.shape[-1] // INTEG, INTEG))
    return jnp.mean(shaped, axis=-1)


def wide_body(samples, prototype, dish_filter, beam_weights, dish_order):
    devices = lax.axis_size("band")
    position = lax.axis_index("band")
    pfb_count, channels = prototype.shape
    fir_count = dish_filter.shape[1]
    dishes = dish_filter.shape[2]
    band_chans = beam_weights.shape[1]
    bands = channels // band_chans
    owners = devices // bands
    frames_dev = samples.shape[2] // channels
    frames = frames_dev * devices
    share = -(-dishes // devices)
    extra = share * devices - dishes

    padded = jnp.pad(samples, ((0, 0), (0, extra), (0, 0)))
    pieces = padded.reshape(2, devices, share, frames_dev, channels)
    pieces = jnp.transpose(pieces, (1, 3, 0, 2, 4)).reshape(
        devices, frames_dev, 2 * share, channels
    )
    arrived = lax.all_to_all(pieces, "band", split_axis=0, concat_axis=0, tiled=True)
    blocks = arrived.reshape(frames, 2 * share, channels)

    history = jnp.pad(blocks, ((pfb_count - 1, 0), (0, 0), (0, 0)))
    polyphase = jnp.zeros_like(blocks)
    for tap_index in range(pfb_count):
        offset = pfb_count - 1 - tap_index
        polyphase = polyphase + prototype[tap_index] * history[offset : offset + frames]
    cosine, sine = fourier_tables(channels)
    both = jnp.dot(polyphase, jnp.concatenate([cosine, sine], axis=1), precision=HIGHEST)
    with_cos = both[..., :channels].reshape(frames, 2, share, channels)
    with_sin = both[..., channels:].reshape(frames, 2, share, channels)
    spec_real = with_cos[:, 0] + with_sin[:, 1]
    spec_imag = with_cos[:, 1] - with_sin[:, 0]

    taps = jnp.pad(dish_filter, ((0, 0), (0, 0), (0, extra), (0, 0)))
    taps = lax.dynamic_slice_in_dim(taps, position * share, share, 2)
    lead = ((fir_count - 1, 0), (0, 0), (0, 0))
    past_real, past_imag = jnp.pad(spec_real, lead), jnp.pad(spec_imag, lead)
    out_real = jnp.zeros_like(spec_real)
    out_imag = jnp.zeros_like(spec_imag)
    for tap_index in range(fir_count):
        offset = fir_count - 1 - tap_index
        part_real = past_real[offset : offset + frames]
        part_imag = past_imag[offset : offset + frames]
        factor_real, factor_imag = taps[0, tap_index], taps[1, tap_index]
        out_real = out_real + factor_real * part_real - factor_imag * part_imag
        out_imag = out_imag + factor_real * part_imag + factor_imag * part_real

    filtered = jnp.stack([out_real, out_imag])
    filtered = filtered.reshape(2, frames, share, bands, band_chans)
    filtered = jnp.transpose(filtered, (3, 0, 2, 4, 1)).reshape(
        bands, 2 * share, band_chans * frames
    )
    filtered = jnp.repeat(filtered, owners, axis=0)
    field = lax.all_to_all(filtered, "band", split_axis=0, concat_axis=0, tiled=True)
    field = field.reshape(devices, 2, share, band_chans, frames)
    field = jnp.transpose(field, (1, 0, 2, 3, 4))
    field = field.reshape(2, devices * share, band_chans, frames)
    field = jnp.take(field, dish_order, axis=1)
    power = detect(beam_weights[0], field[0], field[1])
    return power[None]


def solution(mesh):
    devices = mesh.shape["band"]

    def body(samples, prototype, dish_filter, beam_weights, dish_order):
        channels = prototype.shape[1]
        close = (
            channels == LANES
            and beam_weights.shape[1] == 8
            and devices * 8 == channels
            and dish_filter.shape[2] == 12 * devices
            and samples.shape[2] * devices == 32 * channels
        )
        chosen = close_body if close else wide_body
        return chosen(samples, prototype, dish_filter, beam_weights, dish_order)

    placed = (P(None, None, ("grp", "band")), P(), P(), P("band", None, None, None, None), P())
    return jax.shard_map(
        body,
        mesh=mesh,
        in_specs=placed,
        out_specs=P(("grp", "band"), None, None, None),
        check_vma=False,
    )
```

```python
import math

import jax
import jax.numpy as jnp
import numpy as np
from jax import lax
from jax.experimental import pallas as pl
from jax.experimental.pallas import tpu as pltpu
from jax.sharding import PartitionSpec as P

INTEG = 4
EARLY = 2
LAST = 2
HIGHEST = lax.Precision.HIGHEST
F32 = jnp.float32
BF16 = jnp.bfloat16
LANES = 128
VMEM = pl.BlockSpec(memory_space=pltpu.VMEM)
HBM = pl.BlockSpec(memory_space=pltpu.HBM)
GRANT = pltpu.CompilerParams(vmem_limit_bytes=16 << 20)


def fourier_tables(length):
    counter = jnp.arange(length, dtype=jnp.int32)
    product = counter[:, None] * counter[None, :] % length
    angles = product.astype(jnp.float32) * (2.0 * math.pi / length)
    factor = 1.0 / math.sqrt(length)
    return (jnp.cos(angles) * factor, jnp.sin(angles) * factor)


held = pltpu.with_memory_space_constraint


def split(value):
    high = value.astype(BF16)
    return high, (value - high.astype(F32)).astype(BF16)


def share_row(part, dish):
    return part * 8 + dish if dish < 8 else 16 + part * 4 + dish - 8


def pieces_kernel(x_ref, out_ref):
    devices, frames_dev = out_ref.shape[:2]
    low = lax.broadcasted_iota(jnp.int32, (8, LANES), 0) < 4
    for frame in range(frames_dev):
        lanes = slice(frame * LANES, (frame + 1) * LANES)
        for dev in range(0, devices, 2):
            for one in (dev, dev + 1):
                for part in range(2):
                    out_ref[one, frame, part * 8 : part * 8 + 8, :] = x_ref[
                        part, one * 8 : one * 8 + 8, lanes
                    ]
            start = devices * 8 + dev * 4
            real = x_ref[0, start : start + 8, lanes]
            imag = x_ref[1, start : start + 8, lanes]
            out_ref[dev, frame, 16:24, :] = jnp.where(low, real, pltpu.roll(imag, 4, 0))
            out_ref[dev + 1, frame, 16:24, :] = jnp.where(low, pltpu.roll(real, 4, 0), imag)


def weights_kernel(
    w_ref, order_ref, slot_ref, table_ref, early_ref, late_ref, table_out_ref, *scratch
):
    buffer, made, sems, table_sem = scratch
    table_copy = pltpu.make_async_copy(table_ref, table_out_ref, table_sem)
    loads = [
        pltpu.make_async_copy(w_ref.at[chan], buffer.at[chan], sems.at[0, chan])
        for chan in range(w_ref.shape[0])
    ]
    stores = [
        pltpu.make_async_copy(made.at[chan], late_ref.at[chan], sems.at[1, chan])
        for chan in range(late_ref.shape[0])
    ]
    ahead = 3
    for load in loads[:ahead]:
        load.start()
    hot = (slot_ref[...] == order_ref[...]).astype(F32).T.astype(BF16)
    beams = w_ref.shape[3]
    for chan, load in enumerate(loads):
        load.wait()
        if chan + ahead < len(loads):
            loads[chan + ahead].start()
        elif chan + ahead == len(loads):
            table_copy.start()
        for part in range(2):
            halves = [
                jnp.dot(half, hot, preferred_element_type=F32).astype(BF16)
                for half in split(buffer[chan, part].T)
            ]
            rows = slice(part * beams, (part + 1) * beams)
            both = jnp.concatenate(halves, axis=1)
            if chan < EARLY:
                early_ref[chan, rows, :] = both
            else:
                made[chan - EARLY, rows, :] = both
        if chan >= EARLY:
            stores[chan - EARLY].start()
    for store in stores:
        store.wait()
    table_copy.wait()


def channel_kernel(
    x_ref, proto_ref, table_ref, taps_ref, late_ref, out_ref, late_out_ref, *scratch
):
    past, poly, spec, filt, late_sem = scratch
    count = late_out_ref.shape[0]
    late_copy = pltpu.make_async_copy(late_ref.at[0:count], late_out_ref, late_sem)
    late_copy.start()
    pfb_count = proto_ref.shape[0]
    fir_count = taps_ref.shape[0]
    frames = poly.shape[0]
    group = 8
    low = lax.broadcasted_iota(jnp.int32, (group, 8, LANES), 1) < 4

    past[0 : pfb_count - 1] = jnp.zeros((pfb_count - 1, 24, LANES), F32)
    past[pfb_count - 1 :] = x_ref[...]

    spec[0 : fir_count - 1] = jnp.zeros((fir_count - 1, 24, 2 * LANES), F32)
    for first in range(0, frames, group):
        found = []
        for rows in range(0, 24, 8):
            total = None
            for tap in range(pfb_count):
                begin = first + pfb_count - 1 - tap
                block = past[begin : begin + group, rows : rows + 8, :]
                term = block * proto_ref[tap : tap + 1, :][None]
                total = term if total is None else total + term
            found.append(total)
        turned = pltpu.roll(found[2], 4, 1)
        other = [found[1], -found[0], jnp.where(low, turned, -turned)]
        for index in range(3):
            rows = slice(index * 8, index * 8 + 8)
            poly[first : first + group, rows, 0:LANES] = found[index]
            poly[first : first + group, rows, LANES : 2 * LANES] = other[index]

    for first in range(0, frames, group):
        value = poly[first : first + group].reshape(group * 24, 2 * LANES)
        high, rest = split(value)
        stacked = jnp.concatenate([high, rest, high], axis=1)
        product = jnp.dot(stacked, table_ref[...], preferred_element_type=F32)
        begin = first + fir_count - 1
        spec[begin : begin + group] = product.reshape(group, 24, 2 * LANES)

    for rows in range(0, 24, 8):
        for first in range(0, frames, group):
            total = None
            for tap in range(fir_count):
                begin = first + fir_count - 1 - tap
                near = spec[begin : begin + group, rows : rows + 8, 0:LANES]
                cross = spec[begin : begin + group, rows : rows + 8, LANES : 2 * LANES]
                term = taps_ref[tap, 0, rows : rows + 8, :][None] * near
                term = term + taps_ref[tap, 1, rows : rows + 8, :][None] * cross
                total = term if total is None else total + term
            for frame in range(group):
                begin = (first + frame) * 24 + rows
                filt[begin : begin + 8, :] = total[frame]

    per_band = out_ref.shape[1] // 6
    for pair in range(6):
        rows = [
            filt[pl.ds(share_row(part, pair * 2 + odd), frames, stride=24), :]
            for part in range(2)
            for odd in range(2)
        ]
        turned = jnp.concatenate(rows, axis=0).T
        for dev in range(out_ref.shape[0]):
            out_ref[dev, pair * per_band : (pair + 1) * per_band, :] = turned[
                dev * per_band : (dev + 1) * per_band
            ]
    late_copy.wait()


def beams_kernel(x_ref, early_ref, middle_ref, late_hbm, out_hbm, last_ref, out_ref, sems):
    chans = out_ref.shape[0]
    last_load = pltpu.make_async_copy(late_hbm.at[middle_ref.shape[0] :], last_ref, sems.at[0])
    last_load.start()
    rows = x_ref.shape[0] // 8
    beams = early_ref.shape[1] // 2
    lane = lax.broadcasted_iota(jnp.int32, (rows, LANES), 1)
    even = lane % 64 < 32
    wide = lax.broadcasted_iota(jnp.int32, (beams, LANES), 1)
    even_wide = wide % 64 < 32
    row = lax.broadcasted_iota(jnp.int32, (16, 2 * LANES), 0)
    column = lax.broadcasted_iota(jnp.int32, (16, 2 * LANES), 1)
    pool = jnp.where(row == column % 64 // INTEG, 1.0 / INTEG, 0.0).astype(BF16)
    steps = range(out_ref.shape[0] // 2)
    fields = []
    for step in steps:
        one = x_ref[pl.ds(2 * step, rows, stride=8), :]
        two = x_ref[pl.ds(2 * step + 1, rows, stride=8), :]
        first = jnp.where(even, one, pltpu.roll(two, 32, 1))
        second = jnp.where(even, pltpu.roll(one, LANES - 32, 1), two)
        both = jnp.concatenate(split(jnp.concatenate([first, second], axis=0)), axis=1)
        fields.append(jnp.concatenate([both, both], axis=0))
    beam_of = []
    for step in steps:
        if 2 * step < EARLY:
            w_ref, begin = early_ref, 2 * step
        elif 2 * step < chans - LAST:
            w_ref, begin = middle_ref, 2 * step - EARLY
        else:
            w_ref, begin = last_ref, 2 * step - (chans - LAST)
            if begin == 0:
                last_load.wait()
        sums = []
        for index in range(2):
            weights = w_ref[begin + index]
            product = jnp.dot(weights, fields[step], preferred_element_type=F32)
            sums.append(product[:, 0:LANES] + product[:, LANES : 2 * LANES])
        by_real = jnp.where(even_wide, sums[0][:beams], sums[1][:beams])
        by_imag = jnp.where(even_wide, sums[0][beams:], sums[1][beams:])
        crossed = pltpu.roll(by_imag, 64, 1)
        beam_of.append(by_real + jnp.where(wide < 64, -crossed, crossed))
    stores = []
    for step in steps:
        power = lax.dot_general(
            pool,
            jnp.concatenate(split(beam_of[step] * beam_of[step]), axis=1),
            (((1,), (1,)), ((), ())),
            preferred_element_type=F32,
        )
        out_ref[2 * step] = power[0:8]
        out_ref[2 * step + 1] = power[8:16]
        pair = slice(2 * step, 2 * step + 2)
        stores.append(
            pltpu.make_async_copy(out_ref.at[pair], out_hbm.at[pair], sems.at[1 + step])
        )
        stores[-1].start()
    for store in stores:
        store.wait()


def slots_of(devices):
    index = np.arange(devices * 12, dtype=np.int32)
    own = index % 6 * 2 + index // (devices * 6)
    source = index // 6 % devices
    dishes = np.where(own < 8, source * 8 + own, devices * 8 + source * 4 + own - 8)
    return dishes.astype(np.int32)[:, None]


def dft_parts(channels):
    index = np.arange(channels)
    angle = 2.0 * np.pi * (index[:, None] * index[None, :] % channels) / channels
    cosine = np.cos(angle) / np.sqrt(channels)
    sine = np.sin(angle) / np.sqrt(channels)
    table = np.block([[cosine, sine], [sine, -cosine]]).astype(np.float32)
    high = table.astype(jnp.bfloat16)
    rest = (table - high.astype(np.float32)).astype(jnp.bfloat16)
    return np.concatenate([high, high, rest], axis=0)


def close_body(samples, prototype, dish_filter, beam_weights, dish_order):
    devices = lax.axis_size("band")
    position = lax.axis_index("band")
    channels = prototype.shape[1]
    fir_count = dish_filter.shape[1]
    dishes = dish_filter.shape[2]
    band_chans = beam_weights.shape[1]
    beams = beam_weights.shape[4]
    frames_dev = samples.shape[2] // channels
    frames = frames_dev * devices

    def exchange(value):
        return lax.all_to_all(value, "band", split_axis=0, concat_axis=0, tiled=True)

    pieces = pl.pallas_call(
        pieces_kernel,
        out_shape=jax.ShapeDtypeStruct((devices, frames_dev, 24, channels), F32),
        in_specs=[VMEM],
        out_specs=VMEM,
        name="pieces",
        compiler_params=GRANT,
    )(samples)
    arrived = exchange(pieces).reshape(frames, 24, channels)

    eight = lax.dynamic_slice_in_dim(dish_filter, position * 8, 8, 2)
    four = lax.dynamic_slice_in_dim(dish_filter, devices * 8 + position * 4, 4, 2)
    taps = jnp.concatenate([eight, eight, four, four], axis=2)
    taps = jnp.transpose(taps, (1, 0, 2, 3))
    table = dft_parts(channels)
    early, late, table = pl.pallas_call(
        weights_kernel,
        out_shape=[
            jax.ShapeDtypeStruct((EARLY, 2 * beams, 2 * dishes), BF16),
            pltpu.HBM((band_chans - EARLY, 2 * beams, 2 * dishes), BF16),
            jax.ShapeDtypeStruct(table.shape, BF16),
        ],
        in_specs=[HBM, VMEM, VMEM, HBM],
        out_specs=[VMEM, HBM, VMEM],
        scratch_shapes=[
            pltpu.VMEM((band_chans, 2, dishes, beams), F32),
            pltpu.VMEM((band_chans - EARLY, 2 * beams, 2 * dishes), BF16),
            pltpu.SemaphoreType.DMA((2, band_chans)),
            pltpu.SemaphoreType.DMA(()),
        ],
        name="weights",
        compiler_params=GRANT,
        cost_estimate=pl.CostEstimate(
            flops=8 * 4 * 2 * 192 * 192 * 384, bytes_accessed=5 << 20, transcendentals=0
        ),
    )(
        held(beam_weights[0], pltpu.HBM),
        dish_order.reshape(1, dishes),
        slots_of(devices),
        held(jnp.asarray(table), pltpu.HBM),
    )
    arrived, early, late, table = lax.optimization_barrier((arrived, early, late, table))

    block = (6 * band_chans, channels)
    filtered, middle = pl.pallas_call(
        channel_kernel,
        out_shape=[
            jax.ShapeDtypeStruct((devices,) + block, F32),
            jax.ShapeDtypeStruct((late.shape[0] - LAST,) + late.shape[1:], BF16),
        ],
        in_specs=[VMEM] * 4 + [HBM],
        out_specs=[VMEM] * 2,
        scratch_shapes=[
            pltpu.VMEM((frames + prototype.shape[0] - 1, 24, LANES), F32),
            pltpu.VMEM((frames, 24, 2 * LANES), F32),
            pltpu.VMEM((frames + fir_count - 1, 24, 2 * LANES), F32),
            pltpu.VMEM((frames * 24, LANES), F32),
            pltpu.SemaphoreType.DMA(()),
        ],
        name="channels",
        compiler_params=GRANT,
    )(
        held(arrived, pltpu.VMEM),
        prototype,
        held(table, pltpu.VMEM),
        taps,
        held(late, pltpu.HBM),
    )
    field = exchange(filtered).reshape(devices * 6 * band_chans, channels)

    power_shape = (band_chans, frames // INTEG, beams)
    power = pl.pallas_call(
        beams_kernel,
        out_shape=pltpu.HBM(power_shape, F32),
        in_specs=[VMEM] * 3 + [HBM],
        out_specs=HBM,
        scratch_shapes=[
            pltpu.VMEM((LAST,) + late.shape[1:], BF16),
            pltpu.VMEM(power_shape, F32),
            pltpu.SemaphoreType.DMA((1 + band_chans // 2,)),
        ],
        name="beams",
        compiler_params=GRANT,
    )(
        held(field, pltpu.VMEM),
        held(early, pltpu.VMEM),
        held(middle, pltpu.VMEM),
        held(late, pltpu.HBM),
    )
    return jnp.transpose(power, (0, 2, 1))[None]


def detect(weights, field_real, field_imag):
    def contract(weight_part, field_part):
        return jnp.einsum("qds,dqf->qsf", weight_part, field_part, precision=HIGHEST)

    beam_real = contract(weights[:, 0], field_real) - contract(weights[:, 1], field_imag)
    beam_imag = contract(weights[:, 0], field_imag) + contract(weights[:, 1], field_real)
    energy = beam_real * beam_real + beam_imag * beam_imag
    shaped = energy.reshape(energy.shape[:-1] + (energy.shape[-1] // INTEG, INTEG))
    return jnp.mean(shaped, axis=-1)


def wide_body(samples, prototype, dish_filter, beam_weights, dish_order):
    devices = lax.axis_size("band")
    position = lax.axis_index("band")
    pfb_count, channels = prototype.shape
    fir_count = dish_filter.shape[1]
    dishes = dish_filter.shape[2]
    band_chans = beam_weights.shape[1]
    bands = channels // band_chans
    owners = devices // bands
    frames_dev = samples.shape[2] // channels
    frames = frames_dev * devices
    share = -(-dishes // devices)
    extra = share * devices - dishes

    padded = jnp.pad(samples, ((0, 0), (0, extra), (0, 0)))
    pieces = padded.reshape(2, devices, share, frames_dev, channels)
    pieces = jnp.transpose(pieces, (1, 3, 0, 2, 4)).reshape(
        devices, frames_dev, 2 * share, channels
    )
    arrived = lax.all_to_all(pieces, "band", split_axis=0, concat_axis=0, tiled=True)
    blocks = arrived.reshape(frames, 2 * share, channels)

    history = jnp.pad(blocks, ((pfb_count - 1, 0), (0, 0), (0, 0)))
    polyphase = jnp.zeros_like(blocks)
    for tap_index in range(pfb_count):
        offset = pfb_count - 1 - tap_index
        polyphase = polyphase + prototype[tap_index] * history[offset : offset + frames]
    cosine, sine = fourier_tables(channels)
    both = jnp.dot(polyphase, jnp.concatenate([cosine, sine], axis=1), precision=HIGHEST)
    with_cos = both[..., :channels].reshape(frames, 2, share, channels)
    with_sin = both[..., channels:].reshape(frames, 2, share, channels)
    spec_real = with_cos[:, 0] + with_sin[:, 1]
    spec_imag = with_cos[:, 1] - with_sin[:, 0]

    taps = jnp.pad(dish_filter, ((0, 0), (0, 0), (0, extra), (0, 0)))
    taps = lax.dynamic_slice_in_dim(taps, position * share, share, 2)
    lead = ((fir_count - 1, 0), (0, 0), (0, 0))
    past_real, past_imag = jnp.pad(spec_real, lead), jnp.pad(spec_imag, lead)
    out_real = jnp.zeros_like(spec_real)
    out_imag = jnp.zeros_like(spec_imag)
    for tap_index in range(fir_count):
        offset = fir_count - 1 - tap_index
        part_real = past_real[offset : offset + frames]
        part_imag = past_imag[offset : offset + frames]
        factor_real, factor_imag = taps[0, tap_index], taps[1, tap_index]
        out_real = out_real + factor_real * part_real - factor_imag * part_imag
        out_imag = out_imag + factor_real * part_imag + factor_imag * part_real

    filtered = jnp.stack([out_real, out_imag])
    filtered = filtered.reshape(2, frames, share, bands, band_chans)
    filtered = jnp.transpose(filtered, (3, 0, 2, 4, 1)).reshape(
        bands, 2 * share, band_chans * frames
    )
    filtered = jnp.repeat(filtered, owners, axis=0)
    field = lax.all_to_all(filtered, "band", split_axis=0, concat_axis=0, tiled=True)
    field = field.reshape(devices, 2, share, band_chans, frames)
    field = jnp.transpose(field, (1, 0, 2, 3, 4))
    field = field.reshape(2, devices * share, band_chans, frames)
    field = jnp.take(field, dish_order, axis=1)
    power = detect(beam_weights[0], field[0], field[1])
    return power[None]


def solution(mesh):
    devices = mesh.shape["band"]

    def body(samples, prototype, dish_filter, beam_weights, dish_order):
        channels = prototype.shape[1]
        close = (
            channels == LANES
            and beam_weights.shape[1] == 8
            and devices * 8 == channels
            and dish_filter.shape[2] == 12 * devices
            and samples.shape[2] * devices == 32 * channels
        )
        chosen = close_body if close else wide_body
        return chosen(samples, prototype, dish_filter, beam_weights, dish_order)

    placed = (P(None, None, ("grp", "band")), P(), P(), P("band", None, None, None, None), P())
    return jax.shard_map(
        body,
        mesh=mesh,
        in_specs=placed,
        out_specs=P(("grp", "band"), None, None, None),
        check_vma=False,
    )
```

```python
import math

import jax
import jax.numpy as jnp
import numpy as np
from jax import lax
from jax.experimental import pallas as pl
from jax.experimental.pallas import tpu as pltpu
from jax.sharding import PartitionSpec as P

INTEG = 4
EARLY = 2
HIGHEST = lax.Precision.HIGHEST
F32 = jnp.float32
BF16 = jnp.bfloat16
LANES = 128
VMEM = pl.BlockSpec(memory_space=pltpu.VMEM)
HBM = pl.BlockSpec(memory_space=pltpu.HBM)
GRANT = pltpu.CompilerParams(vmem_limit_bytes=16 << 20)


def fourier_tables(length):
    counter = jnp.arange(length, dtype=jnp.int32)
    product = counter[:, None] * counter[None, :] % length
    angles = product.astype(jnp.float32) * (2.0 * math.pi / length)
    factor = 1.0 / math.sqrt(length)
    return (jnp.cos(angles) * factor, jnp.sin(angles) * factor)


held = pltpu.with_memory_space_constraint


def split(value):
    high = value.astype(BF16)
    return high, (value - high.astype(F32)).astype(BF16)


def share_row(part, dish):
    return part * 8 + dish if dish < 8 else 16 + part * 4 + dish - 8


def pieces_kernel(x_ref, out_ref):
    devices, frames_dev = out_ref.shape[:2]
    low = lax.broadcasted_iota(jnp.int32, (8, LANES), 0) < 4
    for frame in range(frames_dev):
        lanes = slice(frame * LANES, (frame + 1) * LANES)
        for dev in range(0, devices, 2):
            for one in (dev, dev + 1):
                for part in range(2):
                    out_ref[one, frame, part * 8 : part * 8 + 8, :] = x_ref[
                        part, one * 8 : one * 8 + 8, lanes
                    ]
            start = devices * 8 + dev * 4
            real = x_ref[0, start : start + 8, lanes]
            imag = x_ref[1, start : start + 8, lanes]
            out_ref[dev, frame, 16:24, :] = jnp.where(low, real, pltpu.roll(imag, 4, 0))
            out_ref[dev + 1, frame, 16:24, :] = jnp.where(low, pltpu.roll(real, 4, 0), imag)


def weights_kernel(
    w_ref, order_ref, slot_ref, table_ref, early_ref, late_ref, table_out_ref, *scratch
):
    buffer, made, sems, table_sem = scratch
    table_copy = pltpu.make_async_copy(table_ref, table_out_ref, table_sem)
    loads = [
        pltpu.make_async_copy(w_ref.at[chan], buffer.at[chan], sems.at[0, chan])
        for chan in range(w_ref.shape[0])
    ]
    stores = [
        pltpu.make_async_copy(made.at[chan], late_ref.at[chan], sems.at[1, chan])
        for chan in range(late_ref.shape[0])
    ]
    ahead = 3
    for load in loads[:ahead]:
        load.start()
    hot = (slot_ref[...] == order_ref[...]).astype(F32).T.astype(BF16)
    beams = w_ref.shape[3]
    for chan, load in enumerate(loads):
        load.wait()
        if chan + ahead < len(loads):
            loads[chan + ahead].start()
        elif chan + ahead == len(loads):
            table_copy.start()
        for part in range(2):
            halves = [
                jnp.dot(half, hot, preferred_element_type=F32).astype(BF16)
                for half in split(buffer[chan, part].T)
            ]
            rows = slice(part * beams, (part + 1) * beams)
            both = jnp.concatenate(halves, axis=1)
            if chan < EARLY:
                early_ref[chan, rows, :] = both
            else:
                made[chan - EARLY, rows, :] = both
        if chan >= EARLY:
            stores[chan - EARLY].start()
    for store in stores:
        store.wait()
    table_copy.wait()


def channel_kernel(
    x_ref, proto_ref, table_ref, taps_ref, late_ref, out_ref, late_out_ref, *scratch
):
    past, poly, spec, filt, late_sem = scratch
    late_copy = pltpu.make_async_copy(late_ref, late_out_ref, late_sem)
    late_copy.start()
    pfb_count = proto_ref.shape[0]
    fir_count = taps_ref.shape[0]
    frames = poly.shape[0]
    group = 8
    low = lax.broadcasted_iota(jnp.int32, (group, 8, LANES), 1) < 4

    past[0 : pfb_count - 1] = jnp.zeros((pfb_count - 1, 24, LANES), F32)
    past[pfb_count - 1 :] = x_ref[...]

    spec[0 : fir_count - 1] = jnp.zeros((fir_count - 1, 24, 2 * LANES), F32)
    for first in range(0, frames, group):
        found = []
        for rows in range(0, 24, 8):
            total = None
            for tap in range(pfb_count):
                begin = first + pfb_count - 1 - tap
                block = past[begin : begin + group, rows : rows + 8, :]
                term = block * proto_ref[tap : tap + 1, :][None]
                total = term if total is None else total + term
            found.append(total)
        turned = pltpu.roll(found[2], 4, 1)
        other = [found[1], -found[0], jnp.where(low, turned, -turned)]
        for index in range(3):
            rows = slice(index * 8, index * 8 + 8)
            poly[first : first + group, rows, 0:LANES] = found[index]
            poly[first : first + group, rows, LANES : 2 * LANES] = other[index]

    for first in range(0, frames, group):
        value = poly[first : first + group].reshape(group * 24, 2 * LANES)
        high, rest = split(value)
        stacked = jnp.concatenate([high, rest, high], axis=1)
        product = jnp.dot(stacked, table_ref[...], preferred_element_type=F32)
        begin = first + fir_count - 1
        spec[begin : begin + group] = product.reshape(group, 24, 2 * LANES)

    for rows in range(0, 24, 8):
        for first in range(0, frames, group):
            total = None
            for tap in range(fir_count):
                begin = first + fir_count - 1 - tap
                near = spec[begin : begin + group, rows : rows + 8, 0:LANES]
                cross = spec[begin : begin + group, rows : rows + 8, LANES : 2 * LANES]
                term = taps_ref[tap, 0, rows : rows + 8, :][None] * near
                term = term + taps_ref[tap, 1, rows : rows + 8, :][None] * cross
                total = term if total is None else total + term
            for frame in range(group):
                begin = (first + frame) * 24 + rows
                filt[begin : begin + 8, :] = total[frame]

    per_band = out_ref.shape[1] // 6
    for pair in range(6):
        rows = [
            filt[pl.ds(share_row(part, pair * 2 + odd), frames, stride=24), :]
            for part in range(2)
            for odd in range(2)
        ]
        turned = jnp.concatenate(rows, axis=0).T
        for dev in range(out_ref.shape[0]):
            out_ref[dev, pair * per_band : (pair + 1) * per_band, :] = turned[
                dev * per_band : (dev + 1) * per_band
            ]
    late_copy.wait()


def beams_kernel(x_ref, early_ref, late_ref, out_ref):
    rows = x_ref.shape[0] // 8
    beams = early_ref.shape[1] // 2
    lane = lax.broadcasted_iota(jnp.int32, (rows, LANES), 1)
    even = lane % 64 < 32
    wide = lax.broadcasted_iota(jnp.int32, (beams, LANES), 1)
    even_wide = wide % 64 < 32
    row = lax.broadcasted_iota(jnp.int32, (16, 2 * LANES), 0)
    column = lax.broadcasted_iota(jnp.int32, (16, 2 * LANES), 1)
    pool = jnp.where(row == column % 64 // INTEG, 1.0 / INTEG, 0.0).astype(BF16)
    steps = range(out_ref.shape[0] // 2)
    fields = []
    for step in steps:
        one = x_ref[pl.ds(2 * step, rows, stride=8), :]
        two = x_ref[pl.ds(2 * step + 1, rows, stride=8), :]
        first = jnp.where(even, one, pltpu.roll(two, 32, 1))
        second = jnp.where(even, pltpu.roll(one, LANES - 32, 1), two)
        both = jnp.concatenate(split(jnp.concatenate([first, second], axis=0)), axis=1)
        fields.append(jnp.concatenate([both, both], axis=0))
    beam_of = []
    for step in steps:
        if 2 * step < EARLY:
            w_ref, begin = early_ref, 2 * step
        else:
            w_ref, begin = late_ref, 2 * step - EARLY
        pair = w_ref[begin : begin + 2].reshape(4 * beams, w_ref.shape[2])
        product = jnp.dot(pair, fields[step], preferred_element_type=F32)
        sums = product[:, 0:LANES] + product[:, LANES : 2 * LANES]
        by_real = jnp.where(even_wide, sums[:beams], sums[2 * beams : 3 * beams])
        by_imag = jnp.where(even_wide, sums[beams : 2 * beams], sums[3 * beams :])
        crossed = pltpu.roll(by_imag, 64, 1)
        beam_of.append(by_real + jnp.where(wide < 64, -crossed, crossed))
    for step in steps:
        power = lax.dot_general(
            pool,
            jnp.concatenate(split(beam_of[step] * beam_of[step]), axis=1),
            (((1,), (1,)), ((), ())),
            preferred_element_type=F32,
        )
        out_ref[2 * step] = power[0:8]
        out_ref[2 * step + 1] = power[8:16]


def slots_of(devices):
    index = np.arange(devices * 12, dtype=np.int32)
    own = index % 6 * 2 + index // (devices * 6)
    source = index // 6 % devices
    dishes = np.where(own < 8, source * 8 + own, devices * 8 + source * 4 + own - 8)
    return dishes.astype(np.int32)[:, None]


def dft_parts(channels):
    index = np.arange(channels)
    angle = 2.0 * np.pi * (index[:, None] * index[None, :] % channels) / channels
    cosine = np.cos(angle) / np.sqrt(channels)
    sine = np.sin(angle) / np.sqrt(channels)
    table = np.block([[cosine, sine], [sine, -cosine]]).astype(np.float32)
    high = table.astype(jnp.bfloat16)
    rest = (table - high.astype(np.float32)).astype(jnp.bfloat16)
    return np.concatenate([high, high, rest], axis=0)


def close_body(samples, prototype, dish_filter, beam_weights, dish_order):
    devices = lax.axis_size("band")
    position = lax.axis_index("band")
    channels = prototype.shape[1]
    fir_count = dish_filter.shape[1]
    dishes = dish_filter.shape[2]
    band_chans = beam_weights.shape[1]
    beams = beam_weights.shape[4]
    frames_dev = samples.shape[2] // channels
    frames = frames_dev * devices

    def exchange(value):
        return lax.all_to_all(value, "band", split_axis=0, concat_axis=0, tiled=True)

    pieces = pl.pallas_call(
        pieces_kernel,
        out_shape=jax.ShapeDtypeStruct((devices, frames_dev, 24, channels), F32),
        in_specs=[VMEM],
        out_specs=VMEM,
        name="pieces",
        compiler_params=GRANT,
    )(samples)
    arrived = exchange(pieces).reshape(frames, 24, channels)

    eight = lax.dynamic_slice_in_dim(dish_filter, position * 8, 8, 2)
    four = lax.dynamic_slice_in_dim(dish_filter, devices * 8 + position * 4, 4, 2)
    taps = jnp.concatenate([eight, eight, four, four], axis=2)
    taps = jnp.transpose(taps, (1, 0, 2, 3))
    table = dft_parts(channels)
    early, late, table = pl.pallas_call(
        weights_kernel,
        out_shape=[
            jax.ShapeDtypeStruct((EARLY, 2 * beams, 2 * dishes), BF16),
            pltpu.HBM((band_chans - EARLY, 2 * beams, 2 * dishes), BF16),
            jax.ShapeDtypeStruct(table.shape, BF16),
        ],
        in_specs=[HBM, VMEM, VMEM, HBM],
        out_specs=[VMEM, HBM, VMEM],
        scratch_shapes=[
            pltpu.VMEM((band_chans, 2, dishes, beams), F32),
            pltpu.VMEM((band_chans - EARLY, 2 * beams, 2 * dishes), BF16),
            pltpu.SemaphoreType.DMA((2, band_chans)),
            pltpu.SemaphoreType.DMA(()),
        ],
        name="weights",
        compiler_params=GRANT,
        cost_estimate=pl.CostEstimate(
            flops=8 * 4 * 2 * 192 * 192 * 384, bytes_accessed=5 << 20, transcendentals=0
        ),
    )(
        held(beam_weights[0], pltpu.HBM),
        dish_order.reshape(1, dishes),
        slots_of(devices),
        held(jnp.asarray(table), pltpu.HBM),
    )
    arrived, early, late, table = lax.optimization_barrier((arrived, early, late, table))

    block = (6 * band_chans, channels)
    filtered, late = pl.pallas_call(
        channel_kernel,
        out_shape=[
            jax.ShapeDtypeStruct((devices,) + block, F32),
            jax.ShapeDtypeStruct(late.shape, BF16),
        ],
        in_specs=[VMEM] * 4 + [HBM],
        out_specs=[VMEM] * 2,
        scratch_shapes=[
            pltpu.VMEM((frames + prototype.shape[0] - 1, 24, LANES), F32),
            pltpu.VMEM((frames, 24, 2 * LANES), F32),
            pltpu.VMEM((frames + fir_count - 1, 24, 2 * LANES), F32),
            pltpu.VMEM((frames * 24, LANES), F32),
            pltpu.SemaphoreType.DMA(()),
        ],
        name="channels",
        compiler_params=GRANT,
    )(
        held(arrived, pltpu.VMEM),
        prototype,
        held(table, pltpu.VMEM),
        taps,
        held(late, pltpu.HBM),
    )
    field = exchange(filtered).reshape(devices * 6 * band_chans, channels)

    power = pl.pallas_call(
        beams_kernel,
        out_shape=jax.ShapeDtypeStruct((band_chans, frames // INTEG, beams), F32),
        in_specs=[VMEM] * 3,
        out_specs=VMEM,
        name="beams",
        compiler_params=GRANT,
    )(held(field, pltpu.VMEM), held(early, pltpu.VMEM), held(late, pltpu.VMEM))
    return jnp.transpose(power, (0, 2, 1))[None]


def detect(weights, field_real, field_imag):
    def contract(weight_part, field_part):
        return jnp.einsum("qds,dqf->qsf", weight_part, field_part, precision=HIGHEST)

    beam_real = contract(weights[:, 0], field_real) - contract(weights[:, 1], field_imag)
    beam_imag = contract(weights[:, 0], field_imag) + contract(weights[:, 1], field_real)
    energy = beam_real * beam_real + beam_imag * beam_imag
    shaped = energy.reshape(energy.shape[:-1] + (energy.shape[-1] // INTEG, INTEG))
    return jnp.mean(shaped, axis=-1)


def wide_body(samples, prototype, dish_filter, beam_weights, dish_order):
    devices = lax.axis_size("band")
    position = lax.axis_index("band")
    pfb_count, channels = prototype.shape
    fir_count = dish_filter.shape[1]
    dishes = dish_filter.shape[2]
    band_chans = beam_weights.shape[1]
    bands = channels // band_chans
    owners = devices // bands
    frames_dev = samples.shape[2] // channels
    frames = frames_dev * devices
    share = -(-dishes // devices)
    extra = share * devices - dishes

    padded = jnp.pad(samples, ((0, 0), (0, extra), (0, 0)))
    pieces = padded.reshape(2, devices, share, frames_dev, channels)
    pieces = jnp.transpose(pieces, (1, 3, 0, 2, 4)).reshape(
        devices, frames_dev, 2 * share, channels
    )
    arrived = lax.all_to_all(pieces, "band", split_axis=0, concat_axis=0, tiled=True)
    blocks = arrived.reshape(frames, 2 * share, channels)

    history = jnp.pad(blocks, ((pfb_count - 1, 0), (0, 0), (0, 0)))
    polyphase = jnp.zeros_like(blocks)
    for tap_index in range(pfb_count):
        offset = pfb_count - 1 - tap_index
        polyphase = polyphase + prototype[tap_index] * history[offset : offset + frames]
    cosine, sine = fourier_tables(channels)
    both = jnp.dot(polyphase, jnp.concatenate([cosine, sine], axis=1), precision=HIGHEST)
    with_cos = both[..., :channels].reshape(frames, 2, share, channels)
    with_sin = both[..., channels:].reshape(frames, 2, share, channels)
    spec_real = with_cos[:, 0] + with_sin[:, 1]
    spec_imag = with_cos[:, 1] - with_sin[:, 0]

    taps = jnp.pad(dish_filter, ((0, 0), (0, 0), (0, extra), (0, 0)))
    taps = lax.dynamic_slice_in_dim(taps, position * share, share, 2)
    lead = ((fir_count - 1, 0), (0, 0), (0, 0))
    past_real, past_imag = jnp.pad(spec_real, lead), jnp.pad(spec_imag, lead)
    out_real = jnp.zeros_like(spec_real)
    out_imag = jnp.zeros_like(spec_imag)
    for tap_index in range(fir_count):
        offset = fir_count - 1 - tap_index
        part_real = past_real[offset : offset + frames]
        part_imag = past_imag[offset : offset + frames]
        factor_real, factor_imag = taps[0, tap_index], taps[1, tap_index]
        out_real = out_real + factor_real * part_real - factor_imag * part_imag
        out_imag = out_imag + factor_real * part_imag + factor_imag * part_real

    filtered = jnp.stack([out_real, out_imag])
    filtered = filtered.reshape(2, frames, share, bands, band_chans)
    filtered = jnp.transpose(filtered, (3, 0, 2, 4, 1)).reshape(
        bands, 2 * share, band_chans * frames
    )
    filtered = jnp.repeat(filtered, owners, axis=0)
    field = lax.all_to_all(filtered, "band", split_axis=0, concat_axis=0, tiled=True)
    field = field.reshape(devices, 2, share, band_chans, frames)
    field = jnp.transpose(field, (1, 0, 2, 3, 4))
    field = field.reshape(2, devices * share, band_chans, frames)
    field = jnp.take(field, dish_order, axis=1)
    power = detect(beam_weights[0], field[0], field[1])
    return power[None]


def solution(mesh):
    devices = mesh.shape["band"]

    def body(samples, prototype, dish_filter, beam_weights, dish_order):
        channels = prototype.shape[1]
        close = (
            channels == LANES
            and beam_weights.shape[1] == 8
            and devices * 8 == channels
            and dish_filter.shape[2] == 12 * devices
            and samples.shape[2] * devices == 32 * channels
        )
        chosen = close_body if close else wide_body
        return chosen(samples, prototype, dish_filter, beam_weights, dish_order)

    placed = (P(None, None, ("grp", "band")), P(), P(), P("band", None, None, None, None), P())
    return jax.shard_map(
        body,
        mesh=mesh,
        in_specs=placed,
        out_specs=P(("grp", "band"), None, None, None),
        check_vma=False,
    )
```

```python
import math

import jax
import jax.numpy as jnp
import numpy as np
from jax import lax
from jax.experimental import pallas as pl
from jax.experimental.pallas import tpu as pltpu
from jax.sharding import PartitionSpec as P

INTEG = 4
EARLY = 2
HIGHEST = lax.Precision.HIGHEST
F32 = jnp.float32
BF16 = jnp.bfloat16
LANES = 128
VMEM = pl.BlockSpec(memory_space=pltpu.VMEM)
HBM = pl.BlockSpec(memory_space=pltpu.HBM)
GRANT = pltpu.CompilerParams(vmem_limit_bytes=16 << 20)


def fourier_tables(length):
    counter = jnp.arange(length, dtype=jnp.int32)
    product = counter[:, None] * counter[None, :] % length
    angles = product.astype(jnp.float32) * (2.0 * math.pi / length)
    factor = 1.0 / math.sqrt(length)
    return (jnp.cos(angles) * factor, jnp.sin(angles) * factor)


held = pltpu.with_memory_space_constraint


def split(value):
    high = value.astype(BF16)
    return high, (value - high.astype(F32)).astype(BF16)


def share_row(part, dish):
    return part * 8 + dish if dish < 8 else 16 + part * 4 + dish - 8


def pieces_kernel(x_ref, out_ref):
    devices, frames_dev = out_ref.shape[:2]
    low = lax.broadcasted_iota(jnp.int32, (8, LANES), 0) < 4
    for frame in range(frames_dev):
        lanes = slice(frame * LANES, (frame + 1) * LANES)
        for dev in range(0, devices, 2):
            for one in (dev, dev + 1):
                for part in range(2):
                    out_ref[one, frame, part * 8 : part * 8 + 8, :] = x_ref[
                        part, one * 8 : one * 8 + 8, lanes
                    ]
            start = devices * 8 + dev * 4
            real = x_ref[0, start : start + 8, lanes]
            imag = x_ref[1, start : start + 8, lanes]
            out_ref[dev, frame, 16:24, :] = jnp.where(low, real, pltpu.roll(imag, 4, 0))
            out_ref[dev + 1, frame, 16:24, :] = jnp.where(low, pltpu.roll(real, 4, 0), imag)


def weights_kernel(
    w_ref, order_ref, slot_ref, table_ref, early_ref, late_ref, table_out_ref, *scratch
):
    buffer, made, sems, table_sem = scratch
    table_copy = pltpu.make_async_copy(table_ref, table_out_ref, table_sem)
    loads = [
        pltpu.make_async_copy(w_ref.at[chan], buffer.at[chan], sems.at[0, chan])
        for chan in range(w_ref.shape[0])
    ]
    stores = [
        pltpu.make_async_copy(made.at[chan], late_ref.at[chan], sems.at[1, chan])
        for chan in range(late_ref.shape[0])
    ]
    ahead = 3
    for load in loads[:ahead]:
        load.start()
    hot = (slot_ref[...] == order_ref[...]).astype(F32).T.astype(BF16)
    beams = w_ref.shape[3]
    for chan, load in enumerate(loads):
        load.wait()
        if chan + ahead < len(loads):
            loads[chan + ahead].start()
        elif chan + ahead == len(loads):
            table_copy.start()
        for part in range(2):
            halves = [
                jnp.dot(half, hot, preferred_element_type=F32).astype(BF16)
                for half in split(buffer[chan, part].T)
            ]
            rows = slice(part * beams, (part + 1) * beams)
            both = jnp.concatenate(halves, axis=1)
            if chan < EARLY:
                early_ref[chan, rows, :] = both
            else:
                made[chan - EARLY, rows, :] = both
        if chan >= EARLY:
            stores[chan - EARLY].start()
    for store in stores:
        store.wait()
    table_copy.wait()


def channel_kernel(
    x_ref, proto_ref, table_ref, taps_ref, late_ref, out_ref, late_out_ref, *scratch
):
    past, poly, spec, filt, late_sems = scratch
    late_copies = [
        pltpu.make_async_copy(late_ref.at[chan], late_out_ref.at[chan], late_sems.at[chan])
        for chan in range(late_ref.shape[0])
    ]
    for copy in late_copies:
        copy.start()
    pfb_count = proto_ref.shape[0]
    fir_count = taps_ref.shape[0]
    frames = poly.shape[0]
    group = 8
    low = lax.broadcasted_iota(jnp.int32, (group, 8, LANES), 1) < 4

    past[0 : pfb_count - 1] = jnp.zeros((pfb_count - 1, 24, LANES), F32)
    past[pfb_count - 1 :] = x_ref[...]

    spec[0 : fir_count - 1] = jnp.zeros((fir_count - 1, 24, 2 * LANES), F32)
    for first in range(0, frames, group):
        found = []
        for rows in range(0, 24, 8):
            total = None
            for tap in range(pfb_count):
                begin = first + pfb_count - 1 - tap
                block = past[begin : begin + group, rows : rows + 8, :]
                term = block * proto_ref[tap : tap + 1, :][None]
                total = term if total is None else total + term
            found.append(total)
        turned = pltpu.roll(found[2], 4, 1)
        other = [found[1], -found[0], jnp.where(low, turned, -turned)]
        for index in range(3):
            rows = slice(index * 8, index * 8 + 8)
            poly[first : first + group, rows, 0:LANES] = found[index]
            poly[first : first + group, rows, LANES : 2 * LANES] = other[index]

    for first in range(0, frames, group):
        value = poly[first : first + group].reshape(group * 24, 2 * LANES)
        high, rest = split(value)
        stacked = jnp.concatenate([high, rest, high], axis=1)
        product = jnp.dot(stacked, table_ref[...], preferred_element_type=F32)
        begin = first + fir_count - 1
        spec[begin : begin + group] = product.reshape(group, 24, 2 * LANES)

    for rows in range(0, 24, 8):
        for first in range(0, frames, group):
            total = None
            for tap in range(fir_count):
                begin = first + fir_count - 1 - tap
                near = spec[begin : begin + group, rows : rows + 8, 0:LANES]
                cross = spec[begin : begin + group, rows : rows + 8, LANES : 2 * LANES]
                term = taps_ref[tap, 0, rows : rows + 8, :][None] * near
                term = term + taps_ref[tap, 1, rows : rows + 8, :][None] * cross
                total = term if total is None else total + term
            for frame in range(group):
                begin = (first + frame) * 24 + rows
                filt[begin : begin + 8, :] = total[frame]

    per_band = out_ref.shape[1] // 6
    for pair in range(6):
        rows = [
            filt[pl.ds(share_row(part, pair * 2 + odd), frames, stride=24), :]
            for part in range(2)
            for odd in range(2)
        ]
        turned = jnp.concatenate(rows, axis=0).T
        for dev in range(out_ref.shape[0]):
            out_ref[dev, pair * per_band : (pair + 1) * per_band, :] = turned[
                dev * per_band : (dev + 1) * per_band
            ]
    for copy in late_copies:
        copy.wait()


def beams_kernel(x_ref, early_ref, late_ref, out_ref):
    rows = x_ref.shape[0] // 8
    beams = early_ref.shape[1] // 2
    lane = lax.broadcasted_iota(jnp.int32, (rows, LANES), 1)
    even = lane % 64 < 32
    wide = lax.broadcasted_iota(jnp.int32, (beams, LANES), 1)
    even_wide = wide % 64 < 32
    row = lax.broadcasted_iota(jnp.int32, (16, 2 * LANES), 0)
    column = lax.broadcasted_iota(jnp.int32, (16, 2 * LANES), 1)
    pool = jnp.where(row == column % 64 // INTEG, 1.0 / INTEG, 0.0).astype(BF16)
    steps = range(out_ref.shape[0] // 2)
    fields = []
    for step in steps:
        one = x_ref[pl.ds(2 * step, rows, stride=8), :]
        two = x_ref[pl.ds(2 * step + 1, rows, stride=8), :]
        first = jnp.where(even, one, pltpu.roll(two, 32, 1))
        second = jnp.where(even, pltpu.roll(one, LANES - 32, 1), two)
        both = jnp.concatenate(split(jnp.concatenate([first, second], axis=0)), axis=1)
        fields.append(jnp.concatenate([both, both], axis=0))
    beam_of = []
    for step in steps:
        if 2 * step < EARLY:
            w_ref, begin = early_ref, 2 * step
        else:
            w_ref, begin = late_ref, 2 * step - EARLY
        sums = []
        for index in range(2):
            weights = w_ref[begin + index]
            product = jnp.dot(weights, fields[step], preferred_element_type=F32)
            sums.append(product[:, 0:LANES] + product[:, LANES : 2 * LANES])
        by_real = jnp.where(even_wide, sums[0][:beams], sums[1][:beams])
        by_imag = jnp.where(even_wide, sums[0][beams:], sums[1][beams:])
        crossed = pltpu.roll(by_imag, 64, 1)
        beam_of.append(by_real + jnp.where(wide < 64, -crossed, crossed))
    for step in steps:
        power = lax.dot_general(
            pool,
            jnp.concatenate(split(beam_of[step] * beam_of[step]), axis=1),
            (((1,), (1,)), ((), ())),
            preferred_element_type=F32,
        )
        out_ref[2 * step] = power[0:8]
        out_ref[2 * step + 1] = power[8:16]


def slots_of(devices):
    index = np.arange(devices * 12, dtype=np.int32)
    own = index % 6 * 2 + index // (devices * 6)
    source = index // 6 % devices
    dishes = np.where(own < 8, source * 8 + own, devices * 8 + source * 4 + own - 8)
    return dishes.astype(np.int32)[:, None]


def dft_parts(channels):
    index = np.arange(channels)
    angle = 2.0 * np.pi * (index[:, None] * index[None, :] % channels) / channels
    cosine = np.cos(angle) / np.sqrt(channels)
    sine = np.sin(angle) / np.sqrt(channels)
    table = np.block([[cosine, sine], [sine, -cosine]]).astype(np.float32)
    high = table.astype(jnp.bfloat16)
    rest = (table - high.astype(np.float32)).astype(jnp.bfloat16)
    return np.concatenate([high, high, rest], axis=0)


def close_body(samples, prototype, dish_filter, beam_weights, dish_order):
    devices = lax.axis_size("band")
    position = lax.axis_index("band")
    channels = prototype.shape[1]
    fir_count = dish_filter.shape[1]
    dishes = dish_filter.shape[2]
    band_chans = beam_weights.shape[1]
    beams = beam_weights.shape[4]
    frames_dev = samples.shape[2] // channels
    frames = frames_dev * devices

    def exchange(value):
        return lax.all_to_all(value, "band", split_axis=0, concat_axis=0, tiled=True)

    pieces = pl.pallas_call(
        pieces_kernel,
        out_shape=jax.ShapeDtypeStruct((devices, frames_dev, 24, channels), F32),
        in_specs=[VMEM],
        out_specs=VMEM,
        name="pieces",
        compiler_params=GRANT,
    )(samples)
    arrived = exchange(pieces).reshape(frames, 24, channels)

    eight = lax.dynamic_slice_in_dim(dish_filter, position * 8, 8, 2)
    four = lax.dynamic_slice_in_dim(dish_filter, devices * 8 + position * 4, 4, 2)
    taps = jnp.concatenate([eight, eight, four, four], axis=2)
    taps = jnp.transpose(taps, (1, 0, 2, 3))
    table = dft_parts(channels)
    early, late, table = pl.pallas_call(
        weights_kernel,
        out_shape=[
            jax.ShapeDtypeStruct((EARLY, 2 * beams, 2 * dishes), BF16),
            pltpu.HBM((band_chans - EARLY, 2 * beams, 2 * dishes), BF16),
            jax.ShapeDtypeStruct(table.shape, BF16),
        ],
        in_specs=[HBM, VMEM, VMEM, HBM],
        out_specs=[VMEM, HBM, VMEM],
        scratch_shapes=[
            pltpu.VMEM((band_chans, 2, dishes, beams), F32),
            pltpu.VMEM((band_chans - EARLY, 2 * beams, 2 * dishes), BF16),
            pltpu.SemaphoreType.DMA((2, band_chans)),
            pltpu.SemaphoreType.DMA(()),
        ],
        name="weights",
        compiler_params=GRANT,
        cost_estimate=pl.CostEstimate(
            flops=8 * 4 * 2 * 192 * 192 * 384, bytes_accessed=5 << 20, transcendentals=0
        ),
    )(
        held(beam_weights[0], pltpu.HBM),
        dish_order.reshape(1, dishes),
        slots_of(devices),
        held(jnp.asarray(table), pltpu.HBM),
    )
    arrived, early, late, table = lax.optimization_barrier((arrived, early, late, table))

    block = (6 * band_chans, channels)
    filtered, late = pl.pallas_call(
        channel_kernel,
        out_shape=[
            jax.ShapeDtypeStruct((devices,) + block, F32),
            jax.ShapeDtypeStruct(late.shape, BF16),
        ],
        in_specs=[VMEM] * 4 + [HBM],
        out_specs=[VMEM] * 2,
        scratch_shapes=[
            pltpu.VMEM((frames + prototype.shape[0] - 1, 24, LANES), F32),
            pltpu.VMEM((frames, 24, 2 * LANES), F32),
            pltpu.VMEM((frames + fir_count - 1, 24, 2 * LANES), F32),
            pltpu.VMEM((frames * 24, LANES), F32),
            pltpu.SemaphoreType.DMA((late.shape[0],)),
        ],
        name="channels",
        compiler_params=GRANT,
    )(
        held(arrived, pltpu.VMEM),
        prototype,
        held(table, pltpu.VMEM),
        taps,
        held(late, pltpu.HBM),
    )
    field = exchange(filtered).reshape(devices * 6 * band_chans, channels)

    power = pl.pallas_call(
        beams_kernel,
        out_shape=jax.ShapeDtypeStruct((band_chans, frames // INTEG, beams), F32),
        in_specs=[VMEM] * 3,
        out_specs=VMEM,
        name="beams",
        compiler_params=GRANT,
    )(held(field, pltpu.VMEM), held(early, pltpu.VMEM), held(late, pltpu.VMEM))
    return jnp.transpose(power, (0, 2, 1))[None]


def detect(weights, field_real, field_imag):
    def contract(weight_part, field_part):
        return jnp.einsum("qds,dqf->qsf", weight_part, field_part, precision=HIGHEST)

    beam_real = contract(weights[:, 0], field_real) - contract(weights[:, 1], field_imag)
    beam_imag = contract(weights[:, 0], field_imag) + contract(weights[:, 1], field_real)
    energy = beam_real * beam_real + beam_imag * beam_imag
    shaped = energy.reshape(energy.shape[:-1] + (energy.shape[-1] // INTEG, INTEG))
    return jnp.mean(shaped, axis=-1)


def wide_body(samples, prototype, dish_filter, beam_weights, dish_order):
    devices = lax.axis_size("band")
    position = lax.axis_index("band")
    pfb_count, channels = prototype.shape
    fir_count = dish_filter.shape[1]
    dishes = dish_filter.shape[2]
    band_chans = beam_weights.shape[1]
    bands = channels // band_chans
    owners = devices // bands
    frames_dev = samples.shape[2] // channels
    frames = frames_dev * devices
    share = -(-dishes // devices)
    extra = share * devices - dishes

    padded = jnp.pad(samples, ((0, 0), (0, extra), (0, 0)))
    pieces = padded.reshape(2, devices, share, frames_dev, channels)
    pieces = jnp.transpose(pieces, (1, 3, 0, 2, 4)).reshape(
        devices, frames_dev, 2 * share, channels
    )
    arrived = lax.all_to_all(pieces, "band", split_axis=0, concat_axis=0, tiled=True)
    blocks = arrived.reshape(frames, 2 * share, channels)

    history = jnp.pad(blocks, ((pfb_count - 1, 0), (0, 0), (0, 0)))
    polyphase = jnp.zeros_like(blocks)
    for tap_index in range(pfb_count):
        offset = pfb_count - 1 - tap_index
        polyphase = polyphase + prototype[tap_index] * history[offset : offset + frames]
    cosine, sine = fourier_tables(channels)
    both = jnp.dot(polyphase, jnp.concatenate([cosine, sine], axis=1), precision=HIGHEST)
    with_cos = both[..., :channels].reshape(frames, 2, share, channels)
    with_sin = both[..., channels:].reshape(frames, 2, share, channels)
    spec_real = with_cos[:, 0] + with_sin[:, 1]
    spec_imag = with_cos[:, 1] - with_sin[:, 0]

    taps = jnp.pad(dish_filter, ((0, 0), (0, 0), (0, extra), (0, 0)))
    taps = lax.dynamic_slice_in_dim(taps, position * share, share, 2)
    lead = ((fir_count - 1, 0), (0, 0), (0, 0))
    past_real, past_imag = jnp.pad(spec_real, lead), jnp.pad(spec_imag, lead)
    out_real = jnp.zeros_like(spec_real)
    out_imag = jnp.zeros_like(spec_imag)
    for tap_index in range(fir_count):
        offset = fir_count - 1 - tap_index
        part_real = past_real[offset : offset + frames]
        part_imag = past_imag[offset : offset + frames]
        factor_real, factor_imag = taps[0, tap_index], taps[1, tap_index]
        out_real = out_real + factor_real * part_real - factor_imag * part_imag
        out_imag = out_imag + factor_real * part_imag + factor_imag * part_real

    filtered = jnp.stack([out_real, out_imag])
    filtered = filtered.reshape(2, frames, share, bands, band_chans)
    filtered = jnp.transpose(filtered, (3, 0, 2, 4, 1)).reshape(
        bands, 2 * share, band_chans * frames
    )
    filtered = jnp.repeat(filtered, owners, axis=0)
    field = lax.all_to_all(filtered, "band", split_axis=0, concat_axis=0, tiled=True)
    field = field.reshape(devices, 2, share, band_chans, frames)
    field = jnp.transpose(field, (1, 0, 2, 3, 4))
    field = field.reshape(2, devices * share, band_chans, frames)
    field = jnp.take(field, dish_order, axis=1)
    power = detect(beam_weights[0], field[0], field[1])
    return power[None]


def solution(mesh):
    devices = mesh.shape["band"]

    def body(samples, prototype, dish_filter, beam_weights, dish_order):
        channels = prototype.shape[1]
        close = (
            channels == LANES
            and beam_weights.shape[1] == 8
            and devices * 8 == channels
            and dish_filter.shape[2] == 12 * devices
            and samples.shape[2] * devices == 32 * channels
        )
        chosen = close_body if close else wide_body
        return chosen(samples, prototype, dish_filter, beam_weights, dish_order)

    placed = (P(None, None, ("grp", "band")), P(), P(), P("band", None, None, None, None), P())
    return jax.shard_map(
        body,
        mesh=mesh,
        in_specs=placed,
        out_specs=P(("grp", "band"), None, None, None),
        check_vma=False,
    )
```

```python
import math

import jax
import jax.numpy as jnp
import numpy as np
from jax import lax
from jax.experimental import pallas as pl
from jax.experimental.pallas import tpu as pltpu
from jax.sharding import PartitionSpec as P

INTEG = 4
EARLY = 2
HIGHEST = lax.Precision.HIGHEST
F32 = jnp.float32
BF16 = jnp.bfloat16
LANES = 128
VMEM = pl.BlockSpec(memory_space=pltpu.VMEM)
HBM = pl.BlockSpec(memory_space=pltpu.HBM)
GRANT = pltpu.CompilerParams(vmem_limit_bytes=16 << 20)


def fourier_tables(length):
    counter = jnp.arange(length, dtype=jnp.int32)
    product = counter[:, None] * counter[None, :] % length
    angles = product.astype(jnp.float32) * (2.0 * math.pi / length)
    factor = 1.0 / math.sqrt(length)
    return (jnp.cos(angles) * factor, jnp.sin(angles) * factor)


held = pltpu.with_memory_space_constraint


def split(value):
    high = value.astype(BF16)
    return high, (value - high.astype(F32)).astype(BF16)


def share_row(part, dish):
    return part * 8 + dish if dish < 8 else 16 + part * 4 + dish - 8


def pieces_kernel(x_hbm, out_hbm, x_ref, out_ref, sems):
    load = pltpu.make_async_copy(x_hbm, x_ref, sems.at[0])
    load.start()
    load.wait()
    devices, frames_dev = out_ref.shape[:2]
    low = lax.broadcasted_iota(jnp.int32, (8, LANES), 0) < 4
    for frame in range(frames_dev):
        lanes = slice(frame * LANES, (frame + 1) * LANES)
        for dev in range(0, devices, 2):
            for one in (dev, dev + 1):
                for part in range(2):
                    out_ref[one, frame, part * 8 : part * 8 + 8, :] = x_ref[
                        part, one * 8 : one * 8 + 8, lanes
                    ]
            start = devices * 8 + dev * 4
            real = x_ref[0, start : start + 8, lanes]
            imag = x_ref[1, start : start + 8, lanes]
            out_ref[dev, frame, 16:24, :] = jnp.where(low, real, pltpu.roll(imag, 4, 0))
            out_ref[dev + 1, frame, 16:24, :] = jnp.where(low, pltpu.roll(real, 4, 0), imag)
    store = pltpu.make_async_copy(out_ref, out_hbm, sems.at[1])
    store.start()
    store.wait()


def weights_kernel(
    w_ref, order_ref, slot_ref, table_ref, early_ref, late_ref, table_out_ref, *scratch
):
    buffer, made, sems, table_sem = scratch
    table_copy = pltpu.make_async_copy(table_ref, table_out_ref, table_sem)
    loads = [
        pltpu.make_async_copy(w_ref.at[chan], buffer.at[chan], sems.at[0, chan])
        for chan in range(w_ref.shape[0])
    ]
    stores = [
        pltpu.make_async_copy(made.at[chan], late_ref.at[chan], sems.at[1, chan])
        for chan in range(late_ref.shape[0])
    ]
    ahead = 3
    for load in loads[:ahead]:
        load.start()
    hot = (slot_ref[...] == order_ref[...]).astype(F32).T.astype(BF16)
    beams = w_ref.shape[3]
    for chan, load in enumerate(loads):
        load.wait()
        if chan + ahead < len(loads):
            loads[chan + ahead].start()
        elif chan + ahead == len(loads):
            table_copy.start()
        for part in range(2):
            halves = [
                jnp.dot(half, hot, preferred_element_type=F32).astype(BF16)
                for half in split(buffer[chan, part].T)
            ]
            rows = slice(part * beams, (part + 1) * beams)
            both = jnp.concatenate(halves, axis=1)
            if chan < EARLY:
                early_ref[chan, rows, :] = both
            else:
                made[chan - EARLY, rows, :] = both
        if chan >= EARLY:
            stores[chan - EARLY].start()
    for store in stores:
        store.wait()
    table_copy.wait()


def channel_kernel(
    x_ref, proto_ref, table_ref, taps_ref, late_ref, out_ref, late_out_ref, *scratch
):
    past, poly, spec, filt, late_sem = scratch
    late_copy = pltpu.make_async_copy(late_ref, late_out_ref, late_sem)
    late_copy.start()
    pfb_count = proto_ref.shape[0]
    fir_count = taps_ref.shape[0]
    frames = poly.shape[0]
    group = 8
    low = lax.broadcasted_iota(jnp.int32, (group, 8, LANES), 1) < 4

    past[0 : pfb_count - 1] = jnp.zeros((pfb_count - 1, 24, LANES), F32)
    past[pfb_count - 1 :] = x_ref[...]

    spec[0 : fir_count - 1] = jnp.zeros((fir_count - 1, 24, 2 * LANES), F32)
    for first in range(0, frames, group):
        found = []
        for rows in range(0, 24, 8):
            total = None
            for tap in range(pfb_count):
                begin = first + pfb_count - 1 - tap
                block = past[begin : begin + group, rows : rows + 8, :]
                term = block * proto_ref[tap : tap + 1, :][None]
                total = term if total is None else total + term
            found.append(total)
        turned = pltpu.roll(found[2], 4, 1)
        other = [found[1], -found[0], jnp.where(low, turned, -turned)]
        for index in range(3):
            rows = slice(index * 8, index * 8 + 8)
            poly[first : first + group, rows, 0:LANES] = found[index]
            poly[first : first + group, rows, LANES : 2 * LANES] = other[index]

    for first in range(0, frames, group):
        value = poly[first : first + group].reshape(group * 24, 2 * LANES)
        high, rest = split(value)
        stacked = jnp.concatenate([high, rest, high], axis=1)
        product = jnp.dot(stacked, table_ref[...], preferred_element_type=F32)
        begin = first + fir_count - 1
        spec[begin : begin + group] = product.reshape(group, 24, 2 * LANES)

    for rows in range(0, 24, 8):
        for first in range(0, frames, group):
            total = None
            for tap in range(fir_count):
                begin = first + fir_count - 1 - tap
                near = spec[begin : begin + group, rows : rows + 8, 0:LANES]
                cross = spec[begin : begin + group, rows : rows + 8, LANES : 2 * LANES]
                term = taps_ref[tap, 0, rows : rows + 8, :][None] * near
                term = term + taps_ref[tap, 1, rows : rows + 8, :][None] * cross
                total = term if total is None else total + term
            for frame in range(group):
                begin = (first + frame) * 24 + rows
                filt[begin : begin + 8, :] = total[frame]

    per_band = out_ref.shape[1] // 6
    for pair in range(6):
        rows = [
            filt[pl.ds(share_row(part, pair * 2 + odd), frames, stride=24), :]
            for part in range(2)
            for odd in range(2)
        ]
        turned = jnp.concatenate(rows, axis=0).T
        for dev in range(out_ref.shape[0]):
            out_ref[dev, pair * per_band : (pair + 1) * per_band, :] = turned[
                dev * per_band : (dev + 1) * per_band
            ]
    late_copy.wait()


def beams_kernel(x_ref, early_ref, late_ref, out_ref):
    rows = x_ref.shape[0] // 8
    beams = early_ref.shape[1] // 2
    lane = lax.broadcasted_iota(jnp.int32, (rows, LANES), 1)
    even = lane % 64 < 32
    wide = lax.broadcasted_iota(jnp.int32, (beams, LANES), 1)
    even_wide = wide % 64 < 32
    row = lax.broadcasted_iota(jnp.int32, (16, 2 * LANES), 0)
    column = lax.broadcasted_iota(jnp.int32, (16, 2 * LANES), 1)
    pool = jnp.where(row == column % 64 // INTEG, 1.0 / INTEG, 0.0).astype(BF16)
    steps = range(out_ref.shape[0] // 2)
    fields = []
    for step in steps:
        one = x_ref[pl.ds(2 * step, rows, stride=8), :]
        two = x_ref[pl.ds(2 * step + 1, rows, stride=8), :]
        first = jnp.where(even, one, pltpu.roll(two, 32, 1))
        second = jnp.where(even, pltpu.roll(one, LANES - 32, 1), two)
        both = jnp.concatenate(split(jnp.concatenate([first, second], axis=0)), axis=1)
        fields.append(jnp.concatenate([both, both], axis=0))
    beam_of = []
    for step in steps:
        if 2 * step < EARLY:
            w_ref, begin = early_ref, 2 * step
        else:
            w_ref, begin = late_ref, 2 * step - EARLY
        sums = []
        for index in range(2):
            weights = w_ref[begin + index]
            product = jnp.dot(weights, fields[step], preferred_element_type=F32)
            sums.append(product[:, 0:LANES] + product[:, LANES : 2 * LANES])
        by_real = jnp.where(even_wide, sums[0][:beams], sums[1][:beams])
        by_imag = jnp.where(even_wide, sums[0][beams:], sums[1][beams:])
        crossed = pltpu.roll(by_imag, 64, 1)
        beam_of.append(by_real + jnp.where(wide < 64, -crossed, crossed))
    for step in steps:
        power = lax.dot_general(
            pool,
            jnp.concatenate(split(beam_of[step] * beam_of[step]), axis=1),
            (((1,), (1,)), ((), ())),
            preferred_element_type=F32,
        )
        out_ref[2 * step] = power[0:8]
        out_ref[2 * step + 1] = power[8:16]


def slots_of(devices):
    index = np.arange(devices * 12, dtype=np.int32)
    own = index % 6 * 2 + index // (devices * 6)
    source = index // 6 % devices
    dishes = np.where(own < 8, source * 8 + own, devices * 8 + source * 4 + own - 8)
    return dishes.astype(np.int32)[:, None]


def dft_parts(channels):
    index = np.arange(channels)
    angle = 2.0 * np.pi * (index[:, None] * index[None, :] % channels) / channels
    cosine = np.cos(angle) / np.sqrt(channels)
    sine = np.sin(angle) / np.sqrt(channels)
    table = np.block([[cosine, sine], [sine, -cosine]]).astype(np.float32)
    high = table.astype(jnp.bfloat16)
    rest = (table - high.astype(np.float32)).astype(jnp.bfloat16)
    return np.concatenate([high, high, rest], axis=0)


def close_body(samples, prototype, dish_filter, beam_weights, dish_order):
    devices = lax.axis_size("band")
    position = lax.axis_index("band")
    channels = prototype.shape[1]
    fir_count = dish_filter.shape[1]
    dishes = dish_filter.shape[2]
    band_chans = beam_weights.shape[1]
    beams = beam_weights.shape[4]
    frames_dev = samples.shape[2] // channels
    frames = frames_dev * devices

    def exchange(value):
        return lax.all_to_all(value, "band", split_axis=0, concat_axis=0, tiled=True)

    pieces_shape = (devices, frames_dev, 24, channels)
    pieces = pl.pallas_call(
        pieces_kernel,
        out_shape=pltpu.HBM(pieces_shape, F32),
        in_specs=[HBM],
        out_specs=HBM,
        scratch_shapes=[
            pltpu.VMEM(samples.shape, F32),
            pltpu.VMEM(pieces_shape, F32),
            pltpu.SemaphoreType.DMA((2,)),
        ],
        name="pieces",
        compiler_params=GRANT,
    )(held(samples, pltpu.HBM))
    arrived = exchange(pieces).reshape(frames, 24, channels)

    eight = lax.dynamic_slice_in_dim(dish_filter, position * 8, 8, 2)
    four = lax.dynamic_slice_in_dim(dish_filter, devices * 8 + position * 4, 4, 2)
    taps = jnp.concatenate([eight, eight, four, four], axis=2)
    taps = jnp.transpose(taps, (1, 0, 2, 3))
    table = dft_parts(channels)
    early, late, table = pl.pallas_call(
        weights_kernel,
        out_shape=[
            jax.ShapeDtypeStruct((EARLY, 2 * beams, 2 * dishes), BF16),
            pltpu.HBM((band_chans - EARLY, 2 * beams, 2 * dishes), BF16),
            jax.ShapeDtypeStruct(table.shape, BF16),
        ],
        in_specs=[HBM, VMEM, VMEM, HBM],
        out_specs=[VMEM, HBM, VMEM],
        scratch_shapes=[
            pltpu.VMEM((band_chans, 2, dishes, beams), F32),
            pltpu.VMEM((band_chans - EARLY, 2 * beams, 2 * dishes), BF16),
            pltpu.SemaphoreType.DMA((2, band_chans)),
            pltpu.SemaphoreType.DMA(()),
        ],
        name="weights",
        compiler_params=GRANT,
        cost_estimate=pl.CostEstimate(
            flops=8 * 4 * 2 * 192 * 192 * 384, bytes_accessed=5 << 20, transcendentals=0
        ),
    )(
        held(beam_weights[0], pltpu.HBM),
        dish_order.reshape(1, dishes),
        slots_of(devices),
        held(jnp.asarray(table), pltpu.HBM),
    )
    arrived, early, late, table = lax.optimization_barrier((arrived, early, late, table))

    block = (6 * band_chans, channels)
    filtered, late = pl.pallas_call(
        channel_kernel,
        out_shape=[
            jax.ShapeDtypeStruct((devices,) + block, F32),
            jax.ShapeDtypeStruct(late.shape, BF16),
        ],
        in_specs=[VMEM] * 4 + [HBM],
        out_specs=[VMEM] * 2,
        scratch_shapes=[
            pltpu.VMEM((frames + prototype.shape[0] - 1, 24, LANES), F32),
            pltpu.VMEM((frames, 24, 2 * LANES), F32),
            pltpu.VMEM((frames + fir_count - 1, 24, 2 * LANES), F32),
            pltpu.VMEM((frames * 24, LANES), F32),
            pltpu.SemaphoreType.DMA(()),
        ],
        name="channels",
        compiler_params=GRANT,
    )(
        held(arrived, pltpu.VMEM),
        prototype,
        held(table, pltpu.VMEM),
        taps,
        held(late, pltpu.HBM),
    )
    field = exchange(filtered).reshape(devices * 6 * band_chans, channels)

    power = pl.pallas_call(
        beams_kernel,
        out_shape=jax.ShapeDtypeStruct((band_chans, frames // INTEG, beams), F32),
        in_specs=[VMEM] * 3,
        out_specs=VMEM,
        name="beams",
        compiler_params=GRANT,
    )(held(field, pltpu.VMEM), held(early, pltpu.VMEM), held(late, pltpu.VMEM))
    return jnp.transpose(power, (0, 2, 1))[None]


def detect(weights, field_real, field_imag):
    def contract(weight_part, field_part):
        return jnp.einsum("qds,dqf->qsf", weight_part, field_part, precision=HIGHEST)

    beam_real = contract(weights[:, 0], field_real) - contract(weights[:, 1], field_imag)
    beam_imag = contract(weights[:, 0], field_imag) + contract(weights[:, 1], field_real)
    energy = beam_real * beam_real + beam_imag * beam_imag
    shaped = energy.reshape(energy.shape[:-1] + (energy.shape[-1] // INTEG, INTEG))
    return jnp.mean(shaped, axis=-1)


def wide_body(samples, prototype, dish_filter, beam_weights, dish_order):
    devices = lax.axis_size("band")
    position = lax.axis_index("band")
    pfb_count, channels = prototype.shape
    fir_count = dish_filter.shape[1]
    dishes = dish_filter.shape[2]
    band_chans = beam_weights.shape[1]
    bands = channels // band_chans
    owners = devices // bands
    frames_dev = samples.shape[2] // channels
    frames = frames_dev * devices
    share = -(-dishes // devices)
    extra = share * devices - dishes

    padded = jnp.pad(samples, ((0, 0), (0, extra), (0, 0)))
    pieces = padded.reshape(2, devices, share, frames_dev, channels)
    pieces = jnp.transpose(pieces, (1, 3, 0, 2, 4)).reshape(
        devices, frames_dev, 2 * share, channels
    )
    arrived = lax.all_to_all(pieces, "band", split_axis=0, concat_axis=0, tiled=True)
    blocks = arrived.reshape(frames, 2 * share, channels)

    history = jnp.pad(blocks, ((pfb_count - 1, 0), (0, 0), (0, 0)))
    polyphase = jnp.zeros_like(blocks)
    for tap_index in range(pfb_count):
        offset = pfb_count - 1 - tap_index
        polyphase = polyphase + prototype[tap_index] * history[offset : offset + frames]
    cosine, sine = fourier_tables(channels)
    both = jnp.dot(polyphase, jnp.concatenate([cosine, sine], axis=1), precision=HIGHEST)
    with_cos = both[..., :channels].reshape(frames, 2, share, channels)
    with_sin = both[..., channels:].reshape(frames, 2, share, channels)
    spec_real = with_cos[:, 0] + with_sin[:, 1]
    spec_imag = with_cos[:, 1] - with_sin[:, 0]

    taps = jnp.pad(dish_filter, ((0, 0), (0, 0), (0, extra), (0, 0)))
    taps = lax.dynamic_slice_in_dim(taps, position * share, share, 2)
    lead = ((fir_count - 1, 0), (0, 0), (0, 0))
    past_real, past_imag = jnp.pad(spec_real, lead), jnp.pad(spec_imag, lead)
    out_real = jnp.zeros_like(spec_real)
    out_imag = jnp.zeros_like(spec_imag)
    for tap_index in range(fir_count):
        offset = fir_count - 1 - tap_index
        part_real = past_real[offset : offset + frames]
        part_imag = past_imag[offset : offset + frames]
        factor_real, factor_imag = taps[0, tap_index], taps[1, tap_index]
        out_real = out_real + factor_real * part_real - factor_imag * part_imag
        out_imag = out_imag + factor_real * part_imag + factor_imag * part_real

    filtered = jnp.stack([out_real, out_imag])
    filtered = filtered.reshape(2, frames, share, bands, band_chans)
    filtered = jnp.transpose(filtered, (3, 0, 2, 4, 1)).reshape(
        bands, 2 * share, band_chans * frames
    )
    filtered = jnp.repeat(filtered, owners, axis=0)
    field = lax.all_to_all(filtered, "band", split_axis=0, concat_axis=0, tiled=True)
    field = field.reshape(devices, 2, share, band_chans, frames)
    field = jnp.transpose(field, (1, 0, 2, 3, 4))
    field = field.reshape(2, devices * share, band_chans, frames)
    field = jnp.take(field, dish_order, axis=1)
    power = detect(beam_weights[0], field[0], field[1])
    return power[None]


def solution(mesh):
    devices = mesh.shape["band"]

    def body(samples, prototype, dish_filter, beam_weights, dish_order):
        channels = prototype.shape[1]
        close = (
            channels == LANES
            and beam_weights.shape[1] == 8
            and devices * 8 == channels
            and dish_filter.shape[2] == 12 * devices
            and samples.shape[2] * devices == 32 * channels
        )
        chosen = close_body if close else wide_body
        return chosen(samples, prototype, dish_filter, beam_weights, dish_order)

    placed = (P(None, None, ("grp", "band")), P(), P(), P("band", None, None, None, None), P())
    return jax.shard_map(
        body,
        mesh=mesh,
        in_specs=placed,
        out_specs=P(("grp", "band"), None, None, None),
        check_vma=False,
    )
```

```python
import math

import jax
import jax.numpy as jnp
import numpy as np
from jax import lax
from jax.experimental import pallas as pl
from jax.experimental.pallas import tpu as pltpu
from jax.sharding import PartitionSpec as P

INTEG = 4
EARLY = 2
HIGHEST = lax.Precision.HIGHEST
F32 = jnp.float32
BF16 = jnp.bfloat16
LANES = 128
VMEM = pl.BlockSpec(memory_space=pltpu.VMEM)
HBM = pl.BlockSpec(memory_space=pltpu.HBM)
GRANT = pltpu.CompilerParams(vmem_limit_bytes=16 << 20)


def fourier_tables(length):
    counter = jnp.arange(length, dtype=jnp.int32)
    product = counter[:, None] * counter[None, :] % length
    angles = product.astype(jnp.float32) * (2.0 * math.pi / length)
    factor = 1.0 / math.sqrt(length)
    return (jnp.cos(angles) * factor, jnp.sin(angles) * factor)


held = pltpu.with_memory_space_constraint


def split(value):
    high = value.astype(BF16)
    return high, (value - high.astype(F32)).astype(BF16)


def share_row(part, dish):
    return part * 8 + dish if dish < 8 else 16 + part * 4 + dish - 8


def pieces_kernel(x_ref, out_ref):
    devices, frames_dev = out_ref.shape[:2]
    low = lax.broadcasted_iota(jnp.int32, (8, LANES), 0) < 4
    for frame in range(frames_dev):
        lanes = slice(frame * LANES, (frame + 1) * LANES)
        for dev in range(0, devices, 2):
            for one in (dev, dev + 1):
                for part in range(2):
                    out_ref[one, frame, part * 8 : part * 8 + 8, :] = x_ref[
                        part, one * 8 : one * 8 + 8, lanes
                    ]
            start = devices * 8 + dev * 4
            real = x_ref[0, start : start + 8, lanes]
            imag = x_ref[1, start : start + 8, lanes]
            out_ref[dev, frame, 16:24, :] = jnp.where(low, real, pltpu.roll(imag, 4, 0))
            out_ref[dev + 1, frame, 16:24, :] = jnp.where(low, pltpu.roll(real, 4, 0), imag)


def weights_kernel(
    w_ref, order_ref, slot_ref, table_ref, early_ref, late_ref, table_out_ref, *scratch
):
    buffer, made, sems, table_sem = scratch
    table_copy = pltpu.make_async_copy(table_ref, table_out_ref, table_sem)
    loads = [
        pltpu.make_async_copy(w_ref.at[chan], buffer.at[chan], sems.at[0, chan])
        for chan in range(w_ref.shape[0])
    ]
    stores = [
        pltpu.make_async_copy(made.at[chan], late_ref.at[chan], sems.at[1, chan])
        for chan in range(late_ref.shape[0])
    ]
    ahead = 3
    for load in loads[:ahead]:
        load.start()
    hot = (slot_ref[...] == order_ref[...]).astype(F32).T.astype(BF16)
    beams = w_ref.shape[3]
    for chan, load in enumerate(loads):
        load.wait()
        if chan + ahead < len(loads):
            loads[chan + ahead].start()
        elif chan + ahead == len(loads):
            table_copy.start()
        for part in range(2):
            halves = [
                jnp.dot(half, hot, preferred_element_type=F32).astype(BF16)
                for half in split(buffer[chan, part].T)
            ]
            rows = slice(part * beams, (part + 1) * beams)
            both = jnp.concatenate(halves, axis=1)
            if chan < EARLY:
                early_ref[chan, rows, :] = both
            else:
                made[chan - EARLY, rows, :] = both
        if chan >= EARLY:
            stores[chan - EARLY].start()
    for store in stores:
        store.wait()
    table_copy.wait()


def channel_kernel(
    x_ref, proto_ref, table_ref, taps_ref, late_ref, out_ref, late_out_ref, *scratch
):
    poly, spec, filt, late_sem = scratch
    late_copy = pltpu.make_async_copy(late_ref, late_out_ref, late_sem)
    late_copy.start()
    pfb_count = proto_ref.shape[0]
    fir_count = taps_ref.shape[0]
    frames = poly.shape[0]
    group = 8
    low = lax.broadcasted_iota(jnp.int32, (group, 8, LANES), 1) < 4

    spec[0 : fir_count - 1] = jnp.zeros((fir_count - 1, 24, 2 * LANES), F32)
    for first in range(0, frames, group):
        found = []
        for rows in range(0, 24, 8):
            total = None
            for tap in range(pfb_count):
                begin = first - tap
                lost = max(0, -begin)
                if lost >= group:
                    continue
                block = x_ref[begin + lost : begin + group, rows : rows + 8, :]
                term = block * proto_ref[tap : tap + 1, :][None]
                if lost:
                    term = jnp.concatenate([jnp.zeros((lost, 8, LANES), F32), term], axis=0)
                total = term if total is None else total + term
            found.append(total)
        turned = pltpu.roll(found[2], 4, 1)
        other = [found[1], -found[0], jnp.where(low, turned, -turned)]
        for index in range(3):
            rows = slice(index * 8, index * 8 + 8)
            poly[first : first + group, rows, 0:LANES] = found[index]
            poly[first : first + group, rows, LANES : 2 * LANES] = other[index]

    for first in range(0, frames, group):
        value = poly[first : first + group].reshape(group * 24, 2 * LANES)
        high, rest = split(value)
        stacked = jnp.concatenate([high, rest, high], axis=1)
        product = jnp.dot(stacked, table_ref[...], preferred_element_type=F32)
        begin = first + fir_count - 1
        spec[begin : begin + group] = product.reshape(group, 24, 2 * LANES)

    for rows in range(0, 24, 8):
        for first in range(0, frames, group):
            total = None
            for tap in range(fir_count):
                begin = first + fir_count - 1 - tap
                near = spec[begin : begin + group, rows : rows + 8, 0:LANES]
                cross = spec[begin : begin + group, rows : rows + 8, LANES : 2 * LANES]
                term = taps_ref[tap, 0, rows : rows + 8, :][None] * near
                term = term + taps_ref[tap, 1, rows : rows + 8, :][None] * cross
                total = term if total is None else total + term
            for frame in range(group):
                begin = (first + frame) * 24 + rows
                filt[begin : begin + 8, :] = total[frame]

    per_band = out_ref.shape[1] // 6
    for pair in range(6):
        rows = [
            filt[pl.ds(share_row(part, pair * 2 + odd), frames, stride=24), :]
            for part in range(2)
            for odd in range(2)
        ]
        turned = jnp.concatenate(rows, axis=0).T
        for dev in range(out_ref.shape[0]):
            out_ref[dev, pair * per_band : (pair + 1) * per_band, :] = turned[
                dev * per_band : (dev + 1) * per_band
            ]
    late_copy.wait()


def beams_kernel(x_ref, early_ref, late_ref, out_ref):
    rows = x_ref.shape[0] // 8
    beams = early_ref.shape[1] // 2
    lane = lax.broadcasted_iota(jnp.int32, (rows, LANES), 1)
    even = lane % 64 < 32
    wide = lax.broadcasted_iota(jnp.int32, (beams, LANES), 1)
    even_wide = wide % 64 < 32
    row = lax.broadcasted_iota(jnp.int32, (16, 2 * LANES), 0)
    column = lax.broadcasted_iota(jnp.int32, (16, 2 * LANES), 1)
    pool = jnp.where(row == column % 64 // INTEG, 1.0 / INTEG, 0.0).astype(BF16)
    steps = range(out_ref.shape[0] // 2)
    fields = []
    for step in steps:
        one = x_ref[pl.ds(2 * step, rows, stride=8), :]
        two = x_ref[pl.ds(2 * step + 1, rows, stride=8), :]
        first = jnp.where(even, one, pltpu.roll(two, 32, 1))
        second = jnp.where(even, pltpu.roll(one, LANES - 32, 1), two)
        both = jnp.concatenate(split(jnp.concatenate([first, second], axis=0)), axis=1)
        fields.append(jnp.concatenate([both, both], axis=0))
    beam_of = []
    for step in steps:
        if 2 * step < EARLY:
            w_ref, begin = early_ref, 2 * step
        else:
            w_ref, begin = late_ref, 2 * step - EARLY
        sums = []
        for index in range(2):
            weights = w_ref[begin + index]
            product = jnp.dot(weights, fields[step], preferred_element_type=F32)
            sums.append(product[:, 0:LANES] + product[:, LANES : 2 * LANES])
        by_real = jnp.where(even_wide, sums[0][:beams], sums[1][:beams])
        by_imag = jnp.where(even_wide, sums[0][beams:], sums[1][beams:])
        crossed = pltpu.roll(by_imag, 64, 1)
        beam_of.append(by_real + jnp.where(wide < 64, -crossed, crossed))
    for step in steps:
        power = lax.dot_general(
            pool,
            jnp.concatenate(split(beam_of[step] * beam_of[step]), axis=1),
            (((1,), (1,)), ((), ())),
            preferred_element_type=F32,
        )
        out_ref[2 * step] = power[0:8]
        out_ref[2 * step + 1] = power[8:16]


def slots_of(devices):
    index = np.arange(devices * 12, dtype=np.int32)
    own = index % 6 * 2 + index // (devices * 6)
    source = index // 6 % devices
    dishes = np.where(own < 8, source * 8 + own, devices * 8 + source * 4 + own - 8)
    return dishes.astype(np.int32)[:, None]


def dft_parts(channels):
    index = np.arange(channels)
    angle = 2.0 * np.pi * (index[:, None] * index[None, :] % channels) / channels
    cosine = np.cos(angle) / np.sqrt(channels)
    sine = np.sin(angle) / np.sqrt(channels)
    table = np.block([[cosine, sine], [sine, -cosine]]).astype(np.float32)
    high = table.astype(jnp.bfloat16)
    rest = (table - high.astype(np.float32)).astype(jnp.bfloat16)
    return np.concatenate([high, high, rest], axis=0)


def close_body(samples, prototype, dish_filter, beam_weights, dish_order):
    devices = lax.axis_size("band")
    position = lax.axis_index("band")
    channels = prototype.shape[1]
    fir_count = dish_filter.shape[1]
    dishes = dish_filter.shape[2]
    band_chans = beam_weights.shape[1]
    beams = beam_weights.shape[4]
    frames_dev = samples.shape[2] // channels
    frames = frames_dev * devices

    def exchange(value):
        return lax.all_to_all(value, "band", split_axis=0, concat_axis=0, tiled=True)

    pieces = pl.pallas_call(
        pieces_kernel,
        out_shape=jax.ShapeDtypeStruct((devices, frames_dev, 24, channels), F32),
        in_specs=[VMEM],
        out_specs=VMEM,
        name="pieces",
        compiler_params=GRANT,
    )(samples)
    arrived = exchange(pieces).reshape(frames, 24, channels)

    eight = lax.dynamic_slice_in_dim(dish_filter, position * 8, 8, 2)
    four = lax.dynamic_slice_in_dim(dish_filter, devices * 8 + position * 4, 4, 2)
    taps = jnp.concatenate([eight, eight, four, four], axis=2)
    taps = jnp.transpose(taps, (1, 0, 2, 3))
    table = dft_parts(channels)
    early, late, table = pl.pallas_call(
        weights_kernel,
        out_shape=[
            jax.ShapeDtypeStruct((EARLY, 2 * beams, 2 * dishes), BF16),
            pltpu.HBM((band_chans - EARLY, 2 * beams, 2 * dishes), BF16),
            jax.ShapeDtypeStruct(table.shape, BF16),
        ],
        in_specs=[HBM, VMEM, VMEM, HBM],
        out_specs=[VMEM, HBM, VMEM],
        scratch_shapes=[
            pltpu.VMEM((band_chans, 2, dishes, beams), F32),
            pltpu.VMEM((band_chans - EARLY, 2 * beams, 2 * dishes), BF16),
            pltpu.SemaphoreType.DMA((2, band_chans)),
            pltpu.SemaphoreType.DMA(()),
        ],
        name="weights",
        compiler_params=GRANT,
        cost_estimate=pl.CostEstimate(
            flops=8 * 4 * 2 * 192 * 192 * 384, bytes_accessed=5 << 20, transcendentals=0
        ),
    )(
        held(beam_weights[0], pltpu.HBM),
        dish_order.reshape(1, dishes),
        slots_of(devices),
        held(jnp.asarray(table), pltpu.HBM),
    )
    arrived, early, late, table = lax.optimization_barrier((arrived, early, late, table))

    block = (6 * band_chans, channels)
    filtered, late = pl.pallas_call(
        channel_kernel,
        out_shape=[
            jax.ShapeDtypeStruct((devices,) + block, F32),
            jax.ShapeDtypeStruct(late.shape, BF16),
        ],
        in_specs=[VMEM] * 4 + [HBM],
        out_specs=[VMEM] * 2,
        scratch_shapes=[
            pltpu.VMEM((frames, 24, 2 * LANES), F32),
            pltpu.VMEM((frames + fir_count - 1, 24, 2 * LANES), F32),
            pltpu.VMEM((frames * 24, LANES), F32),
            pltpu.SemaphoreType.DMA(()),
        ],
        name="channels",
        compiler_params=GRANT,
    )(
        held(arrived, pltpu.VMEM),
        prototype,
        held(table, pltpu.VMEM),
        taps,
        held(late, pltpu.HBM),
    )
    field = exchange(filtered).reshape(devices * 6 * band_chans, channels)

    power = pl.pallas_call(
        beams_kernel,
        out_shape=jax.ShapeDtypeStruct((band_chans, frames // INTEG, beams), F32),
        in_specs=[VMEM] * 3,
        out_specs=VMEM,
        name="beams",
        compiler_params=GRANT,
    )(held(field, pltpu.VMEM), held(early, pltpu.VMEM), held(late, pltpu.VMEM))
    return jnp.transpose(power, (0, 2, 1))[None]


def detect(weights, field_real, field_imag):
    def contract(weight_part, field_part):
        return jnp.einsum("qds,dqf->qsf", weight_part, field_part, precision=HIGHEST)

    beam_real = contract(weights[:, 0], field_real) - contract(weights[:, 1], field_imag)
    beam_imag = contract(weights[:, 0], field_imag) + contract(weights[:, 1], field_real)
    energy = beam_real * beam_real + beam_imag * beam_imag
    shaped = energy.reshape(energy.shape[:-1] + (energy.shape[-1] // INTEG, INTEG))
    return jnp.mean(shaped, axis=-1)


def wide_body(samples, prototype, dish_filter, beam_weights, dish_order):
    devices = lax.axis_size("band")
    position = lax.axis_index("band")
    pfb_count, channels = prototype.shape
    fir_count = dish_filter.shape[1]
    dishes = dish_filter.shape[2]
    band_chans = beam_weights.shape[1]
    bands = channels // band_chans
    owners = devices // bands
    frames_dev = samples.shape[2] // channels
    frames = frames_dev * devices
    share = -(-dishes // devices)
    extra = share * devices - dishes

    padded = jnp.pad(samples, ((0, 0), (0, extra), (0, 0)))
    pieces = padded.reshape(2, devices, share, frames_dev, channels)
    pieces = jnp.transpose(pieces, (1, 3, 0, 2, 4)).reshape(
        devices, frames_dev, 2 * share, channels
    )
    arrived = lax.all_to_all(pieces, "band", split_axis=0, concat_axis=0, tiled=True)
    blocks = arrived.reshape(frames, 2 * share, channels)

    history = jnp.pad(blocks, ((pfb_count - 1, 0), (0, 0), (0, 0)))
    polyphase = jnp.zeros_like(blocks)
    for tap_index in range(pfb_count):
        offset = pfb_count - 1 - tap_index
        polyphase = polyphase + prototype[tap_index] * history[offset : offset + frames]
    cosine, sine = fourier_tables(channels)
    both = jnp.dot(polyphase, jnp.concatenate([cosine, sine], axis=1), precision=HIGHEST)
    with_cos = both[..., :channels].reshape(frames, 2, share, channels)
    with_sin = both[..., channels:].reshape(frames, 2, share, channels)
    spec_real = with_cos[:, 0] + with_sin[:, 1]
    spec_imag = with_cos[:, 1] - with_sin[:, 0]

    taps = jnp.pad(dish_filter, ((0, 0), (0, 0), (0, extra), (0, 0)))
    taps = lax.dynamic_slice_in_dim(taps, position * share, share, 2)
    lead = ((fir_count - 1, 0), (0, 0), (0, 0))
    past_real, past_imag = jnp.pad(spec_real, lead), jnp.pad(spec_imag, lead)
    out_real = jnp.zeros_like(spec_real)
    out_imag = jnp.zeros_like(spec_imag)
    for tap_index in range(fir_count):
        offset = fir_count - 1 - tap_index
        part_real = past_real[offset : offset + frames]
        part_imag = past_imag[offset : offset + frames]
        factor_real, factor_imag = taps[0, tap_index], taps[1, tap_index]
        out_real = out_real + factor_real * part_real - factor_imag * part_imag
        out_imag = out_imag + factor_real * part_imag + factor_imag * part_real

    filtered = jnp.stack([out_real, out_imag])
    filtered = filtered.reshape(2, frames, share, bands, band_chans)
    filtered = jnp.transpose(filtered, (3, 0, 2, 4, 1)).reshape(
        bands, 2 * share, band_chans * frames
    )
    filtered = jnp.repeat(filtered, owners, axis=0)
    field = lax.all_to_all(filtered, "band", split_axis=0, concat_axis=0, tiled=True)
    field = field.reshape(devices, 2, share, band_chans, frames)
    field = jnp.transpose(field, (1, 0, 2, 3, 4))
    field = field.reshape(2, devices * share, band_chans, frames)
    field = jnp.take(field, dish_order, axis=1)
    power = detect(beam_weights[0], field[0], field[1])
    return power[None]


def solution(mesh):
    devices = mesh.shape["band"]

    def body(samples, prototype, dish_filter, beam_weights, dish_order):
        channels = prototype.shape[1]
        close = (
            channels == LANES
            and beam_weights.shape[1] == 8
            and devices * 8 == channels
            and dish_filter.shape[2] == 12 * devices
            and samples.shape[2] * devices == 32 * channels
        )
        chosen = close_body if close else wide_body
        return chosen(samples, prototype, dish_filter, beam_weights, dish_order)

    placed = (P(None, None, ("grp", "band")), P(), P(), P("band", None, None, None, None), P())
    return jax.shard_map(
        body,
        mesh=mesh,
        in_specs=placed,
        out_specs=P(("grp", "band"), None, None, None),
        check_vma=False,
    )
```
